32 devices in a mesh: groups: 2 (over y), seq: 8 (over z, x), rep: 2 (over core).
Axes of the slice: x: 2, y: 2, z: 4, core: 2. Of those that a mesh axis runs over, the one named last changes fastest.
Arguments:
- stream: bfloat16 [4096, 1536], P(('groups', 'seq', 'rep')), parts along dimension 0, may hold values from -6 to 6
- queries: bfloat16 [4096, 2048], P(('groups', 'seq'), 'rep'), parts along dimension 0, may hold values from -10 to 10
- key_rows: bfloat16 [4096, 256], P(('groups', 'seq'), 'rep'), parts along dimension 0, may hold values from -10 to 10
- value_rows: bfloat16 [4096, 256], P(('groups', 'seq'), 'rep'), parts along dimension 0, may hold values from -6 to 6
- sink_logits: float32 [32], P('rep'), may hold values from 0 to 5
- out_weight: bfloat16 [2048, 1536], P('rep'), may hold values from -0.125 to 0.125
- norm_gain: float32 [1536], replicated, may hold values from 0.25 to 1.75
- expert_ids: int32 [4096, 4], P(('groups', 'seq', 'rep')), parts along dimension 0, may hold values from 0 to 7, all different within a row; in each aligned block of 128 rows (0 to 127, 128 to 255, ...) at most 96 rows name the same one
- route_weights: float32 [4096, 4], P(('groups', 'seq', 'rep')), parts along dimension 0, may hold values from 0.1 to 1
- gate_weight: bfloat16 [8, 1536, 1536], P('seq', None, 'rep'), may hold values from -0.15625 to 0.15625
- up_weight: bfloat16 [8, 1536, 1536], P('seq', None, 'rep'), may hold values from -0.15625 to 0.15625
- down_weight: bfloat16 [8, 1536, 1536], P('seq', 'rep'), may hold values from -0.15625 to 0.15625
Outputs:
- layer_out: bfloat16 [4096, 1536], P(('groups', 'seq', 'rep')), parts along dimension 0
The draws below stay inside these ranges and needn't reach their ends.
There are 2 independent parts, one for each index of `groups`. The reference program is written for one: setup_inputs(seed, part) draws one part's arguments, and reference() takes and returns one part's arrays. A program takes and returns all parts, laid end to end along the dimension named above; an argument that names none is the same for every part. Nothing has to cross between parts.
Inputs may be any that keep to these rules, and one draw needn't show every extreme that they name: `expert_ids`: each token names 4 different experts; among the 128 tokens of one device no expert is named more than 96 times, a bound that some block reaches.
All inputs are finite; a program needn't handle non-finite values.
Results may differ from the reference program's by a relative error of at most 0.009.
Values may be sent and summed in bfloat16 or wider, within the bound.
No kernel may reach another device: no remote copies, remote signals or barrier semaphores. Data moves between devices by JAX's collectives and lax.ppermute only.
A program may use at most 128 MiB of HBM per device.

```python
import math
import jax
import jax.numpy as jnp
import numpy as np
from jax import lax

D = 1536
HEADS = 32
KV_HEADS = 4
HEAD_DIM = 64
WINDOW = 128
FF = 1536
TOP = 4
TOK_DEV = 128
EXPERTS = 8
CAP = 96
TOKENS = 2048
N_REP = 2


def draw_queries(key, part):
    key = jax.random.fold_in(key, 11)
    return jnp.clip(jax.random.normal(key, (TOKENS, HEADS * HEAD_DIM), jnp.float32), -6.0, 6.0).astype(jnp.bfloat16)


def draw_key_rows(key, part):
    key = jax.random.fold_in(key, 12)
    return jnp.clip(jax.random.normal(key, (TOKENS, KV_HEADS * HEAD_DIM), jnp.float32), -6.0, 6.0).astype(jnp.bfloat16)


def block_scale(stream_key, shape, pieces, least, high):
    factor_of = 1.0
    for dim, parts in pieces:
        draws = jax.random.uniform(jax.random.fold_in(jax.random.fold_in(stream_key, 6), dim), (parts,), jnp.float32, least / len(pieces), high / len(pieces))
        factor_of = factor_of * jnp.repeat(jnp.exp(draws), shape[dim] // parts).reshape((-1,) + (1,) * (len(shape) - 1 - dim))
    return factor_of


def assign_block(rng, own, number, rows, count, top, reach, skew):
    sequence = jax.random.permutation(rng, count)
    crowded, ordinary = shares(count, rows * top, reach, skew, True), shares(count, rows * top, reach, skew, False)
    places = jnp.arange(count)

    def named(sizes, turn):
        used = int((sizes > 0).sum())
        fixed = max(1, used // 4)
        moved = fixed + (places - fixed + turn * (used - fixed)) % max(1, count - fixed)
        return jnp.zeros((count,), jnp.int32).at[sequence[jnp.where(places < fixed, places, moved)]].set(jnp.asarray(sizes, jnp.int32))

    sizes = jnp.where(number % 4 == 0, named(crowded, number // 4), named(ordinary, number - number // 4 - 1))
    mixed = jax.random.permutation(jax.random.fold_in(own, 3), count)
    donor, taker = mixed[0:count // 2 * 2:2], mixed[1:count // 2 * 2:2]
    room = jnp.minimum(sizes[donor] - 1, reach - sizes[taker]) // 2
    room = jnp.where((donor == sequence[0]) | (taker == sequence[0]) | (sizes[taker] == 0), 0, jnp.maximum(room, 0))
    moved = jax.random.randint(jax.random.fold_in(own, 4), (count // 2,), 0, 1 << 20) % (room + 1)
    sizes = sizes.at[donor].add(-moved).at[taker].add(moved)
    members = jnp.searchsorted(jnp.cumsum(sizes), jnp.arange(rows * top), side="right").astype(jnp.int32)
    listing = members.reshape(top, rows).T
    listing = listing[jax.random.permutation(jax.random.fold_in(own, 1), rows)]
    turn = jax.random.randint(jax.random.fold_in(own, 2), (rows, 1), 0, top)
    return jnp.take_along_axis(listing, (jnp.arange(top)[None, :] + turn) % top, axis=1)


def shares(count, total, limit, lean, full):
    weights = [(1 << 20) // math.isqrt(rank ** lean) + 1 for rank in range(1, count + 1)]
    largest = limit if full else min(limit, max(-(-total // count), total * weights[0] // sum(weights)))
    least = 1 if total - largest >= count - 1 else 0
    holding, surplus = [largest] + [least] * (count - 1), total - largest - least * (count - 1)
    while surplus > 0:
        free = [i for i in range(1, count) if holding[i] < largest] or [i for i in range(1, count) if holding[i] < limit]
        mass, remaining = sum([weights[i] for i in free]), surplus
        for i in free:
            extra = min(limit - holding[i], max(1, remaining * weights[i] // mass), surplus)
            holding[i] = holding[i] + extra
            surplus = surplus - extra
    return np.array(holding)


def bell_draw(stream_key, dims, scale, bound, split=(), kind=jnp.bfloat16):
    result = jax.random.normal(stream_key, dims, jnp.float32) * scale
    if len(split) > 0:
        result = block_scale(stream_key, dims, split, -0.22, 0.18) * result
    return jnp.clip(result, min=-bound, max=bound).astype(kind)


def setup_inputs(seed: int = 0, part: int = 0) -> dict:
    key_list = jax.random.split(jax.random.key(seed), 13)
    part_keys = jax.random.split(jax.random.fold_in(key_list[12], part), 13)
    stream = bell_draw(part_keys[0], (TOKENS, D), 1.0, 6.0, ((0, 16),))
    queries = draw_queries(jax.random.fold_in(jax.random.fold_in(key_list[12], part), 71), part)
    key_rows = draw_key_rows(jax.random.fold_in(jax.random.fold_in(key_list[12], part), 71), part)
    value_rows = bell_draw(part_keys[3], (TOKENS, KV_HEADS * HEAD_DIM), 1.0, 6.0, ((0, 8), (1, 2)))
    sink_logits = jnp.clip(5.0 * jax.random.uniform(key_list[4], (HEADS,), jnp.float32) ** block_scale(key_list[4], (HEADS,), ((0, 2),), -0.2, 0.2), 0.0, 5.0)
    out_weight = bell_draw(key_list[5], (HEADS * HEAD_DIM, D), (HEADS * HEAD_DIM) ** -0.5, 0.125, ((0, 2),))
    norm_gain = jnp.clip(1.0 + 0.15 * jax.random.normal(key_list[6], (D,), jnp.float32), 0.25, 1.75)
    expert_ids_keys = jax.random.split(jax.random.fold_in(part_keys[7], 1), TOKENS // TOK_DEV)
    expert_ids_turns = jax.random.permutation(jax.random.fold_in(part_keys[7], 3), TOKENS // TOK_DEV)
    expert_ids = jax.vmap(lambda own, number: assign_block(jax.random.fold_in(part_keys[7], 2), own, number, TOK_DEV, EXPERTS, TOP, CAP, 2))(expert_ids_keys, expert_ids_turns).reshape((TOKENS, TOP))
    route_weights = jnp.clip(0.1 + 0.9 * jax.random.uniform(part_keys[8], (TOKENS, TOP), jnp.float32) ** block_scale(part_keys[8], (TOKENS, TOP), ((0, 16),), -0.2, 0.2), 0.1, 1.0)
    gate_weight = bell_draw(key_list[9], (EXPERTS, D, FF), D ** -0.5, 0.15625, ((0, 8), (2, 2)))
    up_weight = bell_draw(key_list[10], (EXPERTS, D, FF), D ** -0.5, 0.15625, ((0, 8), (2, 2)))
    down_weight = bell_draw(key_list[11], (EXPERTS, FF, D), FF ** -0.5, 0.15625, ((0, 8), (1, 2)))
    return dict(stream=stream, queries=queries, key_rows=key_rows, value_rows=value_rows, sink_logits=sink_logits, out_weight=out_weight, norm_gain=norm_gain, expert_ids=expert_ids, route_weights=route_weights, gate_weight=gate_weight, up_weight=up_weight, down_weight=down_weight)


def attention(queries, key_rows, value_rows, sink_logits):
    block_len = TOK_DEV * N_REP
    group_size = HEADS // KV_HEADS
    kv_width = KV_HEADS * HEAD_DIM
    leading = jnp.zeros((WINDOW, kv_width), jnp.bfloat16)
    key_pad = jnp.concatenate([leading, key_rows], axis=0)
    value_pad = jnp.concatenate([leading, value_rows], axis=0)
    sink_grid = sink_logits.reshape(KV_HEADS, group_size)[:, :, None, None]

    def one_block(block_index):
        offset = block_index * block_len
        query_part = lax.dynamic_slice_in_dim(queries, offset, block_len, 0)
        query_part = query_part.reshape(block_len, KV_HEADS, group_size, HEAD_DIM).astype(jnp.float32)
        key_part = lax.dynamic_slice_in_dim(key_pad, offset, WINDOW + block_len, 0)
        key_part = key_part.reshape(WINDOW + block_len, KV_HEADS, HEAD_DIM).astype(jnp.float32)
        value_part = lax.dynamic_slice_in_dim(value_pad, offset, WINDOW + block_len, 0)
        value_part = value_part.reshape(WINDOW + block_len, KV_HEADS, HEAD_DIM).astype(jnp.float32)
        scores = jnp.einsum('igkd,jgd->gkij', query_part, key_part) * (1.0 / math.sqrt(HEAD_DIM))
        query_pos = offset + jnp.arange(block_len, dtype=jnp.int32)
        key_pos = offset - WINDOW + jnp.arange(WINDOW + block_len, dtype=jnp.int32)
        distance = query_pos[:, None] - key_pos[None, :]
        allowed = (distance >= 0) & (distance < WINDOW) & (key_pos[None, :] >= 0)
        scores = jnp.where(allowed, scores, -jnp.inf)
        highest = jnp.maximum(lax.optimization_barrier(jnp.max(scores, axis=-1, keepdims=True)), sink_grid)
        weights = jnp.exp(scores - highest)
        summed = jnp.exp(sink_grid - highest) + lax.optimization_barrier(jnp.sum(weights, axis=-1, keepdims=True))
        attn_probs = (weights / summed).astype(jnp.bfloat16)
        attended = jnp.einsum('gkij,jgd->igkd', attn_probs.astype(jnp.float32), value_part)
        return attended.astype(jnp.bfloat16).reshape(block_len, HEADS * HEAD_DIM)
    blocks = lax.map(one_block, jnp.arange(TOKENS // block_len, dtype=jnp.int32))
    return blocks.reshape(TOKENS, HEADS * HEAD_DIM)

def one_expert(operands):
    row_block, gate_w, up_w, down_w = operands
    gate_pre = jnp.dot(row_block, gate_w, preferred_element_type=jnp.float32)
    up_pre = jnp.dot(row_block, up_w, preferred_element_type=jnp.float32)
    activated = (gate_pre * jax.nn.sigmoid(1.702 * gate_pre) * (up_pre + 1.0)).astype(jnp.bfloat16)
    half_width = FF // N_REP
    summed = jnp.zeros((row_block.shape[0], D), jnp.float32)
    for portion in range(N_REP):
        partial_out = jnp.dot(activated[:, portion * half_width:(portion + 1) * half_width], down_w[portion * half_width:(portion + 1) * half_width], preferred_element_type=jnp.float32).astype(jnp.bfloat16)
        summed = summed + lax.optimization_barrier(partial_out).astype(jnp.float32)
    return summed.astype(jnp.bfloat16)

def reference(stream, queries, key_rows, value_rows, sink_logits, out_weight, norm_gain, expert_ids, route_weights, gate_weight, up_weight, down_weight):
    attended = attention(queries, key_rows, value_rows, sink_logits)
    projected = jnp.dot(attended, out_weight, preferred_element_type=jnp.float32)
    residual = (stream.astype(jnp.float32) + projected).astype(jnp.bfloat16)
    resid_f = residual.astype(jnp.float32)
    normed = (resid_f * lax.rsqrt(lax.optimization_barrier(jnp.mean(resid_f * resid_f, axis=-1, keepdims=True)) + 1e-05) * norm_gain).astype(jnp.bfloat16)
    blocks_total = TOKENS // TOK_DEV
    flat_ids = expert_ids.reshape(blocks_total, TOK_DEV * TOP)
    onehot = (flat_ids[:, :, None] == jnp.arange(EXPERTS, dtype=jnp.int32)).astype(jnp.int32)
    earlier = jnp.cumsum(onehot, axis=1) - onehot
    slot_index = lax.optimization_barrier(jnp.sum(earlier * onehot, axis=-1)).reshape(TOKENS, TOP)
    block_of = (jnp.arange(TOKENS, dtype=jnp.int32) // TOK_DEV)[:, None]
    cell_index = ((expert_ids * blocks_total + block_of) * CAP + slot_index).reshape(-1)
    dispatch_rows = jnp.zeros((EXPERTS * blocks_total * CAP, D), jnp.bfloat16)
    dispatch_rows = dispatch_rows.at[cell_index].set(jnp.repeat(normed, TOP, axis=0))
    dispatch_rows = dispatch_rows.reshape(EXPERTS, blocks_total * CAP, D)
    expert_out = lax.map(one_expert, (dispatch_rows, gate_weight, up_weight, down_weight))
    picked = expert_out.reshape(EXPERTS * blocks_total * CAP, D)[cell_index].reshape(TOKENS, TOP, D)
    expert_sum = lax.optimization_barrier(jnp.sum(route_weights[:, :, None] * picked.astype(jnp.float32), axis=1))
    return (resid_f + expert_sum).astype(jnp.bfloat16)
```

```python
import functools
import math

import jax
import jax.numpy as jnp
from jax import lax
from jax.experimental import pallas as pl
from jax.experimental.pallas import tpu as pltpu
from jax.sharding import PartitionSpec as P

HEAD_DIM = 64
WINDOW = 128
TOP = 4
EXP_DEV = 1
LANES = 128
SNAKES = {8: (0, 2, 4, 6, 7, 5, 3, 1)}
MIB = 1 << 20


def shifted(value, axis, by):
    peers = lax.axis_size(axis)
    pairs = [(i, i + by) for i in range(peers) if 0 <= i + by < peers]
    return lax.ppermute(value, axis, pairs)


def swapped(value, axis, bit=1):
    peers = lax.axis_size(axis)
    return lax.ppermute(value, axis, [(i, i ^ bit) for i in range(peers)])


def mm(a, b):
    return jnp.dot(a, b, preferred_element_type=jnp.float32)


def attend_kernel(
    group_pairs, first_ref, sink_ref, q_ref, kp_ref, kc_ref, vp_ref, vc_ref, ow_ref, *rest
):
    mix = len(rest) > 2
    if mix:
        rank_ref, other_ref, send_ref, own_ref, total = rest
    else:
        out_ref, total = rest
    step = pl.program_id(0)
    rows = q_ref.shape[0]
    keys = kp_ref.shape[0] + kc_ref.shape[0]
    pairs_step = q_ref.shape[1] // LANES
    group = (step * pairs_step) // group_pairs

    lane_k = lax.broadcasted_iota(jnp.int32, (keys, LANES), 1)
    low = lane_k < HEAD_DIM
    k = jnp.concatenate([kp_ref[...], kc_ref[...]], axis=0).astype(jnp.float32)
    v = jnp.concatenate([vp_ref[...], vc_ref[...]], axis=0).astype(jnp.float32)
    k_low = jnp.where(low, jnp.where(group == 0, k, pltpu.roll(k, HEAD_DIM, 1)), 0.0)
    v_low = jnp.where(low, jnp.where(group == 0, v, pltpu.roll(v, HEAD_DIM, 1)), 0.0)
    k_high, v_high = pltpu.roll(k_low, HEAD_DIM, 1), pltpu.roll(v_low, HEAD_DIM, 1)
    kk = jnp.concatenate([k_low, k_high], axis=0).astype(jnp.bfloat16)
    one_low = jnp.where(low, 1.0, 0.0)
    vv = jnp.concatenate(
        [
            jnp.concatenate([v_low, one_low], axis=1),
            jnp.concatenate([v_high, 1.0 - one_low], axis=1),
        ],
        axis=0,
    ).astype(jnp.bfloat16)

    row = lax.broadcasted_iota(jnp.int32, (rows, keys), 0)
    column = lax.broadcasted_iota(jnp.int32, (rows, keys), 1)
    least = jnp.where(first_ref[0] == 1, WINDOW, 0)
    allowed = (column <= row + WINDOW) & (column > row) & (column >= least)
    low_out = lax.broadcasted_iota(jnp.int32, (rows, LANES), 1) < HEAD_DIM
    scale = 1.0 / math.sqrt(HEAD_DIM)

    done = []
    for pair in range(pairs_step):
        q = q_ref[:, pair * LANES : (pair + 1) * LANES]
        scores = lax.dot_general(
            q, kk, (((1,), (1,)), ((), ())), preferred_element_type=jnp.float32
        )
        weights, sinks = [], []
        for side in range(2):
            part = jnp.where(allowed, scores[:, side * keys : (side + 1) * keys] * scale, -jnp.inf)
            sink = sink_ref[(step * pairs_step + pair) * 2 + side]
            highest = jnp.maximum(jnp.max(part, axis=1, keepdims=True), sink)
            weights.append(jnp.exp(part - highest).astype(jnp.bfloat16))
            sinks.append(jnp.exp(sink - highest))
        both = mm(jnp.concatenate(weights, axis=1), vv)
        below = both[:, LANES:] + jnp.where(low_out, sinks[0], sinks[1])
        done.append((both[:, :LANES] / below).astype(jnp.bfloat16))
    part = mm(jnp.concatenate(done, axis=1), ow_ref[...])

    @pl.when(step == 0)
    def _():
        total[...] = part

    @pl.when(step > 0)
    def _():
        total[...] += part

    @pl.when(step == pl.num_programs(0) - 1)
    def _():
        if mix:
            mine = total[...]
            other = other_ref[...]
            own_first = rank_ref[0] == 0
            own_ref[...] = jnp.where(own_first, mine, other)
            send_ref[...] = jnp.where(own_first, other, mine).astype(jnp.bfloat16)
        else:
            out_ref[...] = total[...]


def attend(half, first, sinks, queries, keys, values, out_weight, rank=None, other=None):
    (k_prev, kp_index), (k_cur, kc_index) = keys
    (v_prev, vp_index), (v_cur, vc_index) = values
    rows, width, model = WINDOW, queries.shape[1], out_weight.shape[1]
    block = min(width, 256)
    group_pairs = width // LANES // (k_cur.shape[1] // HEAD_DIM)
    smem = pl.BlockSpec(memory_space=pltpu.SMEM)

    def fixed(index):
        return pl.BlockSpec((rows, LANES), lambda i: (index, 0))

    in_specs = [
        smem,
        smem,
        pl.BlockSpec((rows, block), lambda i: (half, i)),
        fixed(kp_index),
        fixed(kc_index),
        fixed(vp_index),
        fixed(vc_index),
        pl.BlockSpec((block, model), lambda i: (i, 0)),
    ]
    operands = [first, sinks, queries, k_prev, k_cur, v_prev, v_cur, out_weight]
    whole = pl.BlockSpec((rows, model), lambda i: (0, 0))
    wide = jax.ShapeDtypeStruct((rows, model), jnp.float32)
    narrow = jax.ShapeDtypeStruct((rows, model), jnp.bfloat16)
    if rank is None:
        out_shape, out_specs = wide, whole
    else:
        in_specs += [smem, whole]
        operands += [rank, other]
        out_shape, out_specs = (narrow, wide), (whole, whole)
    return pl.pallas_call(
        functools.partial(attend_kernel, group_pairs),
        grid=(width // block,),
        in_specs=in_specs,
        out_specs=out_specs,
        out_shape=out_shape,
        scratch_shapes=[pltpu.VMEM((rows, model), jnp.float32)],
        compiler_params=pltpu.CompilerParams(vmem_limit_bytes=32 * MIB),
        cost_estimate=pl.CostEstimate(
            flops=2 * rows * width * (model + 1024), bytes_accessed=6 * MIB, transcendentals=0
        ),
        name="attend",
    )(*operands)


def norm_kernel(stream_ref, own_ref, came_ref, gain_ref, residual_ref, *normed_refs):
    residual = (
        stream_ref[...].astype(jnp.float32) + own_ref[...] + came_ref[...].astype(jnp.float32)
    ).astype(jnp.bfloat16)
    residual_ref[...] = residual
    wide = residual.astype(jnp.float32)
    mean = jnp.mean(wide * wide, axis=-1, keepdims=True)
    normed = (wide * lax.rsqrt(mean + 1e-05) * gain_ref[...]).astype(jnp.bfloat16)
    rows = normed_refs[0].shape[0]
    for index, ref in enumerate(normed_refs):
        ref[...] = normed[index * rows : (index + 1) * rows]


def norm(stream, own, came, gain, pieces):
    rows, model = stream.shape
    return pl.pallas_call(
        norm_kernel,
        out_shape=[jax.ShapeDtypeStruct((rows, model), jnp.bfloat16)]
        + [jax.ShapeDtypeStruct((rows // pieces, model), jnp.bfloat16)] * pieces,
        compiler_params=pltpu.CompilerParams(vmem_limit_bytes=32 * MIB),
        cost_estimate=pl.CostEstimate(
            flops=8 * rows * model, bytes_accessed=14 * rows * model, transcendentals=rows
        ),
        name="norm",
    )(stream, own, came, gain.reshape(1, model))


def spread_kernel(ids_ref, weights_ref, out_ref):
    rows = ids_ref.shape[0]
    lane = lax.broadcasted_iota(jnp.int32, (rows, LANES), 1)
    dense = jnp.zeros((rows, LANES), jnp.float32)
    for k in range(TOP):
        dense += jnp.where(ids_ref[:, k : k + 1] == lane, weights_ref[:, k : k + 1], 0.0)
    out_ref[...] = dense.T[: out_ref.shape[0]]


def spread(expert_ids, route_weights, expert_count):
    return pl.pallas_call(
        spread_kernel,
        out_shape=jax.ShapeDtypeStruct((expert_count, expert_ids.shape[0]), jnp.float32),
        name="spread",
    )(expert_ids, route_weights)


def expert_kernel(places, *refs):
    count = len(places)
    x_refs, weight_ref, halves = refs[:count], refs[count], refs[count + 1 : count + 7]
    out_refs, (x, total) = refs[count + 7 : count + 7 + count], refs[count + 7 + count :]
    step, steps = pl.program_id(0), pl.num_programs(0)
    rows = x_refs[0].shape[0]

    @pl.when(step == 0)
    def _():
        for index, ref in enumerate(x_refs):
            x[index * rows : (index + 1) * rows] = ref[...]

    def tile(gate_ref, up_ref, down_ref):
        gate_pre = mm(x[...], gate_ref[...])
        up_pre = mm(x[...], up_ref[...])
        activated = gate_pre * jax.nn.sigmoid(1.702 * gate_pre) * (up_pre + 1.0)
        part = mm(activated.astype(jnp.bfloat16), down_ref[...])

        @pl.when(step == 0)
        def _():
            total[...] = part

        @pl.when(step > 0)
        def _():
            total[...] += part

    @pl.when(step < steps // 2)
    def _():
        tile(*halves[:3])

    @pl.when(step >= steps // 2)
    def _():
        tile(*halves[3:])

    @pl.when(step == steps - 1)
    def _():
        columns = weight_ref[...].T
        for index, ((source, start), ref) in enumerate(zip(places, out_refs)):
            scale = columns[start : start + rows, source : source + 1]
            ref[...] = (total[index * rows : (index + 1) * rows] * scale).astype(jnp.bfloat16)


def experts(blocks, places, weights, halves):
    rows, model = blocks[0].shape
    half = halves[0].shape[1]
    tile = min(256, half)
    tiles = half // tile
    block = pl.BlockSpec((rows, model), lambda i: (0, 0))

    def columns(low):
        return pl.BlockSpec((model, tile), lambda i: (0, jnp.clip(i - low, 0, tiles - 1)))

    def lines(low):
        return pl.BlockSpec((tile, model), lambda i: (jnp.clip(i - low, 0, tiles - 1), 0))

    total_rows = rows * len(blocks)
    return pl.pallas_call(
        functools.partial(expert_kernel, tuple(places)),
        grid=(2 * tiles,),
        in_specs=[block] * len(blocks)
        + [pl.BlockSpec(weights.shape, lambda i: (0, 0))]
        + [columns(0), columns(0), lines(0), columns(tiles), columns(tiles), lines(tiles)],
        out_specs=[block] * len(blocks),
        out_shape=[jax.ShapeDtypeStruct((rows, model), jnp.bfloat16)] * len(blocks),
        scratch_shapes=[
            pltpu.VMEM((total_rows, model), jnp.bfloat16),
            pltpu.VMEM((total_rows, model), jnp.float32),
        ],
        compiler_params=pltpu.CompilerParams(vmem_limit_bytes=40 * MIB),
        cost_estimate=pl.CostEstimate(
            flops=12 * total_rows * model * half,
            bytes_accessed=12 * model * half,
            transcendentals=2 * total_rows * half,
        ),
        name="experts",
    )(*blocks, weights, *halves)


def ring_experts(
    residual, pieces, expert_ids, route_weights, gate_weight, up_weight, down_weight, others
):
    chips = lax.axis_size("seq")
    ring = SNAKES.get(chips, tuple(range(chips)))
    far = chips // 2
    ahead = [(ring[i], ring[(i + 1) % chips]) for i in range(chips)]
    back = [(to, of) for of, to in ahead]
    me = lax.axis_index("seq")
    rows = pieces[0].shape[0]

    known = spread(expert_ids, route_weights, chips)
    bit = 1
    while bit < chips:
        known = jnp.concatenate([known, swapped(known, "seq", bit)], axis=0)
        bit *= 2
    known = known.reshape(chips, chips, -1)
    place_of = [ring.index(i) for i in range(chips)]
    mine = jnp.array(place_of, jnp.int32)[me]
    source = jnp.array(ring, jnp.int32)[(mine - jnp.arange(chips, dtype=jnp.int32)) % chips]
    wanted = (
        ((me ^ source)[:, None, None] == jnp.arange(chips, dtype=jnp.int32)[None, :, None])
        & (jnp.arange(chips, dtype=jnp.int32)[None, None, :] == me)
    )
    weights = jnp.sum(jnp.where(wanted[..., None], known[None], 0.0), axis=(1, 2))

    halves = (gate_weight, up_weight, down_weight) + tuple(others)
    lead, trail = 0, 1
    came = [{(0, 0): pieces[0], (0, 1): pieces[1]}, {(0, 0): pieces[0], (0, 1): pieces[1]}]
    hops = (ahead, back)
    leads = (0, 1)

    def bring(distance, kind):
        for side in range(2):
            piece = leads[side] if kind == lead else 1 - leads[side]
            came[side][distance, piece] = lax.ppermute(
                came[side][distance - 1, piece], "seq", hops[side]
            )

    given = {}

    def apply(keys):
        blocks, places = [], []
        for side, distance, piece in keys:
            blocks.append(came[side][distance, piece])
            places.append(((distance if side == 0 else -distance) % chips, piece * rows))
        outs = experts(blocks, places, weights, halves)
        for (at, start), out in zip(places, outs):
            given[at, start // rows] = out

    for distance in range(1, far):
        bring(distance, lead)
        bring(distance, trail)
    bring(far, lead)
    for distance in range(1, far):
        keys = [(side, distance, piece) for side in range(2) for piece in range(2)]
        if distance == 1:
            keys = [(0, 0, 0), (0, 0, 1)] + keys
        if distance < far - 1:
            apply(keys)
    apply(
        [(side, far - 1, leads[side]) for side in range(2)]
        + [(side, far, leads[side]) for side in range(2)]
    )
    apply([(side, far - 1, 1 - leads[side]) for side in range(2)])

    def own(side, distance, piece):
        return given[(-distance if side == 0 else distance) % chips, piece]

    def plus(a, b):
        return (a.astype(jnp.float32) + b.astype(jnp.float32)).astype(jnp.bfloat16)

    moving = {}
    for distance in range(far, 0, -1):
        for kind in (trail, lead):
            if distance == far and kind == trail:
                continue
            for side in range(2):
                piece = leads[side] if kind == lead else 1 - leads[side]
                value = own(side, distance, piece)
                if (side, piece) in moving:
                    value = plus(moving[side, piece], value)
                moving[side, piece] = lax.ppermute(value, "seq", hops[side])
    final = []
    for piece in range(2):
        total = given[0, piece].astype(jnp.float32)
        for side in range(2):
            total += moving[side, piece].astype(jnp.float32)
        final.append(total)
    return (residual.astype(jnp.float32) + jnp.concatenate(final, axis=0)).astype(jnp.bfloat16)


def dispatched_experts(
    residual, normed, expert_ids, route_weights, gate_weight, up_weight, down_weight
):
    tokens_here = normed.shape[0]
    resid_f = residual.astype(jnp.float32)
    expert_count = EXP_DEV * lax.axis_size("seq")
    capacity = max(2, 3 * tokens_here * TOP // (2 * expert_count))
    flat_ids = expert_ids.reshape(-1)
    onehot = (flat_ids[:, None] == jnp.arange(expert_count, dtype=jnp.int32)[None, :]).astype(
        jnp.int32
    )
    earlier_count = jnp.cumsum(onehot, axis=0) - onehot
    slot_index = jnp.sum(earlier_count * onehot, axis=1)
    cell_index = (flat_ids * capacity + slot_index).reshape(tokens_here, TOP)
    chooser = jnp.any(
        cell_index[None, :, :]
        == jnp.arange(expert_count * capacity, dtype=jnp.int32)[:, None, None],
        axis=2,
    ).astype(jnp.bfloat16)
    outgoing = mm(chooser, normed).astype(jnp.bfloat16)
    outgoing = outgoing.reshape(expert_count, capacity, normed.shape[1])
    paired = lax.all_gather(outgoing, "rep", axis=1, tiled=True)
    arrived = lax.all_to_all(paired, "seq", split_axis=0, concat_axis=1, tiled=True)[0]
    gate_pre = mm(arrived, gate_weight)
    up_pre = mm(arrived, up_weight)
    activated = (gate_pre * jax.nn.sigmoid(1.702 * gate_pre) * (up_pre + 1.0)).astype(jnp.bfloat16)
    returned = lax.all_to_all(
        mm(activated, down_weight).astype(jnp.bfloat16)[None],
        "seq",
        split_axis=1,
        concat_axis=0,
        tiled=True,
    )
    expert_out = lax.psum_scatter(returned, "rep", scatter_dimension=1, tiled=True)
    picked = expert_out.reshape(expert_count * capacity, -1)[cell_index.reshape(-1)]
    picked = picked.reshape(tokens_here, TOP, -1)
    expert_sum = jnp.sum(route_weights[:, :, None] * picked.astype(jnp.float32), axis=1)
    return (resid_f + expert_sum).astype(jnp.bfloat16)


def per_device(
    stream,
    queries,
    key_rows,
    value_rows,
    sink_logits,
    out_weight,
    norm_gain,
    expert_ids,
    route_weights,
    gate_weight,
    up_weight,
    down_weight,
):
    block_len = queries.shape[0]
    seq = lax.axis_index("seq")
    rank = lax.axis_index("rep").astype(jnp.int32).reshape(1)
    gate_weight, up_weight, down_weight = gate_weight[0], up_weight[0], down_weight[0]
    use_ring = EXP_DEV * lax.axis_size("seq") <= 2 * TOP

    tail = jnp.concatenate([key_rows[block_len - WINDOW :], value_rows[block_len - WINDOW :]], axis=1)
    earlier = shifted(tail, "seq", 1)
    if use_ring:
        others = [swapped(w, "rep") for w in (gate_weight, up_weight, down_weight)]
    never = jnp.zeros((1,), jnp.int32)
    first = (seq == 0).astype(jnp.int32).reshape(1)
    later_half = attend(
        1,
        never,
        sink_logits,
        queries,
        ((key_rows, 0), (key_rows, 1)),
        ((value_rows, 0), (value_rows, 1)),
        out_weight,
    )
    k_prev, v_prev = earlier[:, : key_rows.shape[1]], earlier[:, key_rows.shape[1] :]
    send, own = attend(
        0,
        first,
        sink_logits,
        queries,
        ((k_prev, 0), (key_rows, 0)),
        ((v_prev, 0), (value_rows, 0)),
        out_weight,
        rank,
        later_half,
    )
    came = swapped(send, "rep")
    residual, *pieces = norm(stream, own, came, norm_gain, 2)
    if use_ring:
        return ring_experts(
            residual,
            pieces,
            expert_ids,
            route_weights,
            gate_weight,
            up_weight,
            down_weight,
            others,
        )
    return dispatched_experts(
        residual,
        jnp.concatenate(pieces, axis=0),
        expert_ids,
        route_weights,
        gate_weight,
        up_weight,
        down_weight,
    )


def solution(mesh):
    return jax.shard_map(
        per_device,
        mesh=mesh,
        in_specs=(
            P(("groups", "seq", "rep"), None),
            P(("groups", "seq"), "rep"),
            P(("groups", "seq"), "rep"),
            P(("groups", "seq"), "rep"),
            P("rep"),
            P("rep", None),
            P(),
            P(("groups", "seq", "rep"), None),
            P(("groups", "seq", "rep"), None),
            P("seq", None, "rep"),
            P("seq", None, "rep"),
            P("seq", "rep", None),
        ),
        out_specs=P(("groups", "seq", "rep"), None),
        check_vma=False,
    )
```

```python
import functools
import math

import jax
import jax.numpy as jnp
from jax import lax
from jax.experimental import pallas as pl
from jax.experimental.pallas import tpu as pltpu
from jax.sharding import PartitionSpec as P

HEAD_DIM = 64
WINDOW = 128
TOP = 4
EXP_DEV = 1
LANES = 128
SNAKES = {8: (0, 2, 4, 6, 7, 5, 3, 1)}
MIB = 1 << 20
EXPERT_VMEM = 16 * MIB


def shifted(value, axis, by):
    peers = lax.axis_size(axis)
    pairs = [(i, i + by) for i in range(peers) if 0 <= i + by < peers]
    return lax.ppermute(value, axis, pairs)


def swapped(value, axis, bit=1):
    peers = lax.axis_size(axis)
    return lax.ppermute(value, axis, [(i, i ^ bit) for i in range(peers)])


def mm(a, b):
    return jnp.dot(a, b, preferred_element_type=jnp.float32)


def attend_kernel(
    group_pairs, first_ref, sink_ref, q_ref, kp_ref, kc_ref, vp_ref, vc_ref, ow_ref, *rest
):
    mix = len(rest) > 2
    if mix:
        rank_ref, other_ref, send_ref, own_ref, total = rest
    else:
        out_ref, total = rest
    step = pl.program_id(0)
    rows = q_ref.shape[0]
    keys = kp_ref.shape[0] + kc_ref.shape[0]
    pairs_step = q_ref.shape[1] // LANES
    group = (step * pairs_step) // group_pairs

    lane_k = lax.broadcasted_iota(jnp.int32, (keys, LANES), 1)
    low = lane_k < HEAD_DIM
    k = jnp.concatenate([kp_ref[...], kc_ref[...]], axis=0).astype(jnp.float32)
    v = jnp.concatenate([vp_ref[...], vc_ref[...]], axis=0).astype(jnp.float32)
    k_low = jnp.where(low, jnp.where(group == 0, k, pltpu.roll(k, HEAD_DIM, 1)), 0.0)
    v_low = jnp.where(low, jnp.where(group == 0, v, pltpu.roll(v, HEAD_DIM, 1)), 0.0)
    k_high, v_high = pltpu.roll(k_low, HEAD_DIM, 1), pltpu.roll(v_low, HEAD_DIM, 1)
    kk = jnp.concatenate([k_low, k_high], axis=0).astype(jnp.bfloat16)
    one_low = jnp.where(low, 1.0, 0.0)
    vv = jnp.concatenate(
        [
            jnp.concatenate([v_low, one_low], axis=1),
            jnp.concatenate([v_high, 1.0 - one_low], axis=1),
        ],
        axis=0,
    ).astype(jnp.bfloat16)

    row = lax.broadcasted_iota(jnp.int32, (rows, keys), 0)
    column = lax.broadcasted_iota(jnp.int32, (rows, keys), 1)
    least = jnp.where(first_ref[0] == 1, WINDOW, 0)
    allowed = (column <= row + WINDOW) & (column > row) & (column >= least)
    low_out = lax.broadcasted_iota(jnp.int32, (rows, LANES), 1) < HEAD_DIM
    scale = 1.0 / math.sqrt(HEAD_DIM)

    done = []
    for pair in range(pairs_step):
        q = q_ref[:, pair * LANES : (pair + 1) * LANES]
        scores = lax.dot_general(
            q, kk, (((1,), (1,)), ((), ())), preferred_element_type=jnp.float32
        )
        weights, sinks = [], []
        for side in range(2):
            part = jnp.where(allowed, scores[:, side * keys : (side + 1) * keys] * scale, -jnp.inf)
            sink = sink_ref[(step * pairs_step + pair) * 2 + side]
            highest = jnp.maximum(jnp.max(part, axis=1, keepdims=True), sink)
            weights.append(jnp.exp(part - highest).astype(jnp.bfloat16))
            sinks.append(jnp.exp(sink - highest))
        both = mm(jnp.concatenate(weights, axis=1), vv)
        below = both[:, LANES:] + jnp.where(low_out, sinks[0], sinks[1])
        done.append((both[:, :LANES] / below).astype(jnp.bfloat16))
    part = mm(jnp.concatenate(done, axis=1), ow_ref[...])

    @pl.when(step == 0)
    def _():
        total[...] = part

    @pl.when(step > 0)
    def _():
        total[...] += part

    @pl.when(step == pl.num_programs(0) - 1)
    def _():
        if mix:
            mine = total[...]
            other = other_ref[...]
            own_first = rank_ref[0] == 0
            own_ref[...] = jnp.where(own_first, mine, other)
            send_ref[...] = jnp.where(own_first, other, mine).astype(jnp.bfloat16)
        else:
            out_ref[...] = total[...]


def attend(half, first, sinks, queries, keys, values, out_weight, rank=None, other=None):
    (k_prev, kp_index), (k_cur, kc_index) = keys
    (v_prev, vp_index), (v_cur, vc_index) = values
    rows, width, model = WINDOW, queries.shape[1], out_weight.shape[1]
    block = min(width, 256)
    group_pairs = width // LANES // (k_cur.shape[1] // HEAD_DIM)
    smem = pl.BlockSpec(memory_space=pltpu.SMEM)

    def fixed(index):
        return pl.BlockSpec((rows, LANES), lambda i: (index, 0))

    in_specs = [
        smem,
        smem,
        pl.BlockSpec((rows, block), lambda i: (half, i)),
        fixed(kp_index),
        fixed(kc_index),
        fixed(vp_index),
        fixed(vc_index),
        pl.BlockSpec((block, model), lambda i: (i, 0)),
    ]
    operands = [first, sinks, queries, k_prev, k_cur, v_prev, v_cur, out_weight]
    whole = pl.BlockSpec((rows, model), lambda i: (0, 0))
    wide = jax.ShapeDtypeStruct((rows, model), jnp.float32)
    narrow = jax.ShapeDtypeStruct((rows, model), jnp.bfloat16)
    if rank is None:
        out_shape, out_specs = wide, whole
    else:
        in_specs += [smem, whole]
        operands += [rank, other]
        out_shape, out_specs = (narrow, wide), (whole, whole)
    return pl.pallas_call(
        functools.partial(attend_kernel, group_pairs),
        grid=(width // block,),
        in_specs=in_specs,
        out_specs=out_specs,
        out_shape=out_shape,
        scratch_shapes=[pltpu.VMEM((rows, model), jnp.float32)],
        compiler_params=pltpu.CompilerParams(vmem_limit_bytes=48 * MIB),
        cost_estimate=pl.CostEstimate(
            flops=2 * rows * width * (model + 1024), bytes_accessed=6 * MIB, transcendentals=0
        ),
        name="attend",
    )(*operands)


def norm_kernel(
    expert_count, stream_ref, own_ref, came_ref, gain_ref, ids_ref, route_ref, *rest
):
    residual_ref, message_ref = rest[-2:]
    rows, model = stream_ref.shape
    residual = (
        stream_ref[...].astype(jnp.float32) + own_ref[...] + came_ref[...].astype(jnp.float32)
    ).astype(jnp.bfloat16)
    residual_ref[...] = residual
    wide = residual.astype(jnp.float32)
    mean = jnp.mean(wide * wide, axis=-1, keepdims=True)
    normed = (wide * lax.rsqrt(mean + 1e-05) * gain_ref[...]).astype(jnp.bfloat16)
    message_ref[:, :model] = normed
    if expert_count:
        expert = lax.broadcasted_iota(jnp.int32, (LANES, rows), 0)
        dense = jnp.zeros((LANES, rows), jnp.float32)
        for k in range(TOP):
            named = ids_ref[k : k + 1, :]
            hit = (expert == named) | (expert == named + expert_count)
            dense += jnp.where(hit, route_ref[k : k + 1, :], 0.0)
        lead = dense.astype(jnp.bfloat16).astype(jnp.float32)
        both = jnp.where(expert < expert_count, lead, dense - lead)
        message_ref[:, model:] = both.T.astype(jnp.bfloat16)


def norm(stream, own, came, gain, expert_ids, route_weights, expert_count, after):
    rows, model = stream.shape
    vmem = pl.BlockSpec(memory_space=pltpu.VMEM)
    extra = LANES if expert_count else 0
    return pl.pallas_call(
        functools.partial(norm_kernel, expert_count),
        in_specs=[vmem] * 6 + [pl.BlockSpec(memory_space=pl.ANY)] * len(after),
        out_shape=[
            jax.ShapeDtypeStruct((rows, model), jnp.bfloat16),
            jax.ShapeDtypeStruct((rows, model + extra), jnp.bfloat16),
        ],
        compiler_params=pltpu.CompilerParams(vmem_limit_bytes=16 * MIB),
        cost_estimate=pl.CostEstimate(
            flops=8 * rows * model, bytes_accessed=14 * rows * model, transcendentals=rows
        ),
        name="norm",
    )(stream, own, came, gain.reshape(1, model), expert_ids.T, route_weights.T, *after)


def expert_kernel(tile, expert_count, count, me_ref, *refs):
    x_refs, halves = refs[:count], refs[count : count + 6]
    out_refs, (x, total) = refs[count + 6 : 2 * count + 6], refs[2 * count + 6 :]
    model = halves[0].shape[0]
    starts = [0]
    for ref in x_refs:
        starts.append(starts[-1] + ref.shape[0])
    for start, ref in zip(starts, x_refs):
        x[start : start + ref.shape[0]] = ref[:, :model]
    total[...] = jnp.zeros_like(total)

    @pl.loop(0, halves[0].shape[1] // tile)
    def _(index):
        span = pl.ds(pl.multiple_of(index * tile, tile), tile)
        rows = x[...]
        parts = []
        for gate_ref, up_ref, down_ref in (halves[:3], halves[3:]):
            gate_pre = mm(rows, gate_ref[:, span])
            up_pre = mm(rows, up_ref[:, span])
            activated = gate_pre * jax.nn.sigmoid(1.702 * gate_pre) * (up_pre + 1.0)
            parts.append(mm(activated.astype(jnp.bfloat16), down_ref[span, :]))
        total[...] += parts[0] + parts[1]

    me = me_ref[0]
    for start, ref, out_ref in zip(starts, x_refs, out_refs):
        rows = ref.shape[0]
        sent = ref[:, model:].astype(jnp.float32)
        lane = lax.broadcasted_iota(jnp.int32, sent.shape, 1)
        mine = (lane == me) | (lane == me + expert_count)
        scale = jnp.sum(jnp.where(mine, sent, 0.0), axis=1, keepdims=True)
        out_ref[...] = (total[start : start + rows] * scale).astype(jnp.bfloat16)


def experts(blocks, me, halves, expert_count):
    model, half = halves[0].shape
    rows = sum(block.shape[0] for block in blocks)
    vmem = pl.BlockSpec(memory_space=pltpu.VMEM)
    return pl.pallas_call(
        functools.partial(expert_kernel, min(256, half), expert_count, len(blocks)),
        in_specs=[pl.BlockSpec(memory_space=pltpu.SMEM)] + [vmem] * (len(blocks) + 6),
        out_specs=[vmem] * len(blocks),
        out_shape=[jax.ShapeDtypeStruct((b.shape[0], model), jnp.bfloat16) for b in blocks],
        scratch_shapes=[
            pltpu.VMEM((rows, model), jnp.bfloat16),
            pltpu.VMEM((rows, model), jnp.float32),
        ],
        compiler_params=pltpu.CompilerParams(vmem_limit_bytes=EXPERT_VMEM),
        cost_estimate=pl.CostEstimate(
            flops=12 * rows * model * half, bytes_accessed=6 * rows * model, transcendentals=0
        ),
        name="experts",
    )(me, *blocks, *halves)


def ring_experts(residual, message, gate_weight, up_weight, down_weight, others):
    chips = lax.axis_size("seq")
    ring = SNAKES.get(chips, tuple(range(chips)))
    far = chips // 2
    ahead = [(ring[i], ring[(i + 1) % chips]) for i in range(chips)]
    hops = (ahead, [(to, of) for of, to in ahead])
    me = lax.axis_index("seq").astype(jnp.int32).reshape(1)
    half = message.shape[0] // 2
    spans = (slice(0, half), slice(half, 2 * half))
    halves = (gate_weight, up_weight, down_weight) + tuple(others)

    def apply(*blocks):
        return experts(blocks, me, halves, chips)

    came = [[message], [message]]
    given = [[None], [None]]
    for distance in range(1, far + 1):
        for side in range(2):
            block = came[side][distance - 1]
            if distance == far:
                block = block[spans[side]]
            came[side].append(lax.ppermute(block, "seq", hops[side]))
    (mine,) = apply(message)
    for distance in range(1, far + 1):
        outs = apply(came[0][distance], came[1][distance])
        given[0].append(outs[0])
        given[1].append(outs[1])

    wide = lambda value: value.astype(jnp.float32)
    total = wide(residual) + wide(mine)
    for side in range(2):
        moving = lax.ppermute(given[side][far], "seq", hops[side])
        for distance in range(far - 1, 0, -1):
            value = given[1 - side][distance]
            if distance == far - 1:
                parts = [value[spans[0]], value[spans[1]]]
                parts[side] = (wide(moving) + wide(parts[side])).astype(jnp.bfloat16)
                value = jnp.concatenate(parts, axis=0)
            else:
                value = (wide(moving) + wide(value)).astype(jnp.bfloat16)
            moving = lax.ppermute(value, "seq", hops[side])
        total += wide(moving)
    return total.astype(jnp.bfloat16)


def dispatched_experts(
    residual, normed, expert_ids, route_weights, gate_weight, up_weight, down_weight
):
    tokens_here = normed.shape[0]
    resid_f = residual.astype(jnp.float32)
    expert_count = EXP_DEV * lax.axis_size("seq")
    capacity = max(2, 3 * tokens_here * TOP // (2 * expert_count))
    flat_ids = expert_ids.reshape(-1)
    onehot = (flat_ids[:, None] == jnp.arange(expert_count, dtype=jnp.int32)[None, :]).astype(
        jnp.int32
    )
    earlier_count = jnp.cumsum(onehot, axis=0) - onehot
    slot_index = jnp.sum(earlier_count * onehot, axis=1)
    cell_index = (flat_ids * capacity + slot_index).reshape(tokens_here, TOP)
    chooser = jnp.any(
        cell_index[None, :, :]
        == jnp.arange(expert_count * capacity, dtype=jnp.int32)[:, None, None],
        axis=2,
    ).astype(jnp.bfloat16)
    outgoing = mm(chooser, normed).astype(jnp.bfloat16)
    outgoing = outgoing.reshape(expert_count, capacity, normed.shape[1])
    paired = lax.all_gather(outgoing, "rep", axis=1, tiled=True)
    arrived = lax.all_to_all(paired, "seq", split_axis=0, concat_axis=1, tiled=True)[0]
    gate_pre = mm(arrived, gate_weight)
    up_pre = mm(arrived, up_weight)
    activated = (gate_pre * jax.nn.sigmoid(1.702 * gate_pre) * (up_pre + 1.0)).astype(jnp.bfloat16)
    returned = lax.all_to_all(
        mm(activated, down_weight).astype(jnp.bfloat16)[None],
        "seq",
        split_axis=1,
        concat_axis=0,
        tiled=True,
    )
    expert_out = lax.psum_scatter(returned, "rep", scatter_dimension=1, tiled=True)
    picked = expert_out.reshape(expert_count * capacity, -1)[cell_index.reshape(-1)]
    picked = picked.reshape(tokens_here, TOP, -1)
    expert_sum = jnp.sum(route_weights[:, :, None] * picked.astype(jnp.float32), axis=1)
    return (resid_f + expert_sum).astype(jnp.bfloat16)


def per_device(
    stream,
    queries,
    key_rows,
    value_rows,
    sink_logits,
    out_weight,
    norm_gain,
    expert_ids,
    route_weights,
    gate_weight,
    up_weight,
    down_weight,
):
    block_len = queries.shape[0]
    seq = lax.axis_index("seq")
    rank = lax.axis_index("rep").astype(jnp.int32).reshape(1)
    gate_weight, up_weight, down_weight = gate_weight[0], up_weight[0], down_weight[0]
    use_ring = EXP_DEV * lax.axis_size("seq") <= 2 * TOP

    k_before, v_before = shifted(key_rows, "seq", 1), shifted(value_rows, "seq", 1)
    others = []
    if use_ring:
        others = [swapped(w, "rep") for w in (gate_weight, up_weight, down_weight)]
    never = jnp.zeros((1,), jnp.int32)
    first = (seq == 0).astype(jnp.int32).reshape(1)
    last = block_len // WINDOW - 1
    later_half = attend(
        1,
        never,
        sink_logits,
        queries,
        ((key_rows, 0), (key_rows, 1)),
        ((value_rows, 0), (value_rows, 1)),
        out_weight,
    )
    send, own = attend(
        0,
        first,
        sink_logits,
        queries,
        ((k_before, last), (key_rows, 0)),
        ((v_before, last), (value_rows, 0)),
        out_weight,
        rank,
        later_half,
    )
    came = swapped(send, "rep")
    expert_count = lax.axis_size("seq") * EXP_DEV if use_ring else 0
    residual, message = norm(
        stream, own, came, norm_gain, expert_ids, route_weights, expert_count, others
    )
    if use_ring:
        return ring_experts(residual, message, gate_weight, up_weight, down_weight, others)
    return dispatched_experts(
        residual, message, expert_ids, route_weights, gate_weight, up_weight, down_weight
    )


def solution(mesh):
    return jax.shard_map(
        per_device,
        mesh=mesh,
        in_specs=(
            P(("groups", "seq", "rep"), None),
            P(("groups", "seq"), "rep"),
            P(("groups", "seq"), "rep"),
            P(("groups", "seq"), "rep"),
            P("rep"),
            P("rep", None),
            P(),
            P(("groups", "seq", "rep"), None),
            P(("groups", "seq", "rep"), None),
            P("seq", None, "rep"),
            P("seq", None, "rep"),
            P("seq", "rep", None),
        ),
        out_specs=P(("groups", "seq", "rep"), None),
        check_vma=False,
    )
```

```python
import functools
import math

import jax
import jax.numpy as jnp
from jax import lax
from jax.experimental import pallas as pl
from jax.experimental.pallas import tpu as pltpu
from jax.sharding import PartitionSpec as P

HEAD_DIM = 64
WINDOW = 128
TOP = 4
EXP_DEV = 1
LANES = 128
SNAKES = {8: (0, 2, 4, 6, 7, 5, 3, 1)}
MIB = 1 << 20
EXPERT_VMEM = 8 * MIB


def shifted(value, axis, by):
    peers = lax.axis_size(axis)
    return lax.ppermute(value, axis, [(i, (i + by) % peers) for i in range(peers)])


def pinned(values, space):
    return [pltpu.with_memory_space_constraint(value, space) for value in values]


def tied(value, *after):
    return lax.optimization_barrier((value,) + after)[0]


def swapped(value, axis, bit=1):
    peers = lax.axis_size(axis)
    return lax.ppermute(value, axis, [(i, i ^ bit) for i in range(peers)])


def mm(a, b):
    return jnp.dot(a, b, preferred_element_type=jnp.float32)


def attend_kernel(half, mix, first_ref, sink_hbm, q_hbm, k_hbm, v_hbm, ow_hbm, *rest):
    if mix:
        k_before, v_before, rank_ref, other_ref, send_ref, own_ref = rest[:6]
    else:
        out_ref = rest[0]
    sink_ref, q_ref, k_ref, v_ref, ow_ref, done_ref, sems = rest[-7:]
    rows, keys = q_ref.shape[0], 2 * q_ref.shape[0]
    pairs = q_ref.shape[1] // LANES
    groups = k_ref.shape[1] // HEAD_DIM
    spans = (pl.ds(half * rows, rows), pl.ds(0, k_ref.shape[0]))
    copies = [
        pltpu.make_async_copy(k_hbm.at[spans[1]], k_ref, sems.at[0]),
        pltpu.make_async_copy(v_hbm.at[spans[1]], v_ref, sems.at[1]),
        pltpu.make_async_copy(q_hbm.at[spans[0]], q_ref, sems.at[2]),
        pltpu.make_async_copy(sink_hbm, sink_ref, sems.at[3]),
        pltpu.make_async_copy(ow_hbm, ow_ref, sems.at[4]),
    ]
    for copy in copies:
        copy.start()
    for copy in copies[:4]:
        copy.wait()

    low = lax.broadcasted_iota(jnp.int32, (keys, LANES), 1) < HEAD_DIM
    k, v = k_ref[...], v_ref[...]
    if mix:
        k = jnp.concatenate([k_before[rows:], k], axis=0)
        v = jnp.concatenate([v_before[rows:], v], axis=0)
    k = k.astype(jnp.float32) * (1.0 / math.sqrt(HEAD_DIM))
    v = v.astype(jnp.float32)
    k_turned, v_turned = pltpu.roll(k, HEAD_DIM, 1), pltpu.roll(v, HEAD_DIM, 1)
    one_low = jnp.where(low, 1.0, 0.0)

    row = lax.broadcasted_iota(jnp.int32, (rows, keys), 0)
    column = lax.broadcasted_iota(jnp.int32, (rows, keys), 1)
    allowed = (column <= row + rows) & (column > row)
    if mix:
        allowed = allowed & (column >= jnp.where(first_ref[0] == 1, rows, 0))
    low_out = lax.broadcasted_iota(jnp.int32, (rows, LANES), 1) < HEAD_DIM

    for group in range(groups):
        here, there = (k, v), (k_turned, v_turned)
        lows, highs = (here, there) if group == 0 else (there, here)
        kk = jnp.concatenate(
            [jnp.where(low, lows[0], 0.0), jnp.where(low, 0.0, highs[0])], axis=0
        ).astype(jnp.bfloat16)
        vv = jnp.concatenate(
            [
                jnp.concatenate([jnp.where(low, lows[1], 0.0), one_low], axis=1),
                jnp.concatenate([jnp.where(low, 0.0, highs[1]), 1.0 - one_low], axis=1),
            ],
            axis=0,
        ).astype(jnp.bfloat16)
        for pair in range(group * pairs // groups, (group + 1) * pairs // groups):
            lanes = slice(pair * LANES, (pair + 1) * LANES)
            scores = lax.dot_general(
                q_ref[:, lanes], kk, (((1,), (1,)), ((), ())), preferred_element_type=jnp.float32
            )
            weights, sinks = [], []
            for side in range(2):
                part = jnp.where(allowed, scores[:, side * keys : (side + 1) * keys], -jnp.inf)
                sink = sink_ref[:, 2 * pair + side : 2 * pair + side + 1]
                highest = jnp.maximum(jnp.max(part, axis=1, keepdims=True), sink)
                weights.append(jnp.exp(part - highest).astype(jnp.bfloat16))
                sinks.append(jnp.exp(sink - highest))
            both = mm(jnp.concatenate(weights, axis=1), vv)
            below = both[:, LANES:] + jnp.where(low_out, sinks[0], sinks[1])
            done_ref[:, lanes] = (both[:, :LANES] / below).astype(jnp.bfloat16)

    copies[4].wait()
    model = ow_ref.shape[1]
    width = 512 if model % 512 == 0 else model
    if mix:
        own_first = rank_ref[0] == 0
    for start in range(0, model, width):
        lanes = slice(start, start + width)
        mine = mm(done_ref[...], ow_ref[:, lanes])
        if mix:
            other = other_ref[:, lanes]
            own_ref[:, lanes] = jnp.where(own_first, mine, other)
            send_ref[:, lanes] = jnp.where(own_first, other, mine).astype(jnp.bfloat16)
        else:
            out_ref[:, lanes] = mine


def attend(half, first, sinks, queries, keys, values, out_weight, before=(), rank=None, other=None):
    mix = bool(before)
    rows, width, model = WINDOW, queries.shape[1], out_weight.shape[1]
    local = rows if mix else 2 * rows
    smem = pl.BlockSpec(memory_space=pltpu.SMEM)
    vmem = pl.BlockSpec(memory_space=pltpu.VMEM)
    hbm = pl.BlockSpec(memory_space=pltpu.HBM)
    wide = jax.ShapeDtypeStruct((rows, model), jnp.float32)
    narrow = jax.ShapeDtypeStruct((rows, model), jnp.bfloat16)
    return pl.pallas_call(
        functools.partial(attend_kernel, half, mix),
        in_specs=[smem] + [hbm] * 5 + ([vmem, vmem, smem, vmem] if mix else []),
        out_specs=(vmem, vmem) if mix else vmem,
        out_shape=(narrow, wide) if mix else wide,
        scratch_shapes=[
            pltpu.VMEM((1, sinks.shape[0]), jnp.float32),
            pltpu.VMEM((rows, width), jnp.bfloat16),
            pltpu.VMEM((local, LANES), jnp.bfloat16),
            pltpu.VMEM((local, LANES), jnp.bfloat16),
            pltpu.VMEM((width, model), jnp.bfloat16),
            pltpu.VMEM((rows, width), jnp.bfloat16),
            pltpu.SemaphoreType.DMA((5,)),
        ],
        compiler_params=pltpu.CompilerParams(vmem_limit_bytes=8 * MIB),
        cost_estimate=pl.CostEstimate(
            flops=2 * rows * width * (model + 1024), bytes_accessed=6 * MIB, transcendentals=0
        ),
        name="attend",
    )(
        first,
        *pinned((sinks.reshape(1, -1), queries, keys, values, out_weight), pltpu.HBM),
        *((*before, rank, other) if mix else ()),
    )


def norm_kernel(
    expert_count, stream_ref, own_ref, came_ref, gain_ref, ids_ref, route_ref, *rest
):
    residual_ref, message_ref = rest[-2:]
    rows, model = stream_ref.shape
    residual = (
        stream_ref[...].astype(jnp.float32) + own_ref[...] + came_ref[...].astype(jnp.float32)
    ).astype(jnp.bfloat16)
    residual_ref[...] = residual
    wide = residual.astype(jnp.float32)
    mean = jnp.mean(wide * wide, axis=-1, keepdims=True)
    normed = (wide * lax.rsqrt(mean + 1e-05) * gain_ref[...]).astype(jnp.bfloat16)
    message_ref[:, :model] = normed
    if expert_count:
        expert = lax.broadcasted_iota(jnp.int32, (LANES, rows), 0)
        dense = jnp.zeros((LANES, rows), jnp.float32)
        for k in range(TOP):
            named = ids_ref[k : k + 1, :]
            hit = (expert == named) | (expert == named + expert_count)
            dense += jnp.where(hit, route_ref[k : k + 1, :], 0.0)
        lead = dense.astype(jnp.bfloat16).astype(jnp.float32)
        both = jnp.where(expert < expert_count, lead, dense - lead)
        message_ref[:, model:] = both.T.astype(jnp.bfloat16)


def norm(stream, own, came, gain, expert_ids, route_weights, expert_count, after):
    rows, model = stream.shape
    vmem = pl.BlockSpec(memory_space=pltpu.VMEM)
    extra = LANES if expert_count else 0
    return pl.pallas_call(
        functools.partial(norm_kernel, expert_count),
        in_specs=[vmem] * 6 + [pl.BlockSpec(memory_space=pl.ANY)] * len(after),
        out_shape=[
            jax.ShapeDtypeStruct((rows, model), jnp.bfloat16),
            jax.ShapeDtypeStruct((rows, model + extra), jnp.bfloat16),
        ],
        compiler_params=pltpu.CompilerParams(vmem_limit_bytes=8 * MIB),
        cost_estimate=pl.CostEstimate(
            flops=8 * rows * model, bytes_accessed=14 * rows * model, transcendentals=rows
        ),
        name="norm",
    )(stream, own, came, gain.reshape(1, model), expert_ids.T, route_weights.T, *after)


def expert_kernel(tile, expert_count, count, me_ref, *refs):
    x_refs, halves = refs[:count], refs[count : count + 6]
    out_refs, (x, hidden) = refs[count + 6 : 2 * count + 6], refs[2 * count + 6 :]
    model, half = halves[0].shape
    starts = [0]
    for ref in x_refs:
        starts.append(starts[-1] + ref.shape[0])
    for start, ref in zip(starts, x_refs):
        x[start : start + ref.shape[0]] = ref[:, :model]

    for at in range(0, half, tile):
        for side in range(2):
            gate_ref, up_ref = halves[3 * side : 3 * side + 2]
            gate_pre = mm(x[...], gate_ref[:, at : at + tile])
            up_pre = mm(x[...], up_ref[:, at : at + tile])
            activated = gate_pre * jax.nn.sigmoid(1.702 * gate_pre) * (up_pre + 1.0)
            hidden[:, side * half + at : side * half + at + tile] = activated.astype(jnp.bfloat16)

    me = me_ref[0]
    scales = []
    for ref in x_refs:
        sent = ref[:, model:].astype(jnp.float32)
        lane = lax.broadcasted_iota(jnp.int32, sent.shape, 1)
        mine = (lane == me) | (lane == me + expert_count)
        scales.append(jnp.sum(jnp.where(mine, sent, 0.0), axis=1, keepdims=True))
    for at in range(0, model, tile):
        lanes = slice(at, at + tile)
        total = mm(hidden[:, :half], halves[2][:, lanes]) + mm(hidden[:, half:], halves[5][:, lanes])
        for start, ref, scale in zip(starts, out_refs, scales):
            ref[:, lanes] = (total[start : start + ref.shape[0]] * scale).astype(jnp.bfloat16)


def experts(blocks, me, halves, expert_count):
    model, half = halves[0].shape
    rows = sum(block.shape[0] for block in blocks)
    vmem = pl.BlockSpec(memory_space=pltpu.VMEM)
    return pl.pallas_call(
        functools.partial(expert_kernel, min(256, half), expert_count, len(blocks)),
        in_specs=[pl.BlockSpec(memory_space=pltpu.SMEM)] + [vmem] * (len(blocks) + 6),
        out_specs=[vmem] * len(blocks),
        out_shape=[jax.ShapeDtypeStruct((b.shape[0], model), jnp.bfloat16) for b in blocks],
        scratch_shapes=[
            pltpu.VMEM((rows, model), jnp.bfloat16),
            pltpu.VMEM((rows, 2 * half), jnp.bfloat16),
        ],
        compiler_params=pltpu.CompilerParams(vmem_limit_bytes=EXPERT_VMEM),
        cost_estimate=pl.CostEstimate(
            flops=12 * rows * model * half, bytes_accessed=6 * rows * model, transcendentals=0
        ),
        name="experts",
    )(me, *blocks, *pinned(halves, pltpu.VMEM))


def ring_experts(residual, message, gate_weight, up_weight, down_weight, others):
    chips = lax.axis_size("seq")
    ring = SNAKES.get(chips, tuple(range(chips)))
    far = chips // 2
    ahead = [(ring[i], ring[(i + 1) % chips]) for i in range(chips)]
    hops = (ahead, [(to, of) for of, to in ahead])
    me = lax.axis_index("seq").astype(jnp.int32).reshape(1)
    half = message.shape[0] // 2
    spans = (slice(0, half), slice(half, 2 * half))
    halves = (gate_weight, up_weight, down_weight) + tuple(others)

    def apply(*blocks):
        return experts(blocks, me, halves, chips)

    came = [[message], [message]]
    given = [[None], [None]]
    (mine,) = apply(message)
    worked = [mine]
    for distance in range(1, far + 1):
        for side in range(2):
            block = came[side][distance - 1]
            if distance == far:
                block = block[spans[side]]
            if distance > 1:
                block = tied(block, worked[distance - 2])
            came[side].append(lax.ppermute(block, "seq", hops[side]))
        if distance < far:
            outs = apply(came[0][distance], came[1][distance])
        else:
            outs = apply(tied(came[0][far], worked[far - 1]), came[1][far])
        worked.append(outs[0])
        given[0].append(outs[0])
        given[1].append(outs[1])

    wide = lambda value: value.astype(jnp.float32)
    total = wide(residual) + wide(mine)
    for side in range(2):
        moving = lax.ppermute(given[side][far], "seq", hops[side])
        for distance in range(far - 1, 0, -1):
            value = given[1 - side][distance]
            if distance == far - 1:
                parts = [value[spans[0]], value[spans[1]]]
                parts[side] = (wide(moving) + wide(parts[side])).astype(jnp.bfloat16)
                value = jnp.concatenate(parts, axis=0)
            else:
                value = (wide(moving) + wide(value)).astype(jnp.bfloat16)
            moving = lax.ppermute(value, "seq", hops[side])
        total += wide(moving)
    return total.astype(jnp.bfloat16)


def dispatched_experts(
    residual, normed, expert_ids, route_weights, gate_weight, up_weight, down_weight
):
    tokens_here = normed.shape[0]
    resid_f = residual.astype(jnp.float32)
    expert_count = EXP_DEV * lax.axis_size("seq")
    capacity = max(2, 3 * tokens_here * TOP // (2 * expert_count))
    flat_ids = expert_ids.reshape(-1)
    onehot = (flat_ids[:, None] == jnp.arange(expert_count, dtype=jnp.int32)[None, :]).astype(
        jnp.int32
    )
    earlier_count = jnp.cumsum(onehot, axis=0) - onehot
    slot_index = jnp.sum(earlier_count * onehot, axis=1)
    cell_index = (flat_ids * capacity + slot_index).reshape(tokens_here, TOP)
    chooser = jnp.any(
        cell_index[None, :, :]
        == jnp.arange(expert_count * capacity, dtype=jnp.int32)[:, None, None],
        axis=2,
    ).astype(jnp.bfloat16)
    outgoing = mm(chooser, normed).astype(jnp.bfloat16)
    outgoing = outgoing.reshape(expert_count, capacity, normed.shape[1])
    paired = lax.all_gather(outgoing, "rep", axis=1, tiled=True)
    arrived = lax.all_to_all(paired, "seq", split_axis=0, concat_axis=1, tiled=True)[0]
    gate_pre = mm(arrived, gate_weight)
    up_pre = mm(arrived, up_weight)
    activated = (gate_pre * jax.nn.sigmoid(1.702 * gate_pre) * (up_pre + 1.0)).astype(jnp.bfloat16)
    returned = lax.all_to_all(
        mm(activated, down_weight).astype(jnp.bfloat16)[None],
        "seq",
        split_axis=1,
        concat_axis=0,
        tiled=True,
    )
    expert_out = lax.psum_scatter(returned, "rep", scatter_dimension=1, tiled=True)
    picked = expert_out.reshape(expert_count * capacity, -1)[cell_index.reshape(-1)]
    picked = picked.reshape(tokens_here, TOP, -1)
    expert_sum = jnp.sum(route_weights[:, :, None] * picked.astype(jnp.float32), axis=1)
    return (resid_f + expert_sum).astype(jnp.bfloat16)


def per_device(
    stream,
    queries,
    key_rows,
    value_rows,
    sink_logits,
    out_weight,
    norm_gain,
    expert_ids,
    route_weights,
    gate_weight,
    up_weight,
    down_weight,
):
    block_len = queries.shape[0]
    seq = lax.axis_index("seq")
    rank = lax.axis_index("rep").astype(jnp.int32).reshape(1)
    gate_weight, up_weight, down_weight = gate_weight[0], up_weight[0], down_weight[0]
    use_ring = EXP_DEV * lax.axis_size("seq") <= 2 * TOP

    k_before, v_before = shifted(key_rows, "seq", 1), shifted(value_rows, "seq", 1)
    others = []
    if use_ring:
        others = [swapped(w, "rep") for w in (gate_weight, up_weight, down_weight)]
    never = jnp.zeros((1,), jnp.int32)
    first = (seq == 0).astype(jnp.int32).reshape(1)
    shared = (sink_logits, queries, key_rows, value_rows, out_weight)
    later_half = attend(1, never, *shared)
    send, own = attend(0, first, *shared, (k_before, v_before), rank, later_half)
    came = swapped(send, "rep")
    expert_count = lax.axis_size("seq") * EXP_DEV if use_ring else 0
    residual, message = norm(
        stream, own, came, norm_gain, expert_ids, route_weights, expert_count, []
    )
    message, *others = lax.optimization_barrier((message, *others))
    if use_ring:
        return ring_experts(residual, message, gate_weight, up_weight, down_weight, others)
    return dispatched_experts(
        residual, message, expert_ids, route_weights, gate_weight, up_weight, down_weight
    )


def solution(mesh):
    return jax.shard_map(
        per_device,
        mesh=mesh,
        in_specs=(
            P(("groups", "seq", "rep"), None),
            P(("groups", "seq"), "rep"),
            P(("groups", "seq"), "rep"),
            P(("groups", "seq"), "rep"),
            P("rep"),
            P("rep", None),
            P(),
            P(("groups", "seq", "rep"), None),
            P(("groups", "seq", "rep"), None),
            P("seq", None, "rep"),
            P("seq", None, "rep"),
            P("seq", "rep", None),
        ),
        out_specs=P(("groups", "seq", "rep"), None),
        check_vma=False,
    )
```

```python
import functools
import math

import jax
import jax.numpy as jnp
from jax import lax
from jax.experimental import pallas as pl
from jax.experimental.pallas import tpu as pltpu
from jax.sharding import PartitionSpec as P

HEAD_DIM = 64
WINDOW = 128
TOP = 4
EXP_DEV = 1
LANES = 128
SNAKES = {8: (0, 2, 4, 6, 7, 5, 3, 1)}
MIB = 1 << 20
EXPERT_VMEM = 8 * MIB


def shifted(value, axis, by):
    peers = lax.axis_size(axis)
    return lax.ppermute(value, axis, [(i, (i + by) % peers) for i in range(peers)])


def pinned(values, space):
    return [pltpu.with_memory_space_constraint(value, space) for value in values]


def tied(value, *after):
    return lax.optimization_barrier((value,) + after)[0]


def swapped(value, axis, bit=1):
    peers = lax.axis_size(axis)
    return lax.ppermute(value, axis, [(i, i ^ bit) for i in range(peers)])


def mm(a, b):
    return jnp.dot(a, b, preferred_element_type=jnp.float32)


def attend_kernel(half, mix, first_ref, sink_hbm, q_hbm, k_hbm, v_hbm, ow_hbm, *rest):
    if mix:
        k_before, v_before, rank_ref, other_ref, send_ref, own_ref = rest[:6]
    else:
        out_ref = rest[0]
    sink_ref, q_ref, k_ref, v_ref, ow_ref, done_ref, sems = rest[-7:]
    rows, keys = q_ref.shape[0], 2 * q_ref.shape[0]
    pairs = q_ref.shape[1] // LANES
    groups = k_ref.shape[1] // HEAD_DIM
    spans = (pl.ds(half * rows, rows), pl.ds(0, k_ref.shape[0]))
    copies = [
        pltpu.make_async_copy(k_hbm.at[spans[1]], k_ref, sems.at[0]),
        pltpu.make_async_copy(v_hbm.at[spans[1]], v_ref, sems.at[1]),
        pltpu.make_async_copy(q_hbm.at[spans[0]], q_ref, sems.at[2]),
        pltpu.make_async_copy(sink_hbm, sink_ref, sems.at[3]),
        pltpu.make_async_copy(ow_hbm, ow_ref, sems.at[4]),
    ]
    for copy in copies:
        copy.start()
    for copy in copies[:4]:
        copy.wait()

    low = lax.broadcasted_iota(jnp.int32, (keys, LANES), 1) < HEAD_DIM
    k, v = k_ref[...], v_ref[...]
    if mix:
        k = jnp.concatenate([k_before[rows:], k], axis=0)
        v = jnp.concatenate([v_before[rows:], v], axis=0)
    k = k.astype(jnp.float32) * (1.0 / math.sqrt(HEAD_DIM))
    v = v.astype(jnp.float32)
    k_turned, v_turned = pltpu.roll(k, HEAD_DIM, 1), pltpu.roll(v, HEAD_DIM, 1)
    one_low = jnp.where(low, 1.0, 0.0)

    row = lax.broadcasted_iota(jnp.int32, (rows, keys), 0)
    column = lax.broadcasted_iota(jnp.int32, (rows, keys), 1)
    allowed = (column <= row + rows) & (column > row)
    if mix:
        allowed = allowed & (column >= jnp.where(first_ref[0] == 1, rows, 0))
    low_out = lax.broadcasted_iota(jnp.int32, (rows, LANES), 1) < HEAD_DIM

    for group in range(groups):
        here, there = (k, v), (k_turned, v_turned)
        lows, highs = (here, there) if group == 0 else (there, here)
        kk = jnp.concatenate(
            [jnp.where(low, lows[0], 0.0), jnp.where(low, 0.0, highs[0])], axis=0
        ).astype(jnp.bfloat16)
        vv = jnp.concatenate(
            [
                jnp.concatenate([jnp.where(low, lows[1], 0.0), one_low], axis=1),
                jnp.concatenate([jnp.where(low, 0.0, highs[1]), 1.0 - one_low], axis=1),
            ],
            axis=0,
        ).astype(jnp.bfloat16)
        for pair in range(group * pairs // groups, (group + 1) * pairs // groups):
            lanes = slice(pair * LANES, (pair + 1) * LANES)
            scores = lax.dot_general(
                q_ref[:, lanes], kk, (((1,), (1,)), ((), ())), preferred_element_type=jnp.float32
            )
            weights, sinks = [], []
            for side in range(2):
                part = jnp.where(allowed, scores[:, side * keys : (side + 1) * keys], -jnp.inf)
                sink = sink_ref[:, 2 * pair + side : 2 * pair + side + 1]
                highest = jnp.maximum(jnp.max(part, axis=1, keepdims=True), sink)
                weights.append(jnp.exp(part - highest).astype(jnp.bfloat16))
                sinks.append(jnp.exp(sink - highest))
            both = mm(jnp.concatenate(weights, axis=1), vv)
            below = both[:, LANES:] + jnp.where(low_out, sinks[0], sinks[1])
            done_ref[:, lanes] = (both[:, :LANES] / below).astype(jnp.bfloat16)

    copies[4].wait()
    model = ow_ref.shape[1]
    width = 512 if model % 512 == 0 else model
    if mix:
        own_first = rank_ref[0] == 0
    for start in range(0, model, width):
        lanes = slice(start, start + width)
        mine = mm(done_ref[...], ow_ref[:, lanes])
        if mix:
            other = other_ref[:, lanes]
            own_ref[:, lanes] = jnp.where(own_first, mine, other)
            send_ref[:, lanes] = jnp.where(own_first, other, mine).astype(jnp.bfloat16)
        else:
            out_ref[:, lanes] = mine


def attend(half, first, sinks, queries, keys, values, out_weight, before=(), rank=None, other=None):
    mix = bool(before)
    rows, width, model = WINDOW, queries.shape[1], out_weight.shape[1]
    local = rows if mix else 2 * rows
    smem = pl.BlockSpec(memory_space=pltpu.SMEM)
    vmem = pl.BlockSpec(memory_space=pltpu.VMEM)
    hbm = pl.BlockSpec(memory_space=pltpu.HBM)
    wide = jax.ShapeDtypeStruct((rows, model), jnp.float32)
    narrow = jax.ShapeDtypeStruct((rows, model), jnp.bfloat16)
    return pl.pallas_call(
        functools.partial(attend_kernel, half, mix),
        in_specs=[smem] + [hbm] * 5 + ([vmem, vmem, smem, vmem] if mix else []),
        out_specs=(vmem, vmem) if mix else vmem,
        out_shape=(narrow, wide) if mix else wide,
        scratch_shapes=[
            pltpu.VMEM((1, sinks.shape[0]), jnp.float32),
            pltpu.VMEM((rows, width), jnp.bfloat16),
            pltpu.VMEM((local, LANES), jnp.bfloat16),
            pltpu.VMEM((local, LANES), jnp.bfloat16),
            pltpu.VMEM((width, model), jnp.bfloat16),
            pltpu.VMEM((rows, width), jnp.bfloat16),
            pltpu.SemaphoreType.DMA((5,)),
        ],
        compiler_params=pltpu.CompilerParams(vmem_limit_bytes=8 * MIB),
        cost_estimate=pl.CostEstimate(
            flops=2 * rows * width * (model + 1024), bytes_accessed=6 * MIB, transcendentals=0
        ),
        name="attend",
    )(
        first,
        *pinned((sinks.reshape(1, -1), queries, keys, values, out_weight), pltpu.HBM),
        *((*before, rank, other) if mix else ()),
    )


def norm_kernel(
    expert_count, stream_ref, own_ref, came_ref, gain_ref, ids_ref, route_ref, *rest
):
    residual_ref, *message_refs = rest
    rows, model = stream_ref.shape
    size = message_refs[0].shape[0]
    residual = (
        stream_ref[...].astype(jnp.float32) + own_ref[...] + came_ref[...].astype(jnp.float32)
    ).astype(jnp.bfloat16)
    residual_ref[...] = residual
    wide = residual.astype(jnp.float32)
    mean = jnp.mean(wide * wide, axis=-1, keepdims=True)
    normed = (wide * lax.rsqrt(mean + 1e-05) * gain_ref[...]).astype(jnp.bfloat16)
    for index, ref in enumerate(message_refs):
        ref[:, :model] = normed[index * size : (index + 1) * size]
    if expert_count:
        expert = lax.broadcasted_iota(jnp.int32, (LANES, rows), 0)
        dense = jnp.zeros((LANES, rows), jnp.float32)
        for k in range(TOP):
            named = ids_ref[k : k + 1, :]
            hit = (expert == named) | (expert == named + expert_count)
            dense += jnp.where(hit, route_ref[k : k + 1, :], 0.0)
        lead = dense.astype(jnp.bfloat16).astype(jnp.float32)
        both = jnp.where(expert < expert_count, lead, dense - lead)
        tail = both.T.astype(jnp.bfloat16)
        for index, ref in enumerate(message_refs):
            ref[:, model:] = tail[index * size : (index + 1) * size]


def norm(stream, own, came, gain, expert_ids, route_weights, expert_count, pieces):
    rows, model = stream.shape
    vmem = pl.BlockSpec(memory_space=pltpu.VMEM)
    width = model + (LANES if expert_count else 0)
    return pl.pallas_call(
        functools.partial(norm_kernel, expert_count),
        in_specs=[vmem] * 6,
        out_shape=[jax.ShapeDtypeStruct((rows, model), jnp.bfloat16)]
        + [jax.ShapeDtypeStruct((rows // pieces, width), jnp.bfloat16)] * pieces,
        compiler_params=pltpu.CompilerParams(vmem_limit_bytes=8 * MIB),
        cost_estimate=pl.CostEstimate(
            flops=8 * rows * model, bytes_accessed=14 * rows * model, transcendentals=rows
        ),
        name="norm",
    )(stream, own, came, gain.reshape(1, model), expert_ids.T, route_weights.T)


def expert_kernel(tile, expert_count, count, load, me_ref, *refs):
    x_refs, halves = refs[:count], refs[count : count + 6]
    out_refs, rest = refs[count + 6 : 2 * count + 6], refs[2 * count + 6 :]
    copies = []
    if load:
        kept, rest = rest[:6], rest[6:]
        copies = [
            pltpu.make_async_copy(here, there, rest[2].at[index])
            for index, (here, there) in enumerate(zip(halves, kept))
        ]
        for index in (0, 1, 3, 4, 2, 5):
            copies[index].start()
        halves = kept
    x, hidden = rest[:2]
    model, half = halves[0].shape
    starts = [0]
    for ref in x_refs:
        starts.append(starts[-1] + ref.shape[0])
    for start, ref in zip(starts, x_refs):
        x[start : start + ref.shape[0]] = ref[:, :model]

    def arrived(*which):
        for index in which:
            if copies:
                copies[index].wait()

    def work(side, at):
        gate_ref, up_ref = halves[3 * side : 3 * side + 2]
        gate_pre = mm(x[...], gate_ref[:, at : at + tile])
        up_pre = mm(x[...], up_ref[:, at : at + tile])
        activated = gate_pre * jax.nn.sigmoid(1.702 * gate_pre) * (up_pre + 1.0)
        hidden[:, side * half + at : side * half + at + tile] = activated.astype(jnp.bfloat16)

    for side in range(2):
        arrived(3 * side, 3 * side + 1)
        for at in range(0, half, tile):
            work(side, at)
    arrived(2, 5)

    me = me_ref[0]
    scales = []
    for ref in x_refs:
        sent = ref[:, model:].astype(jnp.float32)
        lane = lax.broadcasted_iota(jnp.int32, sent.shape, 1)
        mine = (lane == me) | (lane == me + expert_count)
        scales.append(jnp.sum(jnp.where(mine, sent, 0.0), axis=1, keepdims=True))
    for at in range(0, model, tile):
        lanes = slice(at, at + tile)
        total = mm(hidden[:, :half], halves[2][:, lanes]) + mm(hidden[:, half:], halves[5][:, lanes])
        for start, ref, scale in zip(starts, out_refs, scales):
            ref[:, lanes] = (total[start : start + ref.shape[0]] * scale).astype(jnp.bfloat16)


def experts(blocks, me, halves, expert_count, load=False):
    model, half = halves[0].shape
    rows = sum(block.shape[0] for block in blocks)
    vmem = pl.BlockSpec(memory_space=pltpu.VMEM)
    hbm = pl.BlockSpec(memory_space=pltpu.HBM)
    kept = [jax.ShapeDtypeStruct(w.shape, w.dtype) for w in halves] if load else []
    scratch = [
        pltpu.VMEM((rows, model), jnp.bfloat16),
        pltpu.VMEM((rows, 2 * half), jnp.bfloat16),
    ]
    return pl.pallas_call(
        functools.partial(expert_kernel, min(256, half), expert_count, len(blocks), load),
        in_specs=[pl.BlockSpec(memory_space=pltpu.SMEM)]
        + [vmem] * len(blocks)
        + [hbm if load else vmem] * 6,
        out_specs=[vmem] * (len(blocks) + len(kept)),
        out_shape=[jax.ShapeDtypeStruct((b.shape[0], model), jnp.bfloat16) for b in blocks] + kept,
        scratch_shapes=scratch + ([pltpu.SemaphoreType.DMA((6,))] if load else []),
        compiler_params=pltpu.CompilerParams(vmem_limit_bytes=EXPERT_VMEM),
        cost_estimate=pl.CostEstimate(
            flops=12 * rows * model * half, bytes_accessed=6 * rows * model, transcendentals=0
        ),
        name="experts",
    )(me, *blocks, *pinned(halves, pltpu.HBM if load else pltpu.VMEM))


def ring_experts(residual, pieces, gate_weight, up_weight, down_weight, others):
    chips = lax.axis_size("seq")
    ring = SNAKES.get(chips, tuple(range(chips)))
    far = chips // 2
    ahead = [(ring[i], ring[(i + 1) % chips]) for i in range(chips)]
    hops = (ahead, [(to, of) for of, to in ahead])
    sides = (0, 1)
    me = lax.axis_index("seq").astype(jnp.int32).reshape(1)
    given = {}

    def keep(keys, outs):
        for (side, distance, piece), out in zip(keys, outs):
            given[(distance if side == 0 else -distance) % chips, piece] = out

    halves = (gate_weight, up_weight, down_weight) + tuple(others)
    outs = experts(pieces, me, halves, chips, load=True)
    halves = outs[2:]
    keep([(0, 0, 0), (0, 0, 1)], outs)
    worked = {0: outs[0]}
    came = {(side, 0, piece): pieces[piece] for side in sides for piece in sides}

    def bring(distance, lead, *after):
        for side in sides:
            piece = side if lead else 1 - side
            block = tied(came[side, distance - 1, piece], *after)
            came[side, distance, piece] = lax.ppermute(block, "seq", hops[side])

    def apply(distance, *after):
        kinds = (True, False) if distance < far else (True,)
        keys = [(side, distance, side if lead else 1 - side) for lead in kinds for side in sides]
        blocks = [came[key] for key in keys]
        if after:
            blocks[0] = tied(blocks[0], *after)
        outs = experts(blocks, me, halves, chips)
        worked[distance] = outs[0]
        keep(keys, outs)

    for distance in range(1, far + 1):
        bring(distance, True, *([worked[distance - 2]] if distance > 1 else []))
        if distance < far:
            bring(
                distance,
                False,
                *([came[side, distance - 1, side] for side in sides] if distance > 1 else []),
            )
            apply(distance)
        else:
            apply(far, worked[far - 1])

    moving = {}

    def send(distance, lead, *after):
        for side in sides:
            piece = side if lead else 1 - side
            value = given[(-distance if side == 0 else distance) % chips, piece]
            if after:
                value = tied(value, *after)
            if (side, piece) in moving:
                value = moving[side, piece].astype(jnp.float32) + value.astype(jnp.float32)
                value = value.astype(jnp.bfloat16)
            moving[side, piece] = lax.ppermute(value, "seq", hops[side])

    for distance in range(far, 0, -1):
        if distance > 1:
            last = [came[side, far, side] for side in sides] if distance == far else []
            send(distance - 1, False, *last)
        send(distance, True)
    final = []
    for piece in sides:
        total = given[0, piece].astype(jnp.float32)
        for side in sides:
            total += moving[side, piece].astype(jnp.float32)
        final.append(total)
    return (residual.astype(jnp.float32) + jnp.concatenate(final, axis=0)).astype(jnp.bfloat16)


def dispatched_experts(
    residual, normed, expert_ids, route_weights, gate_weight, up_weight, down_weight
):
    tokens_here = normed.shape[0]
    resid_f = residual.astype(jnp.float32)
    expert_count = EXP_DEV * lax.axis_size("seq")
    capacity = max(2, 3 * tokens_here * TOP // (2 * expert_count))
    flat_ids = expert_ids.reshape(-1)
    onehot = (flat_ids[:, None] == jnp.arange(expert_count, dtype=jnp.int32)[None, :]).astype(
        jnp.int32
    )
    earlier_count = jnp.cumsum(onehot, axis=0) - onehot
    slot_index = jnp.sum(earlier_count * onehot, axis=1)
    cell_index = (flat_ids * capacity + slot_index).reshape(tokens_here, TOP)
    chooser = jnp.any(
        cell_index[None, :, :]
        == jnp.arange(expert_count * capacity, dtype=jnp.int32)[:, None, None],
        axis=2,
    ).astype(jnp.bfloat16)
    outgoing = mm(chooser, normed).astype(jnp.bfloat16)
    outgoing = outgoing.reshape(expert_count, capacity, normed.shape[1])
    paired = lax.all_gather(outgoing, "rep", axis=1, tiled=True)
    arrived = lax.all_to_all(paired, "seq", split_axis=0, concat_axis=1, tiled=True)[0]
    gate_pre = mm(arrived, gate_weight)
    up_pre = mm(arrived, up_weight)
    activated = (gate_pre * jax.nn.sigmoid(1.702 * gate_pre) * (up_pre + 1.0)).astype(jnp.bfloat16)
    returned = lax.all_to_all(
        mm(activated, down_weight).astype(jnp.bfloat16)[None],
        "seq",
        split_axis=1,
        concat_axis=0,
        tiled=True,
    )
    expert_out = lax.psum_scatter(returned, "rep", scatter_dimension=1, tiled=True)
    picked = expert_out.reshape(expert_count * capacity, -1)[cell_index.reshape(-1)]
    picked = picked.reshape(tokens_here, TOP, -1)
    expert_sum = jnp.sum(route_weights[:, :, None] * picked.astype(jnp.float32), axis=1)
    return (resid_f + expert_sum).astype(jnp.bfloat16)


def per_device(
    stream,
    queries,
    key_rows,
    value_rows,
    sink_logits,
    out_weight,
    norm_gain,
    expert_ids,
    route_weights,
    gate_weight,
    up_weight,
    down_weight,
):
    block_len = queries.shape[0]
    seq = lax.axis_index("seq")
    rank = lax.axis_index("rep").astype(jnp.int32).reshape(1)
    gate_weight, up_weight, down_weight = gate_weight[0], up_weight[0], down_weight[0]
    use_ring = EXP_DEV * lax.axis_size("seq") <= 2 * TOP

    k_before, v_before = shifted(key_rows, "seq", 1), shifted(value_rows, "seq", 1)
    others = []
    if use_ring:
        others = [swapped(w, "rep") for w in (gate_weight, up_weight, down_weight)]
    never = jnp.zeros((1,), jnp.int32)
    first = (seq == 0).astype(jnp.int32).reshape(1)
    shared = (sink_logits, queries, key_rows, value_rows, out_weight)
    later_half = attend(1, never, *shared)
    send, own = attend(0, first, *shared, (k_before, v_before), rank, later_half)
    came = swapped(send, "rep")
    expert_count = lax.axis_size("seq") * EXP_DEV if use_ring else 0
    residual, *pieces = norm(
        stream, own, came, norm_gain, expert_ids, route_weights, expert_count, 2
    )
    if use_ring:
        *pieces, _ = lax.optimization_barrier((*pieces, others))
        return ring_experts(residual, pieces, gate_weight, up_weight, down_weight, others)
    return dispatched_experts(
        residual,
        jnp.concatenate(pieces, axis=0),
        expert_ids,
        route_weights,
        gate_weight,
        up_weight,
        down_weight,
    )


def solution(mesh):
    return jax.shard_map(
        per_device,
        mesh=mesh,
        in_specs=(
            P(("groups", "seq", "rep"), None),
            P(("groups", "seq"), "rep"),
            P(("groups", "seq"), "rep"),
            P(("groups", "seq"), "rep"),
            P("rep"),
            P("rep", None),
            P(),
            P(("groups", "seq", "rep"), None),
            P(("groups", "seq", "rep"), None),
            P("seq", None, "rep"),
            P("seq", None, "rep"),
            P("seq", "rep", None),
        ),
        out_specs=P(("groups", "seq", "rep"), None),
        check_vma=False,
    )
```

```python
import functools
import math

import jax
import jax.numpy as jnp
from jax import lax
from jax.experimental import pallas as pl
from jax.experimental.pallas import tpu as pltpu
from jax.sharding import PartitionSpec as P

HEAD_DIM = 64
WINDOW = 128
TOP = 4
TAIL = 16
EXP_DEV = 1
LANES = 128
SNAKES = {8: (0, 2, 4, 6, 7, 5, 3, 1)}
MIB = 1 << 20
EXPERT_VMEM = 8 * MIB


def shifted(value, axis, by):
    peers = lax.axis_size(axis)
    return lax.ppermute(value, axis, [(i, (i + by) % peers) for i in range(peers)])


def pinned(values, space):
    return [pltpu.with_memory_space_constraint(value, space) for value in values]


def tied(value, *after):
    return lax.optimization_barrier((value,) + after)[0]


def swapped(value, axis, bit=1):
    peers = lax.axis_size(axis)
    return lax.ppermute(value, axis, [(i, i ^ bit) for i in range(peers)])


def mm(a, b):
    return jnp.dot(a, b, preferred_element_type=jnp.float32)


def attend_kernel(half, mix, first_ref, sink_hbm, q_hbm, k_hbm, v_hbm, ow_hbm, *rest):
    if mix:
        k_before, v_before, rank_ref, other_ref, send_ref, own_ref = rest[:6]
    else:
        out_ref = rest[0]
    sink_ref, q_ref, k_ref, v_ref, ow_ref, done_ref, sems = rest[-7:]
    rows, keys = q_ref.shape[0], 2 * q_ref.shape[0]
    pairs = q_ref.shape[1] // LANES
    groups = k_ref.shape[1] // HEAD_DIM
    spans = (pl.ds(half * rows, rows), pl.ds(0, k_ref.shape[0]))
    copies = [
        pltpu.make_async_copy(k_hbm.at[spans[1]], k_ref, sems.at[0]),
        pltpu.make_async_copy(v_hbm.at[spans[1]], v_ref, sems.at[1]),
        pltpu.make_async_copy(q_hbm.at[spans[0]], q_ref, sems.at[2]),
        pltpu.make_async_copy(sink_hbm, sink_ref, sems.at[3]),
        pltpu.make_async_copy(ow_hbm, ow_ref, sems.at[4]),
    ]
    for copy in copies:
        copy.start()
    for copy in copies[:4]:
        copy.wait()

    low = lax.broadcasted_iota(jnp.int32, (keys, LANES), 1) < HEAD_DIM
    k, v = k_ref[...], v_ref[...]
    if mix:
        k = jnp.concatenate([k_before[rows:], k], axis=0)
        v = jnp.concatenate([v_before[rows:], v], axis=0)
    k = k.astype(jnp.float32) * (1.0 / math.sqrt(HEAD_DIM))
    v = v.astype(jnp.float32)
    k_turned, v_turned = pltpu.roll(k, HEAD_DIM, 1), pltpu.roll(v, HEAD_DIM, 1)
    one_low = jnp.where(low, 1.0, 0.0)

    row = lax.broadcasted_iota(jnp.int32, (rows, keys), 0)
    column = lax.broadcasted_iota(jnp.int32, (rows, keys), 1)
    allowed = (column <= row + rows) & (column > row)
    if mix:
        allowed = allowed & (column >= jnp.where(first_ref[0] == 1, rows, 0))
    low_out = lax.broadcasted_iota(jnp.int32, (rows, LANES), 1) < HEAD_DIM

    for group in range(groups):
        here, there = (k, v), (k_turned, v_turned)
        lows, highs = (here, there) if group == 0 else (there, here)
        kk = jnp.concatenate(
            [jnp.where(low, lows[0], 0.0), jnp.where(low, 0.0, highs[0])], axis=0
        ).astype(jnp.bfloat16)
        vv = jnp.concatenate(
            [
                jnp.concatenate([jnp.where(low, lows[1], 0.0), one_low], axis=1),
                jnp.concatenate([jnp.where(low, 0.0, highs[1]), 1.0 - one_low], axis=1),
            ],
            axis=0,
        ).astype(jnp.bfloat16)
        for pair in range(group * pairs // groups, (group + 1) * pairs // groups):
            lanes = slice(pair * LANES, (pair + 1) * LANES)
            scores = lax.dot_general(
                q_ref[:, lanes], kk, (((1,), (1,)), ((), ())), preferred_element_type=jnp.float32
            )
            weights, sinks = [], []
            for side in range(2):
                part = jnp.where(allowed, scores[:, side * keys : (side + 1) * keys], -jnp.inf)
                sink = sink_ref[:, 2 * pair + side : 2 * pair + side + 1]
                highest = jnp.maximum(jnp.max(part, axis=1, keepdims=True), sink)
                weights.append(jnp.exp(part - highest).astype(jnp.bfloat16))
                sinks.append(jnp.exp(sink - highest))
            both = mm(jnp.concatenate(weights, axis=1), vv)
            below = both[:, LANES:] + jnp.where(low_out, sinks[0], sinks[1])
            done_ref[:, lanes] = (both[:, :LANES] / below).astype(jnp.bfloat16)

    copies[4].wait()
    model = ow_ref.shape[1]
    width = 512 if model % 512 == 0 else model
    if mix:
        own_first = rank_ref[0] == 0
    for start in range(0, model, width):
        lanes = slice(start, start + width)
        mine = mm(done_ref[...], ow_ref[:, lanes])
        if mix:
            other = other_ref[:, lanes]
            own_ref[:, lanes] = jnp.where(own_first, mine, other)
            send_ref[:, lanes] = jnp.where(own_first, other, mine).astype(jnp.bfloat16)
        else:
            out_ref[:, lanes] = mine


def attend(half, first, sinks, queries, keys, values, out_weight, before=(), rank=None, other=None):
    mix = bool(before)
    rows, width, model = WINDOW, queries.shape[1], out_weight.shape[1]
    local = rows if mix else 2 * rows
    smem = pl.BlockSpec(memory_space=pltpu.SMEM)
    vmem = pl.BlockSpec(memory_space=pltpu.VMEM)
    hbm = pl.BlockSpec(memory_space=pltpu.HBM)
    wide = jax.ShapeDtypeStruct((rows, model), jnp.float32)
    narrow = jax.ShapeDtypeStruct((rows, model), jnp.bfloat16)
    return pl.pallas_call(
        functools.partial(attend_kernel, half, mix),
        in_specs=[smem] + [hbm] * 5 + ([vmem, vmem, smem, vmem] if mix else []),
        out_specs=(vmem, vmem) if mix else vmem,
        out_shape=(narrow, wide) if mix else wide,
        scratch_shapes=[
            pltpu.VMEM((1, sinks.shape[0]), jnp.float32),
            pltpu.VMEM((rows, width), jnp.bfloat16),
            pltpu.VMEM((local, LANES), jnp.bfloat16),
            pltpu.VMEM((local, LANES), jnp.bfloat16),
            pltpu.VMEM((width, model), jnp.bfloat16),
            pltpu.VMEM((rows, width), jnp.bfloat16),
            pltpu.SemaphoreType.DMA((5,)),
        ],
        compiler_params=pltpu.CompilerParams(vmem_limit_bytes=8 * MIB),
        cost_estimate=pl.CostEstimate(
            flops=2 * rows * width * (model + 1024), bytes_accessed=6 * MIB, transcendentals=0
        ),
        name="attend",
    )(
        first,
        *pinned((sinks.reshape(1, -1), queries, keys, values, out_weight), pltpu.HBM),
        *((*before, rank, other) if mix else ()),
    )


def norm_kernel(
    expert_count, stream_ref, own_ref, came_ref, gain_ref, ids_ref, route_ref, *rest
):
    residual_ref, *message_refs = rest
    rows, model = stream_ref.shape
    residual = (
        stream_ref[...].astype(jnp.float32) + own_ref[...] + came_ref[...].astype(jnp.float32)
    ).astype(jnp.bfloat16)
    residual_ref[...] = residual
    wide = residual.astype(jnp.float32)
    mean = jnp.mean(wide * wide, axis=-1, keepdims=True)
    normed = (wide * lax.rsqrt(mean + 1e-05) * gain_ref[...]).astype(jnp.bfloat16)
    if not expert_count:
        message_refs[0][...] = normed
        return
    size = rows // len(message_refs)
    expert = lax.broadcasted_iota(jnp.int32, (TAIL, rows), 0)
    dense = jnp.zeros((TAIL, rows), jnp.float32)
    for k in range(TOP):
        dense += jnp.where(expert == ids_ref[k : k + 1, :], route_ref[k : k + 1, :], 0.0)
    lead = dense.astype(jnp.bfloat16).astype(jnp.float32)
    rest = dense - lead
    for index, ref in enumerate(message_refs):
        for block in range(model // LANES):
            ref[block * size : (block + 1) * size] = normed[
                index * size : (index + 1) * size, block * LANES : (block + 1) * LANES
            ]
        span = slice(index * size, (index + 1) * size)
        both = jnp.concatenate([lead[:, span], rest[:, span]], axis=1)
        ref[model // LANES * size :] = both.astype(jnp.bfloat16)


def norm(stream, own, came, gain, expert_ids, route_weights, expert_count):
    rows, model = stream.shape
    vmem = pl.BlockSpec(memory_space=pltpu.VMEM)
    pieces, shape = 1, (rows, model)
    if expert_count:
        pieces = 2
        shape = (rows // pieces * (model // LANES) + TAIL, LANES)
    return pl.pallas_call(
        functools.partial(norm_kernel, expert_count),
        in_specs=[vmem] * 6,
        out_shape=[jax.ShapeDtypeStruct((rows, model), jnp.bfloat16)]
        + [jax.ShapeDtypeStruct(shape, jnp.bfloat16)] * pieces,
        compiler_params=pltpu.CompilerParams(vmem_limit_bytes=8 * MIB),
        cost_estimate=pl.CostEstimate(
            flops=8 * rows * model, bytes_accessed=14 * rows * model, transcendentals=rows
        ),
        name="norm",
    )(stream, own, came, gain.reshape(1, model), expert_ids.T, route_weights.T)


def expert_kernel(tile, count, load, me_ref, *refs):
    x_refs, halves = refs[:count], refs[count : count + 6]
    out_refs, rest = refs[count + 6 : 2 * count + 6], refs[2 * count + 6 :]
    copies = []
    if load:
        kept, rest = rest[:6], rest[6:]
        copies = [
            pltpu.make_async_copy(here, there, rest[2].at[index])
            for index, (here, there) in enumerate(zip(halves, kept))
        ]
        for index in (0, 1, 3, 4, 2, 5):
            copies[index].start()
        halves = kept
    x, hidden = rest[:2]
    model, half = halves[0].shape
    rows = x.shape[0] // count
    body = rows * (model // LANES)
    for index, ref in enumerate(x_refs):
        for block in range(model // LANES):
            x[index * rows : (index + 1) * rows, block * LANES : (block + 1) * LANES] = ref[
                block * rows : (block + 1) * rows
            ]

    def arrived(*which):
        for index in which:
            if copies:
                copies[index].wait()

    def work(side, at):
        gate_ref, up_ref = halves[3 * side : 3 * side + 2]
        gate_pre = mm(x[...], gate_ref[:, at : at + tile])
        up_pre = mm(x[...], up_ref[:, at : at + tile])
        activated = gate_pre * jax.nn.sigmoid(1.702 * gate_pre) * (up_pre + 1.0)
        hidden[:, side * half + at : side * half + at + tile] = activated.astype(jnp.bfloat16)

    for side in range(2):
        arrived(3 * side, 3 * side + 1)
        for at in range(0, half, tile):
            work(side, at)
    arrived(2, 5)

    me = me_ref[0]
    scales = []
    for ref in x_refs:
        sent = ref[body:].astype(jnp.float32)
        expert = lax.broadcasted_iota(jnp.int32, sent.shape, 0)
        mine = jnp.sum(jnp.where(expert == me, sent, 0.0), axis=0, keepdims=True)
        mine = jnp.broadcast_to(mine, (8, LANES))
        scales.append((mine + pltpu.roll(mine, LANES - rows, 1)).T[:rows, :1])
    for at in range(0, model, tile):
        lanes = slice(at, at + tile)
        total = mm(hidden[:, :half], halves[2][:, lanes]) + mm(hidden[:, half:], halves[5][:, lanes])
        for index, (ref, scale) in enumerate(zip(out_refs, scales)):
            ref[:, lanes] = (total[index * rows : (index + 1) * rows] * scale).astype(jnp.bfloat16)


def experts(blocks, me, halves, load=False):
    model, half = halves[0].shape
    size = (blocks[0].shape[0] - TAIL) // (model // LANES)
    rows = size * len(blocks)
    vmem = pl.BlockSpec(memory_space=pltpu.VMEM)
    hbm = pl.BlockSpec(memory_space=pltpu.HBM)
    kept = [jax.ShapeDtypeStruct(w.shape, w.dtype) for w in halves] if load else []
    scratch = [
        pltpu.VMEM((rows, model), jnp.bfloat16),
        pltpu.VMEM((rows, 2 * half), jnp.bfloat16),
    ]
    return pl.pallas_call(
        functools.partial(expert_kernel, min(256, half), len(blocks), load),
        in_specs=[pl.BlockSpec(memory_space=pltpu.SMEM)]
        + [vmem] * len(blocks)
        + [hbm if load else vmem] * 6,
        out_specs=[vmem] * (len(blocks) + len(kept)),
        out_shape=[jax.ShapeDtypeStruct((size, model), jnp.bfloat16)] * len(blocks) + kept,
        scratch_shapes=scratch + ([pltpu.SemaphoreType.DMA((6,))] if load else []),
        compiler_params=pltpu.CompilerParams(vmem_limit_bytes=EXPERT_VMEM),
        cost_estimate=pl.CostEstimate(
            flops=12 * rows * model * half, bytes_accessed=6 * rows * model, transcendentals=0
        ),
        name="experts",
    )(me, *blocks, *pinned(halves, pltpu.HBM if load else pltpu.VMEM))


def ring_experts(residual, pieces, gate_weight, up_weight, down_weight, others):
    chips = lax.axis_size("seq")
    ring = SNAKES.get(chips, tuple(range(chips)))
    far = chips // 2
    ahead = [(ring[i], ring[(i + 1) % chips]) for i in range(chips)]
    hops = (ahead, [(to, of) for of, to in ahead])
    sides = (0, 1)
    me = lax.axis_index("seq").astype(jnp.int32).reshape(1)
    given = {}

    def keep(keys, outs):
        for (side, distance, piece), out in zip(keys, outs):
            given[(distance if side == 0 else -distance) % chips, piece] = out

    halves = (gate_weight, up_weight, down_weight) + tuple(others)
    outs = experts(pieces, me, halves, load=True)
    halves = outs[2:]
    keep([(0, 0, 0), (0, 0, 1)], outs)
    worked = {0: outs[0]}
    came = {(side, 0, piece): pieces[piece] for side in sides for piece in sides}

    def bring(distance, lead, *after):
        for side in sides:
            piece = side if lead else 1 - side
            block = tied(came[side, distance - 1, piece], *after)
            with jax.named_scope(f"out_{'lead' if lead else 'trail'}{distance}"):
                came[side, distance, piece] = lax.ppermute(block, "seq", hops[side])

    def apply(distance, kinds, *after):
        keys = [(side, distance, side if lead else 1 - side) for lead in kinds for side in sides]
        blocks = [came[key] for key in keys]
        if after:
            blocks[0] = tied(blocks[0], *after)
        with jax.named_scope(f"hop{distance}"):
            outs = experts(blocks, me, halves)
        worked[distance] = outs[0]
        keep(keys, outs)

    for distance in range(1, far + 1):
        bring(distance, True, *([worked[distance - 2]] if distance > 1 else []))
        if distance < far:
            bring(
                distance,
                False,
                *([came[side, distance - 1, side] for side in sides] if distance > 1 else []),
            )
        if distance < far - 1:
            apply(distance, (True, False))
        elif distance < far:
            apply(distance, (True,), worked[distance - 1])
    apply(far, (True,), worked[far - 1])
    apply(far - 1, (False,), worked[far])

    moving = {}

    def send(distance, lead, *after):
        for side in sides:
            piece = side if lead else 1 - side
            value = given[(-distance if side == 0 else distance) % chips, piece]
            if after:
                value = tied(value, *after)
            if (side, piece) in moving:
                value = moving[side, piece].astype(jnp.float32) + value.astype(jnp.float32)
                value = value.astype(jnp.bfloat16)
            with jax.named_scope(f"back_{'lead' if lead else 'trail'}{distance}"):
                moving[side, piece] = lax.ppermute(value, "seq", hops[side])

    for distance in range(far, 0, -1):
        if distance == far:
            send(far - 1, False, *[came[side, far, side] for side in sides])
        elif distance > 1:
            send(distance - 1, False, worked[far] if distance == far - 1 else moving[0, 0])
        send(distance, True)
    final = []
    for piece in sides:
        total = given[0, piece].astype(jnp.float32)
        for side in sides:
            total += moving[side, piece].astype(jnp.float32)
        final.append(total)
    return (residual.astype(jnp.float32) + jnp.concatenate(final, axis=0)).astype(jnp.bfloat16)


def dispatched_experts(
    residual, normed, expert_ids, route_weights, gate_weight, up_weight, down_weight
):
    tokens_here = normed.shape[0]
    resid_f = residual.astype(jnp.float32)
    expert_count = EXP_DEV * lax.axis_size("seq")
    capacity = max(2, 3 * tokens_here * TOP // (2 * expert_count))
    flat_ids = expert_ids.reshape(-1)
    onehot = (flat_ids[:, None] == jnp.arange(expert_count, dtype=jnp.int32)[None, :]).astype(
        jnp.int32
    )
    earlier_count = jnp.cumsum(onehot, axis=0) - onehot
    slot_index = jnp.sum(earlier_count * onehot, axis=1)
    cell_index = (flat_ids * capacity + slot_index).reshape(tokens_here, TOP)
    chooser = jnp.any(
        cell_index[None, :, :]
        == jnp.arange(expert_count * capacity, dtype=jnp.int32)[:, None, None],
        axis=2,
    ).astype(jnp.bfloat16)
    outgoing = mm(chooser, normed).astype(jnp.bfloat16)
    outgoing = outgoing.reshape(expert_count, capacity, normed.shape[1])
    paired = lax.all_gather(outgoing, "rep", axis=1, tiled=True)
    arrived = lax.all_to_all(paired, "seq", split_axis=0, concat_axis=1, tiled=True)[0]
    gate_pre = mm(arrived, gate_weight)
    up_pre = mm(arrived, up_weight)
    activated = (gate_pre * jax.nn.sigmoid(1.702 * gate_pre) * (up_pre + 1.0)).astype(jnp.bfloat16)
    returned = lax.all_to_all(
        mm(activated, down_weight).astype(jnp.bfloat16)[None],
        "seq",
        split_axis=1,
        concat_axis=0,
        tiled=True,
    )
    expert_out = lax.psum_scatter(returned, "rep", scatter_dimension=1, tiled=True)
    picked = expert_out.reshape(expert_count * capacity, -1)[cell_index.reshape(-1)]
    picked = picked.reshape(tokens_here, TOP, -1)
    expert_sum = jnp.sum(route_weights[:, :, None] * picked.astype(jnp.float32), axis=1)
    return (resid_f + expert_sum).astype(jnp.bfloat16)


def per_device(
    stream,
    queries,
    key_rows,
    value_rows,
    sink_logits,
    out_weight,
    norm_gain,
    expert_ids,
    route_weights,
    gate_weight,
    up_weight,
    down_weight,
):
    block_len = queries.shape[0]
    seq = lax.axis_index("seq")
    rank = lax.axis_index("rep").astype(jnp.int32).reshape(1)
    gate_weight, up_weight, down_weight = gate_weight[0], up_weight[0], down_weight[0]
    use_ring = EXP_DEV * lax.axis_size("seq") <= 2 * TOP

    k_before, v_before = shifted(key_rows, "seq", 1), shifted(value_rows, "seq", 1)
    others = []
    if use_ring:
        others = [swapped(w, "rep") for w in (gate_weight, up_weight, down_weight)]
    never = jnp.zeros((1,), jnp.int32)
    first = (seq == 0).astype(jnp.int32).reshape(1)
    shared = (sink_logits, queries, key_rows, value_rows, out_weight)
    later_half = attend(1, never, *shared)
    send, own = attend(0, first, *shared, (k_before, v_before), rank, later_half)
    came = swapped(send, "rep")
    expert_count = lax.axis_size("seq") * EXP_DEV if use_ring else 0
    residual, *pieces = norm(
        stream, own, came, norm_gain, expert_ids, route_weights, expert_count
    )
    if use_ring:
        *pieces, _ = lax.optimization_barrier((*pieces, others))
        return ring_experts(residual, pieces, gate_weight, up_weight, down_weight, others)
    return dispatched_experts(
        residual,
        pieces[0],
        expert_ids,
        route_weights,
        gate_weight,
        up_weight,
        down_weight,
    )


def solution(mesh):
    return jax.shard_map(
        per_device,
        mesh=mesh,
        in_specs=(
            P(("groups", "seq", "rep"), None),
            P(("groups", "seq"), "rep"),
            P(("groups", "seq"), "rep"),
            P(("groups", "seq"), "rep"),
            P("rep"),
            P("rep", None),
            P(),
            P(("groups", "seq", "rep"), None),
            P(("groups", "seq", "rep"), None),
            P("seq", None, "rep"),
            P("seq", None, "rep"),
            P("seq", "rep", None),
        ),
        out_specs=P(("groups", "seq", "rep"), None),
        check_vma=False,
    )
```

```python
import functools
import math

import jax
import jax.numpy as jnp
from jax import lax
from jax.experimental import pallas as pl
from jax.experimental.pallas import tpu as pltpu
from jax.sharding import PartitionSpec as P

HEAD_DIM = 64
WINDOW = 128
TOP = 4
TAIL = 16
EXP_DEV = 1
LANES = 128
SNAKES = {8: (0, 2, 4, 6, 7, 5, 3, 1)}
MIB = 1 << 20
EXPERT_VMEM = 8 * MIB


def shifted(value, axis, by):
    peers = lax.axis_size(axis)
    return lax.ppermute(value, axis, [(i, (i + by) % peers) for i in range(peers)])


def pinned(values, space):
    return [pltpu.with_memory_space_constraint(value, space) for value in values]


def tied(value, *after):
    return lax.optimization_barrier((value,) + after)[0]


def swapped(value, axis, bit=1):
    peers = lax.axis_size(axis)
    return lax.ppermute(value, axis, [(i, i ^ bit) for i in range(peers)])


def mm(a, b):
    return jnp.dot(a, b, preferred_element_type=jnp.float32)


def attend_kernel(half, mix, first_ref, sink_hbm, q_hbm, k_hbm, v_hbm, ow_hbm, *rest):
    if mix:
        k_before, v_before, rank_ref, other_ref, send_ref, own_ref = rest[:6]
    else:
        out_ref = rest[0]
    sink_ref, q_ref, k_ref, v_ref, ow_ref, done_ref, sems = rest[-7:]
    rows, keys = q_ref.shape[0], 2 * q_ref.shape[0]
    pairs = q_ref.shape[1] // LANES
    groups = k_ref.shape[1] // HEAD_DIM
    spans = (pl.ds(half * rows, rows), pl.ds(0, k_ref.shape[0]))
    copies = [
        pltpu.make_async_copy(k_hbm.at[spans[1]], k_ref, sems.at[0]),
        pltpu.make_async_copy(v_hbm.at[spans[1]], v_ref, sems.at[1]),
        pltpu.make_async_copy(q_hbm.at[spans[0]], q_ref, sems.at[2]),
        pltpu.make_async_copy(sink_hbm, sink_ref, sems.at[3]),
        pltpu.make_async_copy(ow_hbm, ow_ref, sems.at[4]),
    ]
    for copy in copies:
        copy.start()
    for copy in copies[:4]:
        copy.wait()

    low = lax.broadcasted_iota(jnp.int32, (keys, LANES), 1) < HEAD_DIM
    k, v = k_ref[...], v_ref[...]
    if mix:
        k = jnp.concatenate([k_before[rows:], k], axis=0)
        v = jnp.concatenate([v_before[rows:], v], axis=0)
    k = k.astype(jnp.float32) * (1.0 / math.sqrt(HEAD_DIM))
    v = v.astype(jnp.float32)
    k_turned, v_turned = pltpu.roll(k, HEAD_DIM, 1), pltpu.roll(v, HEAD_DIM, 1)
    one_low = jnp.where(low, 1.0, 0.0)

    row = lax.broadcasted_iota(jnp.int32, (rows, keys), 0)
    column = lax.broadcasted_iota(jnp.int32, (rows, keys), 1)
    allowed = (column <= row + rows) & (column > row)
    if mix:
        allowed = allowed & (column >= jnp.where(first_ref[0] == 1, rows, 0))
    low_out = lax.broadcasted_iota(jnp.int32, (rows, LANES), 1) < HEAD_DIM

    for group in range(groups):
        here, there = (k, v), (k_turned, v_turned)
        lows, highs = (here, there) if group == 0 else (there, here)
        kk = jnp.concatenate(
            [jnp.where(low, lows[0], 0.0), jnp.where(low, 0.0, highs[0])], axis=0
        ).astype(jnp.bfloat16)
        vv = jnp.concatenate(
            [
                jnp.concatenate([jnp.where(low, lows[1], 0.0), one_low], axis=1),
                jnp.concatenate([jnp.where(low, 0.0, highs[1]), 1.0 - one_low], axis=1),
            ],
            axis=0,
        ).astype(jnp.bfloat16)
        for pair in range(group * pairs // groups, (group + 1) * pairs // groups):
            lanes = slice(pair * LANES, (pair + 1) * LANES)
            scores = lax.dot_general(
                q_ref[:, lanes], kk, (((1,), (1,)), ((), ())), preferred_element_type=jnp.float32
            )
            weights, sinks = [], []
            for side in range(2):
                part = jnp.where(allowed, scores[:, side * keys : (side + 1) * keys], -jnp.inf)
                sink = sink_ref[:, 2 * pair + side : 2 * pair + side + 1]
                highest = jnp.maximum(jnp.max(part, axis=1, keepdims=True), sink)
                weights.append(jnp.exp(part - highest).astype(jnp.bfloat16))
                sinks.append(jnp.exp(sink - highest))
            both = mm(jnp.concatenate(weights, axis=1), vv)
            below = both[:, LANES:] + jnp.where(low_out, sinks[0], sinks[1])
            done_ref[:, lanes] = (both[:, :LANES] / below).astype(jnp.bfloat16)

    copies[4].wait()
    model = ow_ref.shape[1]
    width = 512 if model % 512 == 0 else model
    if mix:
        own_first = rank_ref[0] == 0
    for start in range(0, model, width):
        lanes = slice(start, start + width)
        mine = mm(done_ref[...], ow_ref[:, lanes])
        if mix:
            other = other_ref[:, lanes]
            own_ref[:, lanes] = jnp.where(own_first, mine, other)
            send_ref[:, lanes] = jnp.where(own_first, other, mine).astype(jnp.bfloat16)
        else:
            out_ref[:, lanes] = mine


def attend(half, first, sinks, queries, keys, values, out_weight, before=(), rank=None, other=None):
    mix = bool(before)
    rows, width, model = WINDOW, queries.shape[1], out_weight.shape[1]
    local = rows if mix else 2 * rows
    smem = pl.BlockSpec(memory_space=pltpu.SMEM)
    vmem = pl.BlockSpec(memory_space=pltpu.VMEM)
    hbm = pl.BlockSpec(memory_space=pltpu.HBM)
    wide = jax.ShapeDtypeStruct((rows, model), jnp.float32)
    narrow = jax.ShapeDtypeStruct((rows, model), jnp.bfloat16)
    return pl.pallas_call(
        functools.partial(attend_kernel, half, mix),
        in_specs=[smem] + [hbm] * 5 + ([vmem, vmem, smem, vmem] if mix else []),
        out_specs=(vmem, vmem) if mix else vmem,
        out_shape=(narrow, wide) if mix else wide,
        scratch_shapes=[
            pltpu.VMEM((1, sinks.shape[0]), jnp.float32),
            pltpu.VMEM((rows, width), jnp.bfloat16),
            pltpu.VMEM((local, LANES), jnp.bfloat16),
            pltpu.VMEM((local, LANES), jnp.bfloat16),
            pltpu.VMEM((width, model), jnp.bfloat16),
            pltpu.VMEM((rows, width), jnp.bfloat16),
            pltpu.SemaphoreType.DMA((5,)),
        ],
        compiler_params=pltpu.CompilerParams(vmem_limit_bytes=8 * MIB),
        cost_estimate=pl.CostEstimate(
            flops=2 * rows * width * (model + 1024), bytes_accessed=6 * MIB, transcendentals=0
        ),
        name="attend",
    )(
        first,
        *pinned((sinks.reshape(1, -1), queries, keys, values, out_weight), pltpu.HBM),
        *((*before, rank, other) if mix else ()),
    )


def norm_kernel(
    expert_count, stream_ref, own_ref, came_ref, gain_ref, ids_ref, route_ref, *rest
):
    residual_ref, *message_refs = rest
    rows, model = stream_ref.shape
    residual = (
        stream_ref[...].astype(jnp.float32) + own_ref[...] + came_ref[...].astype(jnp.float32)
    ).astype(jnp.bfloat16)
    residual_ref[...] = residual
    wide = residual.astype(jnp.float32)
    mean = jnp.mean(wide * wide, axis=-1, keepdims=True)
    normed = (wide * lax.rsqrt(mean + 1e-05) * gain_ref[...]).astype(jnp.bfloat16)
    if not expert_count:
        message_refs[0][...] = normed
        return
    size = rows // len(message_refs)
    expert = lax.broadcasted_iota(jnp.int32, (TAIL, rows), 0)
    dense = jnp.zeros((TAIL, rows), jnp.float32)
    for k in range(TOP):
        dense += jnp.where(expert == ids_ref[k : k + 1, :], route_ref[k : k + 1, :], 0.0)
    lead = dense.astype(jnp.bfloat16).astype(jnp.float32)
    rest = dense - lead
    for index, ref in enumerate(message_refs):
        for block in range(model // LANES):
            ref[block * size : (block + 1) * size] = normed[
                index * size : (index + 1) * size, block * LANES : (block + 1) * LANES
            ]
        span = slice(index * size, (index + 1) * size)
        both = jnp.concatenate([lead[:, span], rest[:, span]], axis=1)
        ref[model // LANES * size :] = both.astype(jnp.bfloat16)


def norm(stream, own, came, gain, expert_ids, route_weights, expert_count):
    rows, model = stream.shape
    vmem = pl.BlockSpec(memory_space=pltpu.VMEM)
    pieces, shape = 1, (rows, model)
    if expert_count:
        pieces = 2
        shape = (rows // pieces * (model // LANES) + TAIL, LANES)
    return pl.pallas_call(
        functools.partial(norm_kernel, expert_count),
        in_specs=[vmem] * 6,
        out_shape=[jax.ShapeDtypeStruct((rows, model), jnp.bfloat16)]
        + [jax.ShapeDtypeStruct(shape, jnp.bfloat16)] * pieces,
        compiler_params=pltpu.CompilerParams(vmem_limit_bytes=8 * MIB),
        cost_estimate=pl.CostEstimate(
            flops=8 * rows * model, bytes_accessed=14 * rows * model, transcendentals=rows
        ),
        name="norm",
    )(stream, own, came, gain.reshape(1, model), expert_ids.T, route_weights.T)


def expert_kernel(tile, count, load, me_ref, *refs):
    x_refs, halves = refs[:count], refs[count : count + 6]
    out_refs, rest = refs[count + 6 : 2 * count + 6], refs[2 * count + 6 :]
    copies = []
    if load:
        kept, rest = rest[:6], rest[6:]
        copies = [
            pltpu.make_async_copy(here, there, rest[2].at[index])
            for index, (here, there) in enumerate(zip(halves, kept))
        ]
        for index in (0, 1, 3, 4, 2, 5):
            copies[index].start()
        halves = kept
    x, hidden = rest[:2]
    model, half = halves[0].shape
    rows = x.shape[0] // count
    body = rows * (model // LANES)
    for index, ref in enumerate(x_refs):
        for block in range(model // LANES):
            x[index * rows : (index + 1) * rows, block * LANES : (block + 1) * LANES] = ref[
                block * rows : (block + 1) * rows
            ]

    def arrived(*which):
        for index in which:
            if copies:
                copies[index].wait()

    def work(side, at):
        gate_ref, up_ref = halves[3 * side : 3 * side + 2]
        gate_pre = mm(x[...], gate_ref[:, at : at + tile])
        up_pre = mm(x[...], up_ref[:, at : at + tile])
        activated = gate_pre * jax.nn.sigmoid(1.702 * gate_pre) * (up_pre + 1.0)
        hidden[:, side * half + at : side * half + at + tile] = activated.astype(jnp.bfloat16)

    for side in range(2):
        arrived(3 * side, 3 * side + 1)
        for at in range(0, half, tile):
            work(side, at)
    arrived(2, 5)

    me = me_ref[0]
    scales = []
    for ref in x_refs:
        sent = ref[body:].astype(jnp.float32)
        expert = lax.broadcasted_iota(jnp.int32, sent.shape, 0)
        mine = jnp.sum(jnp.where(expert == me, sent, 0.0), axis=0, keepdims=True)
        mine = jnp.broadcast_to(mine, (8, LANES))
        scales.append((mine + pltpu.roll(mine, LANES - rows, 1)).T[:rows, :1])
    for at in range(0, model, tile):
        lanes = slice(at, at + tile)
        total = mm(hidden[:, :half], halves[2][:, lanes]) + mm(hidden[:, half:], halves[5][:, lanes])
        for index, (ref, scale) in enumerate(zip(out_refs, scales)):
            ref[:, lanes] = (total[index * rows : (index + 1) * rows] * scale).astype(jnp.bfloat16)


def experts(blocks, me, halves, load=False):
    model, half = halves[0].shape
    size = (blocks[0].shape[0] - TAIL) // (model // LANES)
    rows = size * len(blocks)
    vmem = pl.BlockSpec(memory_space=pltpu.VMEM)
    hbm = pl.BlockSpec(memory_space=pltpu.HBM)
    kept = [jax.ShapeDtypeStruct(w.shape, w.dtype) for w in halves] if load else []
    scratch = [
        pltpu.VMEM((rows, model), jnp.bfloat16),
        pltpu.VMEM((rows, 2 * half), jnp.bfloat16),
    ]
    return pl.pallas_call(
        functools.partial(expert_kernel, min(256, half), len(blocks), load),
        in_specs=[pl.BlockSpec(memory_space=pltpu.SMEM)]
        + [vmem] * len(blocks)
        + [hbm if load else vmem] * 6,
        out_specs=[vmem] * (len(blocks) + len(kept)),
        out_shape=[jax.ShapeDtypeStruct((size, model), jnp.bfloat16)] * len(blocks) + kept,
        scratch_shapes=scratch + ([pltpu.SemaphoreType.DMA((6,))] if load else []),
        compiler_params=pltpu.CompilerParams(vmem_limit_bytes=EXPERT_VMEM),
        cost_estimate=pl.CostEstimate(
            flops=12 * rows * model * half, bytes_accessed=6 * rows * model, transcendentals=0
        ),
        name="experts",
    )(me, *blocks, *pinned(halves, pltpu.HBM if load else pltpu.VMEM))


def ring_experts(residual, pieces, gate_weight, up_weight, down_weight, others):
    chips = lax.axis_size("seq")
    ring = SNAKES.get(chips, tuple(range(chips)))
    far = chips // 2
    ahead = [(ring[i], ring[(i + 1) % chips]) for i in range(chips)]
    hops = (ahead, [(to, of) for of, to in ahead])
    sides = (0, 1)
    me = lax.axis_index("seq").astype(jnp.int32).reshape(1)
    given = {}

    def keep(keys, outs):
        for (side, distance, piece), out in zip(keys, outs):
            given[(distance if side == 0 else -distance) % chips, piece] = out

    halves = (gate_weight, up_weight, down_weight) + tuple(others)
    outs = experts(pieces, me, halves, load=True)
    halves = outs[2:]
    keep([(0, 0, 0), (0, 0, 1)], outs)
    came = {(side, 0, piece): pieces[piece] for side in sides for piece in sides}

    def bring(distance, lead, *after):
        for side in sides:
            piece = side if lead else 1 - side
            block = tied(came[side, distance - 1, piece], *after)
            with jax.named_scope(f"out_{'lead' if lead else 'trail'}{distance}"):
                came[side, distance, piece] = lax.ppermute(block, "seq", hops[side])

    def apply(distance, kinds, *after):
        keys = [(side, distance, side if lead else 1 - side) for lead in kinds for side in sides]
        blocks = [came[key] for key in keys]
        blocks[0] = tied(blocks[0], *after)
        with jax.named_scope(f"hop{distance}"):
            outs = experts(blocks, me, halves)
        keep(keys, outs)
        return outs[0]

    worked = earlier = outs[0]
    for distance in range(1, far + 1):
        bring(distance, True, *([earlier] if distance > 1 else []))
        earlier = worked
        if distance == far:
            bring(far - 1, False, *[came[side, far - 1, side] for side in sides])
            worked = apply(far - 1, (True,), worked)
            worked = apply(far, (True,), worked)
        elif distance < far - 1:
            bring(
                distance,
                False,
                *([came[side, distance - 1, side] for side in sides] if distance > 1 else []),
            )
            kinds = (True, False) if distance < far - 2 else (True,)
            trail = [came[side, distance, 1 - side] for side in sides] if distance > 1 else []
            worked = apply(distance, kinds, worked, *trail)
    worked = apply(far - 1, (False,), worked)
    worked = apply(far - 2, (False,), worked)

    moving = {}

    def send(distance, lead, *after):
        for side in sides:
            piece = side if lead else 1 - side
            value = given[(-distance if side == 0 else distance) % chips, piece]
            if after:
                value = tied(value, *after)
            if (side, piece) in moving:
                value = moving[side, piece].astype(jnp.float32) + value.astype(jnp.float32)
                value = value.astype(jnp.bfloat16)
            with jax.named_scope(f"back_{'lead' if lead else 'trail'}{distance}"):
                moving[side, piece] = lax.ppermute(value, "seq", hops[side])

    for distance in range(far, 0, -1):
        if distance == far:
            send(far, True)
            send(far - 1, False, worked, *[moving[side, side] for side in sides])
            continue
        send(distance, True)
        if distance > 1:
            send(distance - 1, False, moving[0, 0])
    final = []
    for piece in sides:
        total = given[0, piece].astype(jnp.float32)
        for side in sides:
            total += moving[side, piece].astype(jnp.float32)
        final.append(total)
    return (residual.astype(jnp.float32) + jnp.concatenate(final, axis=0)).astype(jnp.bfloat16)


def dispatched_experts(
    residual, normed, expert_ids, route_weights, gate_weight, up_weight, down_weight
):
    tokens_here = normed.shape[0]
    resid_f = residual.astype(jnp.float32)
    expert_count = EXP_DEV * lax.axis_size("seq")
    capacity = max(2, 3 * tokens_here * TOP // (2 * expert_count))
    flat_ids = expert_ids.reshape(-1)
    onehot = (flat_ids[:, None] == jnp.arange(expert_count, dtype=jnp.int32)[None, :]).astype(
        jnp.int32
    )
    earlier_count = jnp.cumsum(onehot, axis=0) - onehot
    slot_index = jnp.sum(earlier_count * onehot, axis=1)
    cell_index = (flat_ids * capacity + slot_index).reshape(tokens_here, TOP)
    chooser = jnp.any(
        cell_index[None, :, :]
        == jnp.arange(expert_count * capacity, dtype=jnp.int32)[:, None, None],
        axis=2,
    ).astype(jnp.bfloat16)
    outgoing = mm(chooser, normed).astype(jnp.bfloat16)
    outgoing = outgoing.reshape(expert_count, capacity, normed.shape[1])
    paired = lax.all_gather(outgoing, "rep", axis=1, tiled=True)
    arrived = lax.all_to_all(paired, "seq", split_axis=0, concat_axis=1, tiled=True)[0]
    gate_pre = mm(arrived, gate_weight)
    up_pre = mm(arrived, up_weight)
    activated = (gate_pre * jax.nn.sigmoid(1.702 * gate_pre) * (up_pre + 1.0)).astype(jnp.bfloat16)
    returned = lax.all_to_all(
        mm(activated, down_weight).astype(jnp.bfloat16)[None],
        "seq",
        split_axis=1,
        concat_axis=0,
        tiled=True,
    )
    expert_out = lax.psum_scatter(returned, "rep", scatter_dimension=1, tiled=True)
    picked = expert_out.reshape(expert_count * capacity, -1)[cell_index.reshape(-1)]
    picked = picked.reshape(tokens_here, TOP, -1)
    expert_sum = jnp.sum(route_weights[:, :, None] * picked.astype(jnp.float32), axis=1)
    return (resid_f + expert_sum).astype(jnp.bfloat16)


def per_device(
    stream,
    queries,
    key_rows,
    value_rows,
    sink_logits,
    out_weight,
    norm_gain,
    expert_ids,
    route_weights,
    gate_weight,
    up_weight,
    down_weight,
):
    block_len = queries.shape[0]
    seq = lax.axis_index("seq")
    rank = lax.axis_index("rep").astype(jnp.int32).reshape(1)
    gate_weight, up_weight, down_weight = gate_weight[0], up_weight[0], down_weight[0]
    use_ring = EXP_DEV * lax.axis_size("seq") <= 2 * TOP

    k_before, v_before = shifted(key_rows, "seq", 1), shifted(value_rows, "seq", 1)
    others = []
    if use_ring:
        others = [swapped(w, "rep") for w in (gate_weight, up_weight, down_weight)]
    never = jnp.zeros((1,), jnp.int32)
    first = (seq == 0).astype(jnp.int32).reshape(1)
    shared = (sink_logits, queries, key_rows, value_rows, out_weight)
    later_half = attend(1, never, *shared)
    send, own = attend(0, first, *shared, (k_before, v_before), rank, later_half)
    came = swapped(send, "rep")
    expert_count = lax.axis_size("seq") * EXP_DEV if use_ring else 0
    residual, *pieces = norm(
        stream, own, came, norm_gain, expert_ids, route_weights, expert_count
    )
    if use_ring:
        *pieces, _ = lax.optimization_barrier((*pieces, others))
        return ring_experts(residual, pieces, gate_weight, up_weight, down_weight, others)
    return dispatched_experts(
        residual,
        pieces[0],
        expert_ids,
        route_weights,
        gate_weight,
        up_weight,
        down_weight,
    )


def solution(mesh):
    return jax.shard_map(
        per_device,
        mesh=mesh,
        in_specs=(
            P(("groups", "seq", "rep"), None),
            P(("groups", "seq"), "rep"),
            P(("groups", "seq"), "rep"),
            P(("groups", "seq"), "rep"),
            P("rep"),
            P("rep", None),
            P(),
            P(("groups", "seq", "rep"), None),
            P(("groups", "seq", "rep"), None),
            P("seq", None, "rep"),
            P("seq", None, "rep"),
            P("seq", "rep", None),
        ),
        out_specs=P(("groups", "seq", "rep"), None),
        check_vma=False,
    )
```

```python
import functools
import math

import jax
import jax.numpy as jnp
from jax import lax
from jax.experimental import pallas as pl
from jax.experimental.pallas import tpu as pltpu
from jax.sharding import PartitionSpec as P

HEAD_DIM = 64
WINDOW = 128
TOP = 4
TAIL = 16
EXP_DEV = 1
LANES = 128
SNAKES = {8: (0, 2, 4, 6, 7, 5, 3, 1)}
MIB = 1 << 20
EXPERT_VMEM = 8 * MIB


def shifted(value, axis, by):
    peers = lax.axis_size(axis)
    return lax.ppermute(value, axis, [(i, (i + by) % peers) for i in range(peers)])


def pinned(values, space):
    return [pltpu.with_memory_space_constraint(value, space) for value in values]


def tied(value, *after):
    return lax.optimization_barrier((value,) + after)[0]


def swapped(value, axis, bit=1):
    peers = lax.axis_size(axis)
    return lax.ppermute(value, axis, [(i, i ^ bit) for i in range(peers)])


def mm(a, b):
    return jnp.dot(a, b, preferred_element_type=jnp.float32)


def attend_kernel(half, mix, first_ref, sink_hbm, q_hbm, k_hbm, v_hbm, ow_hbm, *rest):
    if mix:
        k_before, v_before, rank_ref, other_ref, send_ref, own_ref = rest[:6]
    else:
        out_ref = rest[0]
    sink_ref, q_ref, k_ref, v_ref, ow_ref, done_ref, sems = rest[-7:]
    rows, keys = q_ref.shape[0], 2 * q_ref.shape[0]
    pairs = q_ref.shape[1] // LANES
    groups = k_ref.shape[1] // HEAD_DIM
    spans = (pl.ds(half * rows, rows), pl.ds(0, k_ref.shape[0]))
    copies = [
        pltpu.make_async_copy(k_hbm.at[spans[1]], k_ref, sems.at[0]),
        pltpu.make_async_copy(v_hbm.at[spans[1]], v_ref, sems.at[1]),
        pltpu.make_async_copy(q_hbm.at[spans[0]], q_ref, sems.at[2]),
        pltpu.make_async_copy(sink_hbm, sink_ref, sems.at[3]),
        pltpu.make_async_copy(ow_hbm, ow_ref, sems.at[4]),
    ]
    for copy in copies:
        copy.start()
    for copy in copies[:4]:
        copy.wait()

    low = lax.broadcasted_iota(jnp.int32, (keys, LANES), 1) < HEAD_DIM
    k, v = k_ref[...], v_ref[...]
    if mix:
        k = jnp.concatenate([k_before[rows:], k], axis=0)
        v = jnp.concatenate([v_before[rows:], v], axis=0)
    k = k.astype(jnp.float32) * (1.0 / math.sqrt(HEAD_DIM))
    v = v.astype(jnp.float32)
    k_turned, v_turned = pltpu.roll(k, HEAD_DIM, 1), pltpu.roll(v, HEAD_DIM, 1)
    one_low = jnp.where(low, 1.0, 0.0)

    row = lax.broadcasted_iota(jnp.int32, (rows, keys), 0)
    column = lax.broadcasted_iota(jnp.int32, (rows, keys), 1)
    allowed = (column <= row + rows) & (column > row)
    if mix:
        allowed = allowed & (column >= jnp.where(first_ref[0] == 1, rows, 0))
    low_out = lax.broadcasted_iota(jnp.int32, (rows, LANES), 1) < HEAD_DIM

    for group in range(groups):
        here, there = (k, v), (k_turned, v_turned)
        lows, highs = (here, there) if group == 0 else (there, here)
        kk = jnp.concatenate(
            [jnp.where(low, lows[0], 0.0), jnp.where(low, 0.0, highs[0])], axis=0
        ).astype(jnp.bfloat16)
        vv = jnp.concatenate(
            [
                jnp.concatenate([jnp.where(low, lows[1], 0.0), one_low], axis=1),
                jnp.concatenate([jnp.where(low, 0.0, highs[1]), 1.0 - one_low], axis=1),
            ],
            axis=0,
        ).astype(jnp.bfloat16)
        for pair in range(group * pairs // groups, (group + 1) * pairs // groups):
            lanes = slice(pair * LANES, (pair + 1) * LANES)
            scores = lax.dot_general(
                q_ref[:, lanes], kk, (((1,), (1,)), ((), ())), preferred_element_type=jnp.float32
            )
            weights, sinks = [], []
            for side in range(2):
                part = jnp.where(allowed, scores[:, side * keys : (side + 1) * keys], -jnp.inf)
                sink = sink_ref[:, 2 * pair + side : 2 * pair + side + 1]
                highest = jnp.maximum(jnp.max(part, axis=1, keepdims=True), sink)
                weights.append(jnp.exp(part - highest).astype(jnp.bfloat16))
                sinks.append(jnp.exp(sink - highest))
            both = mm(jnp.concatenate(weights, axis=1), vv)
            below = both[:, LANES:] + jnp.where(low_out, sinks[0], sinks[1])
            done_ref[:, lanes] = (both[:, :LANES] / below).astype(jnp.bfloat16)

    copies[4].wait()
    model = ow_ref.shape[1]
    width = 512 if model % 512 == 0 else model
    if mix:
        own_first = rank_ref[0] == 0
    for start in range(0, model, width):
        lanes = slice(start, start + width)
        mine = mm(done_ref[...], ow_ref[:, lanes])
        if mix:
            other = other_ref[:, lanes]
            own_ref[:, lanes] = jnp.where(own_first, mine, other)
            send_ref[:, lanes] = jnp.where(own_first, other, mine).astype(jnp.bfloat16)
        else:
            out_ref[:, lanes] = mine


def attend(half, first, sinks, queries, keys, values, out_weight, before=(), rank=None, other=None):
    mix = bool(before)
    rows, width, model = WINDOW, queries.shape[1], out_weight.shape[1]
    local = rows if mix else 2 * rows
    smem = pl.BlockSpec(memory_space=pltpu.SMEM)
    vmem = pl.BlockSpec(memory_space=pltpu.VMEM)
    hbm = pl.BlockSpec(memory_space=pltpu.HBM)
    wide = jax.ShapeDtypeStruct((rows, model), jnp.float32)
    narrow = jax.ShapeDtypeStruct((rows, model), jnp.bfloat16)
    return pl.pallas_call(
        functools.partial(attend_kernel, half, mix),
        in_specs=[smem] + [hbm] * 5 + ([vmem, vmem, smem, vmem] if mix else []),
        out_specs=(vmem, vmem) if mix else vmem,
        out_shape=(narrow, wide) if mix else wide,
        scratch_shapes=[
            pltpu.VMEM((1, sinks.shape[0]), jnp.float32),
            pltpu.VMEM((rows, width), jnp.bfloat16),
            pltpu.VMEM((local, LANES), jnp.bfloat16),
            pltpu.VMEM((local, LANES), jnp.bfloat16),
            pltpu.VMEM((width, model), jnp.bfloat16),
            pltpu.VMEM((rows, width), jnp.bfloat16),
            pltpu.SemaphoreType.DMA((5,)),
        ],
        compiler_params=pltpu.CompilerParams(vmem_limit_bytes=8 * MIB),
        cost_estimate=pl.CostEstimate(
            flops=2 * rows * width * (model + 1024), bytes_accessed=6 * MIB, transcendentals=0
        ),
        name="attend",
    )(
        first,
        *pinned((sinks.reshape(1, -1), queries, keys, values, out_weight), pltpu.HBM),
        *((*before, rank, other) if mix else ()),
    )


def norm_kernel(
    expert_count, stream_ref, own_ref, came_ref, gain_ref, ids_ref, route_ref, *rest
):
    residual_ref, *message_refs = rest
    rows, model = stream_ref.shape
    residual = (
        stream_ref[...].astype(jnp.float32) + own_ref[...] + came_ref[...].astype(jnp.float32)
    ).astype(jnp.bfloat16)
    residual_ref[...] = residual
    wide = residual.astype(jnp.float32)
    mean = jnp.mean(wide * wide, axis=-1, keepdims=True)
    normed = (wide * lax.rsqrt(mean + 1e-05) * gain_ref[...]).astype(jnp.bfloat16)
    if not expert_count:
        message_refs[0][...] = normed
        return
    size = rows // len(message_refs)
    expert = lax.broadcasted_iota(jnp.int32, (TAIL, rows), 0)
    dense = jnp.zeros((TAIL, rows), jnp.float32)
    for k in range(TOP):
        dense += jnp.where(expert == ids_ref[k : k + 1, :], route_ref[k : k + 1, :], 0.0)
    lead = dense.astype(jnp.bfloat16).astype(jnp.float32)
    rest = dense - lead
    for index, ref in enumerate(message_refs):
        for block in range(model // LANES):
            ref[block * size : (block + 1) * size] = normed[
                index * size : (index + 1) * size, block * LANES : (block + 1) * LANES
            ]
        span = slice(index * size, (index + 1) * size)
        both = jnp.concatenate([lead[:, span], rest[:, span]], axis=1)
        ref[model // LANES * size :] = both.astype(jnp.bfloat16)


def norm(stream, own, came, gain, expert_ids, route_weights, expert_count):
    rows, model = stream.shape
    vmem = pl.BlockSpec(memory_space=pltpu.VMEM)
    pieces, shape = 1, (rows, model)
    if expert_count:
        pieces = 2
        shape = (rows // pieces * (model // LANES) + TAIL, LANES)
    return pl.pallas_call(
        functools.partial(norm_kernel, expert_count),
        in_specs=[vmem] * 6,
        out_shape=[jax.ShapeDtypeStruct((rows, model), jnp.bfloat16)]
        + [jax.ShapeDtypeStruct(shape, jnp.bfloat16)] * pieces,
        compiler_params=pltpu.CompilerParams(vmem_limit_bytes=8 * MIB),
        cost_estimate=pl.CostEstimate(
            flops=8 * rows * model, bytes_accessed=14 * rows * model, transcendentals=rows
        ),
        name="norm",
    )(stream, own, came, gain.reshape(1, model), expert_ids.T, route_weights.T)


def expert_kernel(tile, count, load, me_ref, *refs):
    x_refs, halves = refs[:count], refs[count : count + 6]
    out_refs, rest = refs[count + 6 : 2 * count + 6], refs[2 * count + 6 :]
    copies = []
    if load:
        kept, rest = rest[:6], rest[6:]
        copies = [
            pltpu.make_async_copy(here, there, rest[2].at[index])
            for index, (here, there) in enumerate(zip(halves, kept))
        ]
        for index in (0, 1, 3, 4, 2, 5):
            copies[index].start()
        halves = kept
    x, hidden = rest[:2]
    model, half = halves[0].shape
    rows = x.shape[0] // count
    body = rows * (model // LANES)
    for index, ref in enumerate(x_refs):
        for block in range(model // LANES):
            x[index * rows : (index + 1) * rows, block * LANES : (block + 1) * LANES] = ref[
                block * rows : (block + 1) * rows
            ]

    def arrived(*which):
        for index in which:
            if copies:
                copies[index].wait()

    def work(side, at):
        gate_ref, up_ref = halves[3 * side : 3 * side + 2]
        gate_pre = mm(x[...], gate_ref[:, at : at + tile])
        up_pre = mm(x[...], up_ref[:, at : at + tile])
        activated = gate_pre * jax.nn.sigmoid(1.702 * gate_pre) * (up_pre + 1.0)
        hidden[:, side * half + at : side * half + at + tile] = activated.astype(jnp.bfloat16)

    for side in range(2):
        arrived(3 * side, 3 * side + 1)
        for at in range(0, half, tile):
            work(side, at)
    arrived(2, 5)

    me = me_ref[0]
    scales = []
    for ref in x_refs:
        sent = ref[body:].astype(jnp.float32)
        expert = lax.broadcasted_iota(jnp.int32, sent.shape, 0)
        mine = jnp.sum(jnp.where(expert == me, sent, 0.0), axis=0, keepdims=True)
        mine = jnp.broadcast_to(mine, (8, LANES))
        scales.append((mine + pltpu.roll(mine, LANES - rows, 1)).T[:rows, :1])
    for at in range(0, model, tile):
        lanes = slice(at, at + tile)
        total = mm(hidden[:, :half], halves[2][:, lanes]) + mm(hidden[:, half:], halves[5][:, lanes])
        for index, (ref, scale) in enumerate(zip(out_refs, scales)):
            ref[:, lanes] = (total[index * rows : (index + 1) * rows] * scale).astype(jnp.bfloat16)


def experts(blocks, me, halves, load=False):
    model, half = halves[0].shape
    size = (blocks[0].shape[0] - TAIL) // (model // LANES)
    rows = size * len(blocks)
    vmem = pl.BlockSpec(memory_space=pltpu.VMEM)
    hbm = pl.BlockSpec(memory_space=pltpu.HBM)
    kept = [jax.ShapeDtypeStruct(w.shape, w.dtype) for w in halves] if load else []
    scratch = [
        pltpu.VMEM((rows, model), jnp.bfloat16),
        pltpu.VMEM((rows, 2 * half), jnp.bfloat16),
    ]
    return pl.pallas_call(
        functools.partial(expert_kernel, min(256, half), len(blocks), load),
        in_specs=[pl.BlockSpec(memory_space=pltpu.SMEM)]
        + [vmem] * len(blocks)
        + [hbm if load else vmem] * 6,
        out_specs=[vmem] * (len(blocks) + len(kept)),
        out_shape=[jax.ShapeDtypeStruct((size, model), jnp.bfloat16)] * len(blocks) + kept,
        scratch_shapes=scratch + ([pltpu.SemaphoreType.DMA((6,))] if load else []),
        compiler_params=pltpu.CompilerParams(vmem_limit_bytes=EXPERT_VMEM),
        cost_estimate=pl.CostEstimate(
            flops=12 * rows * model * half, bytes_accessed=6 * rows * model, transcendentals=0
        ),
        name="experts",
    )(me, *blocks, *pinned(halves, pltpu.HBM if load else pltpu.VMEM))


def ring_experts(residual, pieces, gate_weight, up_weight, down_weight, others):
    chips = lax.axis_size("seq")
    ring = SNAKES.get(chips, tuple(range(chips)))
    far = chips // 2
    ahead = [(ring[i], ring[(i + 1) % chips]) for i in range(chips)]
    hops = (ahead, [(to, of) for of, to in ahead])
    sides = (0, 1)
    me = lax.axis_index("seq").astype(jnp.int32).reshape(1)
    given = {}

    def keep(keys, outs):
        for (side, distance, piece), out in zip(keys, outs):
            given[(distance if side == 0 else -distance) % chips, piece] = out

    halves = (gate_weight, up_weight, down_weight) + tuple(others)
    outs = experts(pieces, me, halves, load=True)
    halves = outs[2:]
    keep([(0, 0, 0), (0, 0, 1)], outs)
    worked = {0: outs[0]}
    came = {(side, 0, piece): pieces[piece] for side in sides for piece in sides}

    def bring(distance, lead, *after):
        for side in sides:
            piece = side if lead else 1 - side
            block = tied(came[side, distance - 1, piece], *after)
            with jax.named_scope(f"out_{'lead' if lead else 'trail'}{distance}"):
                came[side, distance, piece] = lax.ppermute(block, "seq", hops[side])

    def apply(distance, kinds, *after):
        keys = [(side, distance, side if lead else 1 - side) for lead in kinds for side in sides]
        blocks = [came[key] for key in keys]
        if after:
            blocks[0] = tied(blocks[0], *after)
        with jax.named_scope(f"hop{distance}"):
            outs = experts(blocks, me, halves)
        worked[distance] = outs[0]
        keep(keys, outs)

    for distance in range(1, far + 1):
        bring(distance, True, *([worked[distance - 2]] if distance > 1 else []))
        if distance < far:
            bring(
                distance,
                False,
                *([came[side, distance - 1, side] for side in sides] if distance > 1 else []),
            )
        if distance < far - 1:
            apply(distance, (True, False))
        elif distance < far:
            apply(distance, (True,), worked[distance - 1])
    apply(far, (True,), worked[far - 1])
    apply(far - 1, (False,), worked[far])

    moving = {}

    def send(distance, lead, *after):
        met = [moving.get((side, side if lead else 1 - side)) for side in sides]
        if met[0] is not None:
            met = list(lax.optimization_barrier(tuple(met)))
        for side in sides:
            piece = side if lead else 1 - side
            value = given[(-distance if side == 0 else distance) % chips, piece]
            if after:
                value = tied(value, *after)
            if met[0] is not None:
                value = met[side].astype(jnp.float32) + value.astype(jnp.float32)
                value = value.astype(jnp.bfloat16)
            with jax.named_scope(f"back_{'lead' if lead else 'trail'}{distance}"):
                moving[side, piece] = lax.ppermute(value, "seq", hops[side])

    for distance in range(far, 0, -1):
        if distance == far:
            send(far - 1, False, *[came[side, far, side] for side in sides])
        elif distance > 1:
            send(distance - 1, False, worked[far] if distance == far - 1 else moving[0, 0])
        send(distance, True)
    final = []
    for piece in sides:
        total = given[0, piece].astype(jnp.float32)
        for side in sides:
            total += moving[side, piece].astype(jnp.float32)
        final.append(total)
    return (residual.astype(jnp.float32) + jnp.concatenate(final, axis=0)).astype(jnp.bfloat16)


def dispatched_experts(
    residual, normed, expert_ids, route_weights, gate_weight, up_weight, down_weight
):
    tokens_here = normed.shape[0]
    resid_f = residual.astype(jnp.float32)
    expert_count = EXP_DEV * lax.axis_size("seq")
    capacity = max(2, 3 * tokens_here * TOP // (2 * expert_count))
    flat_ids = expert_ids.reshape(-1)
    onehot = (flat_ids[:, None] == jnp.arange(expert_count, dtype=jnp.int32)[None, :]).astype(
        jnp.int32
    )
    earlier_count = jnp.cumsum(onehot, axis=0) - onehot
    slot_index = jnp.sum(earlier_count * onehot, axis=1)
    cell_index = (flat_ids * capacity + slot_index).reshape(tokens_here, TOP)
    chooser = jnp.any(
        cell_index[None, :, :]
        == jnp.arange(expert_count * capacity, dtype=jnp.int32)[:, None, None],
        axis=2,
    ).astype(jnp.bfloat16)
    outgoing = mm(chooser, normed).astype(jnp.bfloat16)
    outgoing = outgoing.reshape(expert_count, capacity, normed.shape[1])
    paired = lax.all_gather(outgoing, "rep", axis=1, tiled=True)
    arrived = lax.all_to_all(paired, "seq", split_axis=0, concat_axis=1, tiled=True)[0]
    gate_pre = mm(arrived, gate_weight)
    up_pre = mm(arrived, up_weight)
    activated = (gate_pre * jax.nn.sigmoid(1.702 * gate_pre) * (up_pre + 1.0)).astype(jnp.bfloat16)
    returned = lax.all_to_all(
        mm(activated, down_weight).astype(jnp.bfloat16)[None],
        "seq",
        split_axis=1,
        concat_axis=0,
        tiled=True,
    )
    expert_out = lax.psum_scatter(returned, "rep", scatter_dimension=1, tiled=True)
    picked = expert_out.reshape(expert_count * capacity, -1)[cell_index.reshape(-1)]
    picked = picked.reshape(tokens_here, TOP, -1)
    expert_sum = jnp.sum(route_weights[:, :, None] * picked.astype(jnp.float32), axis=1)
    return (resid_f + expert_sum).astype(jnp.bfloat16)


def per_device(
    stream,
    queries,
    key_rows,
    value_rows,
    sink_logits,
    out_weight,
    norm_gain,
    expert_ids,
    route_weights,
    gate_weight,
    up_weight,
    down_weight,
):
    block_len = queries.shape[0]
    seq = lax.axis_index("seq")
    rank = lax.axis_index("rep").astype(jnp.int32).reshape(1)
    gate_weight, up_weight, down_weight = gate_weight[0], up_weight[0], down_weight[0]
    use_ring = EXP_DEV * lax.axis_size("seq") <= 2 * TOP

    k_before, v_before = shifted(key_rows, "seq", 1), shifted(value_rows, "seq", 1)
    others = []
    if use_ring:
        others = [swapped(w, "rep") for w in (gate_weight, up_weight, down_weight)]
    never = jnp.zeros((1,), jnp.int32)
    first = (seq == 0).astype(jnp.int32).reshape(1)
    shared = (sink_logits, queries, key_rows, value_rows, out_weight)
    later_half = attend(1, never, *shared)
    send, own = attend(0, first, *shared, (k_before, v_before), rank, later_half)
    came = swapped(send, "rep")
    expert_count = lax.axis_size("seq") * EXP_DEV if use_ring else 0
    residual, *pieces = norm(
        stream, own, came, norm_gain, expert_ids, route_weights, expert_count
    )
    if use_ring:
        *pieces, _ = lax.optimization_barrier((*pieces, others))
        return ring_experts(residual, pieces, gate_weight, up_weight, down_weight, others)
    return dispatched_experts(
        residual,
        pieces[0],
        expert_ids,
        route_weights,
        gate_weight,
        up_weight,
        down_weight,
    )


def solution(mesh):
    return jax.shard_map(
        per_device,
        mesh=mesh,
        in_specs=(
            P(("groups", "seq", "rep"), None),
            P(("groups", "seq"), "rep"),
            P(("groups", "seq"), "rep"),
            P(("groups", "seq"), "rep"),
            P("rep"),
            P("rep", None),
            P(),
            P(("groups", "seq", "rep"), None),
            P(("groups", "seq", "rep"), None),
            P("seq", None, "rep"),
            P("seq", None, "rep"),
            P("seq", "rep", None),
        ),
        out_specs=P(("groups", "seq", "rep"), None),
        check_vma=False,
    )
```

```python
import functools
import math

import jax
import jax.numpy as jnp
from jax import lax
from jax.experimental import pallas as pl
from jax.experimental.pallas import tpu as pltpu
from jax.sharding import PartitionSpec as P

HEAD_DIM = 64
WINDOW = 128
TOP = 4
TAIL = 16
EXP_DEV = 1
LANES = 128
SNAKES = {8: (0, 2, 4, 6, 7, 5, 3, 1)}
MIB = 1 << 20
EXPERT_VMEM = 8 * MIB


def shifted(value, axis, by):
    peers = lax.axis_size(axis)
    return lax.ppermute(value, axis, [(i, (i + by) % peers) for i in range(peers)])


def pinned(values, space):
    return [pltpu.with_memory_space_constraint(value, space) for value in values]


def tied(value, *after):
    return lax.optimization_barrier((value,) + after)[0]


def swapped(value, axis, bit=1):
    peers = lax.axis_size(axis)
    return lax.ppermute(value, axis, [(i, i ^ bit) for i in range(peers)])


def mm(a, b):
    return jnp.dot(a, b, preferred_element_type=jnp.float32)


def attend_kernel(mix, *refs):
    done_ref = refs[-2]
    rows = done_ref.shape[0]
    keys = 2 * rows
    if mix:
        sink_ref, q_ref, k_ref, v_ref, ow_ref = refs[:5]
        first_ref, k_before, v_before, rank_ref, other_ref, send_ref, own_ref = refs[5:12]
        queries = slice(0, rows)
        k = jnp.concatenate([k_before[rows:], k_ref[:rows]], axis=0)
        v = jnp.concatenate([v_before[rows:], v_ref[:rows]], axis=0)
        copies = []
    else:
        sink_ref, q_ref, k_ref, v_ref, ow_ref, out_ref = refs[5:11]
        queries = slice(rows, 2 * rows)
        sems = refs[-1]
        early, late = pl.ds(0, rows), pl.ds(rows, rows)
        sources = [(refs[2], k_ref), (refs[3], v_ref), (refs[1].at[late], q_ref.at[late])]
        sources += [(refs[0], sink_ref), (refs[4], ow_ref), (refs[1].at[early], q_ref.at[early])]
        copies = [
            pltpu.make_async_copy(here, there, sems.at[index])
            for index, (here, there) in enumerate(sources)
        ]
        for copy in copies:
            copy.start()
        for copy in copies[:4]:
            copy.wait()
        k, v = k_ref[...], v_ref[...]
    pairs = q_ref.shape[1] // LANES
    groups = k_ref.shape[1] // HEAD_DIM

    low = lax.broadcasted_iota(jnp.int32, (keys, LANES), 1) < HEAD_DIM
    k = k.astype(jnp.float32) * (1.0 / math.sqrt(HEAD_DIM))
    v = v.astype(jnp.float32)
    k_turned, v_turned = pltpu.roll(k, HEAD_DIM, 1), pltpu.roll(v, HEAD_DIM, 1)
    key = lax.broadcasted_iota(jnp.int32, (keys, rows), 0)
    query = lax.broadcasted_iota(jnp.int32, (keys, rows), 1)
    allowed = (key <= query + rows) & (key > query)
    if mix:
        allowed = allowed & (key >= jnp.where(first_ref[0] == 1, rows, 0))
    ones = jnp.ones((8, keys), jnp.float32)
    zeros = jnp.zeros((8, keys), jnp.float32)

    for group in range(groups):
        here, there = (k, v), (k_turned, v_turned)
        lows, highs = (here, there) if group == 0 else (there, here)
        kk = jnp.concatenate(
            [jnp.where(low, lows[0], 0.0), jnp.where(low, 0.0, highs[0])], axis=0
        ).astype(jnp.bfloat16)
        v_low = jnp.where(low, lows[1], 0.0).T
        v_high = jnp.where(low, 0.0, highs[1]).T
        vv = jnp.concatenate(
            [
                jnp.concatenate([v_low, v_high], axis=1),
                jnp.concatenate([ones, zeros], axis=1),
                jnp.concatenate([zeros, ones], axis=1),
            ],
            axis=0,
        ).astype(jnp.bfloat16)
        for pair in range(group * pairs // groups, (group + 1) * pairs // groups):
            lanes = slice(pair * LANES, (pair + 1) * LANES)
            scores = lax.dot_general(
                kk, q_ref[queries, lanes], (((1,), (1,)), ((), ())), preferred_element_type=jnp.float32
            )
            weights, sinks = [], []
            for side in range(2):
                part = jnp.where(allowed, scores[side * keys : (side + 1) * keys], -jnp.inf)
                sink = sink_ref[:, 2 * pair + side : 2 * pair + side + 1]
                highest = jnp.maximum(jnp.max(part, axis=0, keepdims=True), sink)
                weights.append(jnp.exp(part - highest).astype(jnp.bfloat16))
                sinks.append(jnp.exp(sink - highest))
            both = mm(vv, jnp.concatenate(weights, axis=0))
            parts = [
                both[side * HEAD_DIM : (side + 1) * HEAD_DIM]
                / (both[LANES + 8 * side : LANES + 8 * side + 1] + sinks[side])
                for side in range(2)
            ]
            done_ref[:, lanes] = jnp.concatenate(parts, axis=0).T.astype(jnp.bfloat16)

    for copy in copies[4:]:
        copy.wait()
    model = ow_ref.shape[1]
    width = 512 if model % 512 == 0 else model
    if mix:
        own_first = rank_ref[0] == 0
    for start in range(0, model, width):
        lanes = slice(start, start + width)
        mine = mm(done_ref[...], ow_ref[:, lanes])
        if mix:
            other = other_ref[:, lanes]
            own_ref[:, lanes] = jnp.where(own_first, mine, other)
            send_ref[:, lanes] = jnp.where(own_first, other, mine).astype(jnp.bfloat16)
        else:
            out_ref[:, lanes] = mine


def attend(sinks, queries, keys, values, out_weight, mixed=()):
    mix = bool(mixed)
    rows, width, model = WINDOW, queries.shape[1], out_weight.shape[1]
    smem = pl.BlockSpec(memory_space=pltpu.SMEM)
    vmem = pl.BlockSpec(memory_space=pltpu.VMEM)
    hbm = pl.BlockSpec(memory_space=pltpu.HBM)
    operands = (sinks, queries, keys, values, out_weight)
    wide = jax.ShapeDtypeStruct((rows, model), jnp.float32)
    narrow = jax.ShapeDtypeStruct((rows, model), jnp.bfloat16)
    shapes = (narrow, wide)
    if not mix:
        shapes = tuple(jax.ShapeDtypeStruct(a.shape, a.dtype) for a in operands) + (wide,)
    return pl.pallas_call(
        functools.partial(attend_kernel, mix),
        in_specs=[vmem if mix else hbm] * 5 + ([smem, vmem, vmem, smem, vmem] if mix else []),
        out_specs=(vmem,) * len(shapes),
        out_shape=shapes,
        scratch_shapes=[
            pltpu.VMEM((rows, width), jnp.bfloat16),
            pltpu.SemaphoreType.DMA((6,)),
        ],
        compiler_params=pltpu.CompilerParams(vmem_limit_bytes=8 * MIB),
        cost_estimate=pl.CostEstimate(
            flops=2 * rows * width * (model + 1024), bytes_accessed=6 * MIB, transcendentals=0
        ),
        name="attend",
    )(*pinned(operands, pltpu.VMEM if mix else pltpu.HBM), *mixed)


def norm_kernel(
    expert_count, stream_ref, own_ref, came_ref, gain_ref, ids_ref, route_ref, *rest
):
    residual_ref, *message_refs = rest
    rows, model = stream_ref.shape
    residual = (
        stream_ref[...].astype(jnp.float32) + own_ref[...] + came_ref[...].astype(jnp.float32)
    ).astype(jnp.bfloat16)
    residual_ref[...] = residual
    wide = residual.astype(jnp.float32)
    mean = jnp.mean(wide * wide, axis=-1, keepdims=True)
    normed = (wide * lax.rsqrt(mean + 1e-05) * gain_ref[...]).astype(jnp.bfloat16)
    if not expert_count:
        message_refs[0][...] = normed
        return
    size = rows // len(message_refs)
    expert = lax.broadcasted_iota(jnp.int32, (TAIL, rows), 0)
    dense = jnp.zeros((TAIL, rows), jnp.float32)
    for k in range(TOP):
        dense += jnp.where(expert == ids_ref[k : k + 1, :], route_ref[k : k + 1, :], 0.0)
    lead = dense.astype(jnp.bfloat16).astype(jnp.float32)
    rest = dense - lead
    for index, ref in enumerate(message_refs):
        for block in range(model // LANES):
            ref[block * size : (block + 1) * size] = normed[
                index * size : (index + 1) * size, block * LANES : (block + 1) * LANES
            ]
        span = slice(index * size, (index + 1) * size)
        both = jnp.concatenate([lead[:, span], rest[:, span]], axis=1)
        ref[model // LANES * size :] = both.astype(jnp.bfloat16)


def norm(stream, own, came, gain, expert_ids, route_weights, expert_count):
    rows, model = stream.shape
    vmem = pl.BlockSpec(memory_space=pltpu.VMEM)
    pieces, shape = 1, (rows, model)
    if expert_count:
        pieces = 2
        shape = (rows // pieces * (model // LANES) + TAIL, LANES)
    return pl.pallas_call(
        functools.partial(norm_kernel, expert_count),
        in_specs=[vmem] * 6,
        out_shape=[jax.ShapeDtypeStruct((rows, model), jnp.bfloat16)]
        + [jax.ShapeDtypeStruct(shape, jnp.bfloat16)] * pieces,
        compiler_params=pltpu.CompilerParams(vmem_limit_bytes=8 * MIB),
        cost_estimate=pl.CostEstimate(
            flops=8 * rows * model, bytes_accessed=14 * rows * model, transcendentals=rows
        ),
        name="norm",
    )(stream, own, came, gain.reshape(1, model), expert_ids.T, route_weights.T)


def expert_kernel(tile, count, load, me_ref, *refs):
    x_refs, halves = refs[:count], refs[count : count + 6]
    out_refs, rest = refs[count + 6 : 2 * count + 6], refs[2 * count + 6 :]
    copies = []
    if load:
        kept, rest = rest[:3], rest[3:]
        copies = [
            pltpu.make_async_copy(here, there, rest[2].at[index])
            for index, (here, there) in enumerate(zip(halves[3:], kept))
        ]
        for copy in copies:
            copy.start()
        halves = halves[:3] + kept
    x, hidden = rest[:2]
    model, half = halves[0].shape
    rows = x.shape[0] // count
    body = rows * (model // LANES)
    for index, ref in enumerate(x_refs):
        for block in range(model // LANES):
            x[index * rows : (index + 1) * rows, block * LANES : (block + 1) * LANES] = ref[
                block * rows : (block + 1) * rows
            ]

    def arrived(*which):
        for index in which:
            if copies:
                copies[index].wait()

    def work(side, at):
        gate_ref, up_ref = halves[3 * side : 3 * side + 2]
        gate_pre = mm(x[...], gate_ref[:, at : at + tile])
        up_pre = mm(x[...], up_ref[:, at : at + tile])
        activated = gate_pre * jax.nn.sigmoid(1.702 * gate_pre) * (up_pre + 1.0)
        hidden[:, side * half + at : side * half + at + tile] = activated.astype(jnp.bfloat16)

    for side in range(2):
        if side == 1:
            arrived(0, 1)
        for at in range(0, half, tile):
            work(side, at)
    arrived(2)

    me = me_ref[0]
    scales = []
    for ref in x_refs:
        sent = ref[body:].astype(jnp.float32)
        expert = lax.broadcasted_iota(jnp.int32, sent.shape, 0)
        mine = jnp.sum(jnp.where(expert == me, sent, 0.0), axis=0, keepdims=True)
        mine = jnp.broadcast_to(mine, (8, LANES))
        scales.append((mine + pltpu.roll(mine, LANES - rows, 1)).T[:rows, :1])
    for at in range(0, model, tile):
        lanes = slice(at, at + tile)
        total = mm(hidden[:, :half], halves[2][:, lanes]) + mm(hidden[:, half:], halves[5][:, lanes])
        for index, (ref, scale) in enumerate(zip(out_refs, scales)):
            ref[:, lanes] = (total[index * rows : (index + 1) * rows] * scale).astype(jnp.bfloat16)


def experts(blocks, me, halves, load=False):
    model, half = halves[0].shape
    size = (blocks[0].shape[0] - TAIL) // (model // LANES)
    rows = size * len(blocks)
    vmem = pl.BlockSpec(memory_space=pltpu.VMEM)
    hbm = pl.BlockSpec(memory_space=pltpu.HBM)
    kept = [jax.ShapeDtypeStruct(w.shape, w.dtype) for w in halves[3:]] if load else []
    scratch = [
        pltpu.VMEM((rows, model), jnp.bfloat16),
        pltpu.VMEM((rows, 2 * half), jnp.bfloat16),
    ]
    return pl.pallas_call(
        functools.partial(expert_kernel, min(256, half), len(blocks), load),
        in_specs=[pl.BlockSpec(memory_space=pltpu.SMEM)]
        + [vmem] * len(blocks)
        + [vmem] * 3
        + [hbm if load else vmem] * 3,
        out_specs=[vmem] * (len(blocks) + len(kept)),
        out_shape=[jax.ShapeDtypeStruct((size, model), jnp.bfloat16)] * len(blocks) + kept,
        scratch_shapes=scratch + ([pltpu.SemaphoreType.DMA((3,))] if load else []),
        compiler_params=pltpu.CompilerParams(vmem_limit_bytes=EXPERT_VMEM),
        cost_estimate=pl.CostEstimate(
            flops=12 * rows * model * half, bytes_accessed=6 * rows * model, transcendentals=0
        ),
        name="experts",
    )(
        me,
        *blocks,
        *pinned(halves[:3], pltpu.VMEM),
        *pinned(halves[3:], pltpu.HBM if load else pltpu.VMEM),
    )


def ring_experts(residual, pieces, gate_weight, up_weight, down_weight, others):
    chips = lax.axis_size("seq")
    ring = SNAKES.get(chips, tuple(range(chips)))
    far = chips // 2
    ahead = [(ring[i], ring[(i + 1) % chips]) for i in range(chips)]
    hops = (ahead, [(to, of) for of, to in ahead])
    sides = (0, 1)
    me = lax.axis_index("seq").astype(jnp.int32).reshape(1)
    given = {}

    def keep(keys, outs):
        for (side, distance, piece), out in zip(keys, outs):
            given[(distance if side == 0 else -distance) % chips, piece] = out

    halves = (gate_weight, up_weight, down_weight) + tuple(others)
    outs = experts(pieces, me, halves, load=True)
    halves = halves[:3] + tuple(outs[2:])
    keep([(0, 0, 0), (0, 0, 1)], outs)
    worked = {0: outs[0]}
    came = {(side, 0, piece): pieces[piece] for side in sides for piece in sides}

    def bring(distance, lead, *after):
        keys = [(side, distance - 1, side if lead else 1 - side) for side in sides]
        met = lax.optimization_barrier((*(came[key] for key in keys), *after))
        for (side, _, piece), block in zip(keys, met):
            with jax.named_scope(f"out_{'lead' if lead else 'trail'}{distance}"):
                came[side, distance, piece] = lax.ppermute(block, "seq", hops[side])

    def apply(distance, kinds, *after):
        keys = [(side, distance, side if lead else 1 - side) for lead in kinds for side in sides]
        blocks = [came[key] for key in keys]
        if after:
            blocks[0] = tied(blocks[0], *after)
        with jax.named_scope(f"hop{distance}"):
            outs = experts(blocks, me, halves)
        worked[distance] = outs[0]
        keep(keys, outs)

    for distance in range(1, far + 1):
        bring(distance, True, *([worked[distance - 2]] if distance > 1 else []))
        if distance < far:
            bring(
                distance,
                False,
                *([came[side, distance - 1, side] for side in sides] if distance > 1 else []),
            )
        if distance < far - 1:
            apply(distance, (True, False))
        elif distance < far:
            apply(distance, (True,), worked[distance - 1])
    apply(far, (True,), worked[far - 1])
    apply(far - 1, (False,), worked[far])

    moving = {}

    def send(distance, lead, *after):
        met = [moving.get((side, side if lead else 1 - side)) for side in sides]
        if met[0] is not None:
            met = list(lax.optimization_barrier(tuple(met)))
        for side in sides:
            piece = side if lead else 1 - side
            value = given[(-distance if side == 0 else distance) % chips, piece]
            if after:
                value = tied(value, *after)
            if met[0] is not None:
                value = met[side].astype(jnp.float32) + value.astype(jnp.float32)
                value = value.astype(jnp.bfloat16)
            with jax.named_scope(f"back_{'lead' if lead else 'trail'}{distance}"):
                moving[side, piece] = lax.ppermute(value, "seq", hops[side])

    for distance in range(far, 0, -1):
        if distance == far:
            send(far - 1, False, *[came[side, far, side] for side in sides])
        elif distance > 1:
            send(distance - 1, False, worked[far] if distance == far - 1 else moving[0, 0])
        send(distance, True)
    final = []
    for piece in sides:
        total = given[0, piece].astype(jnp.float32)
        for side in sides:
            total += moving[side, piece].astype(jnp.float32)
        final.append(total)
    return (residual.astype(jnp.float32) + jnp.concatenate(final, axis=0)).astype(jnp.bfloat16)


def dispatched_experts(
    residual, normed, expert_ids, route_weights, gate_weight, up_weight, down_weight
):
    tokens_here = normed.shape[0]
    resid_f = residual.astype(jnp.float32)
    expert_count = EXP_DEV * lax.axis_size("seq")
    capacity = max(2, 3 * tokens_here * TOP // (2 * expert_count))
    flat_ids = expert_ids.reshape(-1)
    onehot = (flat_ids[:, None] == jnp.arange(expert_count, dtype=jnp.int32)[None, :]).astype(
        jnp.int32
    )
    earlier_count = jnp.cumsum(onehot, axis=0) - onehot
    slot_index = jnp.sum(earlier_count * onehot, axis=1)
    cell_index = (flat_ids * capacity + slot_index).reshape(tokens_here, TOP)
    chooser = jnp.any(
        cell_index[None, :, :]
        == jnp.arange(expert_count * capacity, dtype=jnp.int32)[:, None, None],
        axis=2,
    ).astype(jnp.bfloat16)
    outgoing = mm(chooser, normed).astype(jnp.bfloat16)
    outgoing = outgoing.reshape(expert_count, capacity, normed.shape[1])
    paired = lax.all_gather(outgoing, "rep", axis=1, tiled=True)
    arrived = lax.all_to_all(paired, "seq", split_axis=0, concat_axis=1, tiled=True)[0]
    gate_pre = mm(arrived, gate_weight)
    up_pre = mm(arrived, up_weight)
    activated = (gate_pre * jax.nn.sigmoid(1.702 * gate_pre) * (up_pre + 1.0)).astype(jnp.bfloat16)
    returned = lax.all_to_all(
        mm(activated, down_weight).astype(jnp.bfloat16)[None],
        "seq",
        split_axis=1,
        concat_axis=0,
        tiled=True,
    )
    expert_out = lax.psum_scatter(returned, "rep", scatter_dimension=1, tiled=True)
    picked = expert_out.reshape(expert_count * capacity, -1)[cell_index.reshape(-1)]
    picked = picked.reshape(tokens_here, TOP, -1)
    expert_sum = jnp.sum(route_weights[:, :, None] * picked.astype(jnp.float32), axis=1)
    return (resid_f + expert_sum).astype(jnp.bfloat16)


def per_device(
    stream,
    queries,
    key_rows,
    value_rows,
    sink_logits,
    out_weight,
    norm_gain,
    expert_ids,
    route_weights,
    gate_weight,
    up_weight,
    down_weight,
):
    block_len = queries.shape[0]
    seq = lax.axis_index("seq")
    rank = lax.axis_index("rep").astype(jnp.int32).reshape(1)
    gate_weight, up_weight, down_weight = gate_weight[0], up_weight[0], down_weight[0]
    use_ring = EXP_DEV * lax.axis_size("seq") <= 2 * TOP

    k_before, v_before = shifted(key_rows, "seq", 1), shifted(value_rows, "seq", 1)
    others = []
    if use_ring:
        others = [swapped(w, "rep") for w in (gate_weight, up_weight, down_weight)]
    first = (seq == 0).astype(jnp.int32).reshape(1)
    *operands, later_half = attend(
        sink_logits.reshape(1, -1), queries, key_rows, value_rows, out_weight
    )
    send, own = attend(*operands, (first, k_before, v_before, rank, later_half))
    came = swapped(send, "rep")
    expert_count = lax.axis_size("seq") * EXP_DEV if use_ring else 0
    residual, *pieces = norm(
        stream, own, came, norm_gain, expert_ids, route_weights, expert_count
    )
    if use_ring:
        *pieces, _ = lax.optimization_barrier((*pieces, others))
        return ring_experts(residual, pieces, gate_weight, up_weight, down_weight, others)
    return dispatched_experts(
        residual,
        pieces[0],
        expert_ids,
        route_weights,
        gate_weight,
        up_weight,
        down_weight,
    )


def solution(mesh):
    return jax.shard_map(
        per_device,
        mesh=mesh,
        in_specs=(
            P(("groups", "seq", "rep"), None),
            P(("groups", "seq"), "rep"),
            P(("groups", "seq"), "rep"),
            P(("groups", "seq"), "rep"),
            P("rep"),
            P("rep", None),
            P(),
            P(("groups", "seq", "rep"), None),
            P(("groups", "seq", "rep"), None),
            P("seq", None, "rep"),
            P("seq", None, "rep"),
            P("seq", "rep", None),
        ),
        out_specs=P(("groups", "seq", "rep"), None),
        check_vma=False,
    )
```

```python
import functools
import math

import jax
import jax.numpy as jnp
from jax import lax
from jax.experimental import pallas as pl
from jax.experimental.pallas import tpu as pltpu
from jax.sharding import PartitionSpec as P

HEAD_DIM = 64
WINDOW = 128
TOP = 4
TAIL = 16
EXP_DEV = 1
LANES = 128
SNAKES = {8: (0, 2, 4, 6, 7, 5, 3, 1)}
MIB = 1 << 20
EXPERT_VMEM = 8 * MIB


def shifted(value, axis, by):
    peers = lax.axis_size(axis)
    pairs = [(i, i + by) for i in range(peers) if 0 <= i + by < peers]
    return lax.ppermute(value, axis, pairs)


def pinned(values, space):
    return [pltpu.with_memory_space_constraint(value, space) for value in values]


def tied(value, *after):
    return lax.optimization_barrier((value,) + after)[0]


def swapped(value, axis, bit=1):
    peers = lax.axis_size(axis)
    return lax.ppermute(value, axis, [(i, i ^ bit) for i in range(peers)])


def mm(a, b):
    return jnp.dot(a, b, preferred_element_type=jnp.float32)


def tail_kernel(keys_hbm, values_hbm, out_ref, sems):
    rows, width = out_ref.shape
    last = pl.ds(keys_hbm.shape[0] - rows, rows)
    copies = [
        pltpu.make_async_copy(
            ref.at[last], out_ref.at[:, pl.ds(index * width // 2, width // 2)], sems.at[index]
        )
        for index, ref in enumerate((keys_hbm, values_hbm))
    ]
    for copy in copies:
        copy.start()
    for copy in copies:
        copy.wait()


def tail(keys, values):
    return pl.pallas_call(
        tail_kernel,
        in_specs=[pl.BlockSpec(memory_space=pltpu.HBM)] * 2,
        out_specs=pl.BlockSpec(memory_space=pltpu.VMEM),
        out_shape=jax.ShapeDtypeStruct((WINDOW, 2 * keys.shape[1]), keys.dtype),
        scratch_shapes=[pltpu.SemaphoreType.DMA((2,))],
        name="tail",
    )(*pinned((keys, values), pltpu.HBM))


def attend_kernel(mix, *refs):
    if mix:
        sink_ref, q_ref, k_ref, v_ref, ow_ref = refs[:5]
        first_ref, before_ref, rank_ref, later_ref, send_ref, own_ref, done_ref = refs[5:]
        rows, width = before_ref.shape[0], k_ref.shape[1]
        queries = slice(0, rows)
        k = jnp.concatenate([before_ref[:, :width], k_ref[:rows]], axis=0)
        v = jnp.concatenate([before_ref[:, width:], v_ref[:rows]], axis=0)
        done_ref[rows:] = later_ref[...]
        copies = []
    else:
        sink_ref, q_ref, k_ref, v_ref, ow_ref, done_ref = refs[5:11]
        rows = done_ref.shape[0]
        queries = slice(rows, 2 * rows)
        sems = refs[-1]
        early, late = pl.ds(0, rows), pl.ds(rows, rows)
        sources = [(refs[2], k_ref), (refs[3], v_ref), (refs[1].at[late], q_ref.at[late])]
        sources += [(refs[0], sink_ref), (refs[4], ow_ref), (refs[1].at[early], q_ref.at[early])]
        copies = [
            pltpu.make_async_copy(here, there, sems.at[index])
            for index, (here, there) in enumerate(sources)
        ]
        for copy in copies:
            copy.start()
        for copy in copies[:4]:
            copy.wait()
        k, v = k_ref[...], v_ref[...]
    keys = 2 * rows
    pairs = q_ref.shape[1] // LANES
    groups = k_ref.shape[1] // HEAD_DIM

    low = lax.broadcasted_iota(jnp.int32, (keys, LANES), 1) < HEAD_DIM
    k = k.astype(jnp.float32) * (1.0 / math.sqrt(HEAD_DIM))
    v = v.astype(jnp.float32)
    k_turned, v_turned = pltpu.roll(k, HEAD_DIM, 1), pltpu.roll(v, HEAD_DIM, 1)
    key = lax.broadcasted_iota(jnp.int32, (keys, rows), 0)
    query = lax.broadcasted_iota(jnp.int32, (keys, rows), 1)
    allowed = (key <= query + rows) & (key > query)
    if mix:
        allowed = allowed & (key >= jnp.where(first_ref[0] == 1, rows, 0))
    ones = jnp.ones((8, keys), jnp.float32)
    zeros = jnp.zeros((8, keys), jnp.float32)

    for group in range(groups):
        here, there = (k, v), (k_turned, v_turned)
        lows, highs = (here, there) if group == 0 else (there, here)
        kk = jnp.concatenate(
            [jnp.where(low, lows[0], 0.0), jnp.where(low, 0.0, highs[0])], axis=0
        ).astype(jnp.bfloat16)
        v_low = jnp.where(low, lows[1], 0.0).T
        v_high = jnp.where(low, 0.0, highs[1]).T
        vv = jnp.concatenate(
            [
                jnp.concatenate([v_low, v_high], axis=1),
                jnp.concatenate([ones, zeros], axis=1),
                jnp.concatenate([zeros, ones], axis=1),
            ],
            axis=0,
        ).astype(jnp.bfloat16)
        for pair in range(group * pairs // groups, (group + 1) * pairs // groups):
            lanes = slice(pair * LANES, (pair + 1) * LANES)
            scores = lax.dot_general(
                kk, q_ref[queries, lanes], (((1,), (1,)), ((), ())), preferred_element_type=jnp.float32
            )
            weights, sinks = [], []
            for side in range(2):
                part = jnp.where(allowed, scores[side * keys : (side + 1) * keys], -jnp.inf)
                sink = sink_ref[:, 2 * pair + side : 2 * pair + side + 1]
                highest = jnp.maximum(jnp.max(part, axis=0, keepdims=True), sink)
                weights.append(jnp.exp(part - highest).astype(jnp.bfloat16))
                sinks.append(jnp.exp(sink - highest))
            both = mm(vv, jnp.concatenate(weights, axis=0))
            parts = [
                both[side * HEAD_DIM : (side + 1) * HEAD_DIM]
                / (both[LANES + 8 * side : LANES + 8 * side + 1] + sinks[side])
                for side in range(2)
            ]
            done_ref[:rows, lanes] = jnp.concatenate(parts, axis=0).T.astype(jnp.bfloat16)

    for copy in copies[4:]:
        copy.wait()
    if not mix:
        return
    model = ow_ref.shape[1]
    width = 512 if model % 512 == 0 else model
    own_first = rank_ref[0] == 0
    for start in range(0, model, width):
        lanes = slice(start, start + width)
        both = mm(done_ref[...], ow_ref[:, lanes])
        early, late = both[:rows], both[rows:]
        own_ref[:, lanes] = jnp.where(own_first, early, late)
        send_ref[:, lanes] = jnp.where(own_first, late, early).astype(jnp.bfloat16)


def attend(sinks, queries, keys, values, out_weight, mixed=()):
    mix = bool(mixed)
    rows, width, model = WINDOW, queries.shape[1], out_weight.shape[1]
    smem = pl.BlockSpec(memory_space=pltpu.SMEM)
    vmem = pl.BlockSpec(memory_space=pltpu.VMEM)
    hbm = pl.BlockSpec(memory_space=pltpu.HBM)
    operands = (sinks, queries, keys, values, out_weight)
    wide = jax.ShapeDtypeStruct((rows, model), jnp.float32)
    narrow = jax.ShapeDtypeStruct((rows, model), jnp.bfloat16)
    shapes = (narrow, wide)
    if not mix:
        shapes = tuple(jax.ShapeDtypeStruct(a.shape, a.dtype) for a in operands)
        shapes += (jax.ShapeDtypeStruct((rows, width), jnp.bfloat16),)
    return pl.pallas_call(
        functools.partial(attend_kernel, mix),
        in_specs=[vmem if mix else hbm] * 5 + ([smem, vmem, smem, vmem] if mix else []),
        out_specs=(vmem,) * len(shapes),
        out_shape=shapes,
        scratch_shapes=[
            pltpu.VMEM((2 * rows, width), jnp.bfloat16) if mix else pltpu.SemaphoreType.DMA((6,))
        ],
        compiler_params=pltpu.CompilerParams(vmem_limit_bytes=8 * MIB),
        cost_estimate=pl.CostEstimate(
            flops=2 * rows * width * (model + 1024), bytes_accessed=6 * MIB, transcendentals=0
        ),
        name="attend",
    )(*pinned(operands, pltpu.VMEM if mix else pltpu.HBM), *mixed)


def norm_kernel(
    expert_count, stream_ref, own_ref, came_ref, gain_ref, ids_ref, route_ref, *rest
):
    residual_ref, *message_refs = rest
    rows, model = stream_ref.shape
    residual = (
        stream_ref[...].astype(jnp.float32) + own_ref[...] + came_ref[...].astype(jnp.float32)
    ).astype(jnp.bfloat16)
    residual_ref[...] = residual
    wide = residual.astype(jnp.float32)
    mean = jnp.mean(wide * wide, axis=-1, keepdims=True)
    normed = (wide * lax.rsqrt(mean + 1e-05) * gain_ref[...]).astype(jnp.bfloat16)
    if not expert_count:
        message_refs[0][...] = normed
        return
    size = rows // len(message_refs)
    expert = lax.broadcasted_iota(jnp.int32, (TAIL, rows), 0)
    dense = jnp.zeros((TAIL, rows), jnp.float32)
    for k in range(TOP):
        dense += jnp.where(expert == ids_ref[k : k + 1, :], route_ref[k : k + 1, :], 0.0)
    lead = dense.astype(jnp.bfloat16).astype(jnp.float32)
    rest = dense - lead
    for index, ref in enumerate(message_refs):
        for block in range(model // LANES):
            ref[block * size : (block + 1) * size] = normed[
                index * size : (index + 1) * size, block * LANES : (block + 1) * LANES
            ]
        span = slice(index * size, (index + 1) * size)
        both = jnp.concatenate([lead[:, span], rest[:, span]], axis=1)
        ref[model // LANES * size :] = both.astype(jnp.bfloat16)


def norm(stream, own, came, gain, expert_ids, route_weights, expert_count):
    rows, model = stream.shape
    vmem = pl.BlockSpec(memory_space=pltpu.VMEM)
    pieces, shape = 1, (rows, model)
    if expert_count:
        pieces = 2
        shape = (rows // pieces * (model // LANES) + TAIL, LANES)
    return pl.pallas_call(
        functools.partial(norm_kernel, expert_count),
        in_specs=[vmem] * 6,
        out_shape=[jax.ShapeDtypeStruct((rows, model), jnp.bfloat16)]
        + [jax.ShapeDtypeStruct(shape, jnp.bfloat16)] * pieces,
        compiler_params=pltpu.CompilerParams(vmem_limit_bytes=8 * MIB),
        cost_estimate=pl.CostEstimate(
            flops=8 * rows * model, bytes_accessed=14 * rows * model, transcendentals=rows
        ),
        name="norm",
    )(stream, own, came, gain.reshape(1, model), expert_ids.T, route_weights.T)


def expert_kernel(tile, count, load, me_ref, *refs):
    x_refs, halves = refs[:count], refs[count : count + 6]
    out_refs, rest = refs[count + 6 : 2 * count + 6], refs[2 * count + 6 :]
    copies = []
    if load:
        kept, rest = rest[:3], rest[3:]
        copies = [
            pltpu.make_async_copy(here, there, rest[2].at[index])
            for index, (here, there) in enumerate(zip(halves[3:], kept))
        ]
        for copy in copies:
            copy.start()
        halves = halves[:3] + kept
    x, hidden = rest[:2]
    model, half = halves[0].shape
    rows = x.shape[0] // count
    body = rows * (model // LANES)
    for index, ref in enumerate(x_refs):
        for block in range(model // LANES):
            x[index * rows : (index + 1) * rows, block * LANES : (block + 1) * LANES] = ref[
                block * rows : (block + 1) * rows
            ]

    def arrived(*which):
        for index in which:
            if copies:
                copies[index].wait()

    def work(side, at):
        gate_ref, up_ref = halves[3 * side : 3 * side + 2]
        gate_pre = mm(x[...], gate_ref[:, at : at + tile])
        up_pre = mm(x[...], up_ref[:, at : at + tile])
        activated = gate_pre * jax.nn.sigmoid(1.702 * gate_pre) * (up_pre + 1.0)
        hidden[:, side * half + at : side * half + at + tile] = activated.astype(jnp.bfloat16)

    for side in range(2):
        if side == 1:
            arrived(0, 1)
        for at in range(0, half, tile):
            work(side, at)
    arrived(2)

    me = me_ref[0]
    scales = []
    for ref in x_refs:
        sent = ref[body:].astype(jnp.float32)
        expert = lax.broadcasted_iota(jnp.int32, sent.shape, 0)
        mine = jnp.sum(jnp.where(expert == me, sent, 0.0), axis=0, keepdims=True)
        mine = jnp.broadcast_to(mine, (8, LANES))
        scales.append((mine + pltpu.roll(mine, LANES - rows, 1)).T[:rows, :1])
    for at in range(0, model, tile):
        lanes = slice(at, at + tile)
        total = mm(hidden[:, :half], halves[2][:, lanes]) + mm(hidden[:, half:], halves[5][:, lanes])
        for index, (ref, scale) in enumerate(zip(out_refs, scales)):
            ref[:, lanes] = (total[index * rows : (index + 1) * rows] * scale).astype(jnp.bfloat16)


def experts(blocks, me, halves, load=False):
    model, half = halves[0].shape
    size = (blocks[0].shape[0] - TAIL) // (model // LANES)
    rows = size * len(blocks)
    vmem = pl.BlockSpec(memory_space=pltpu.VMEM)
    hbm = pl.BlockSpec(memory_space=pltpu.HBM)
    kept = [jax.ShapeDtypeStruct(w.shape, w.dtype) for w in halves[3:]] if load else []
    scratch = [
        pltpu.VMEM((rows, model), jnp.bfloat16),
        pltpu.VMEM((rows, 2 * half), jnp.bfloat16),
    ]
    return pl.pallas_call(
        functools.partial(expert_kernel, min(256, half), len(blocks), load),
        in_specs=[pl.BlockSpec(memory_space=pltpu.SMEM)]
        + [vmem] * len(blocks)
        + [vmem] * 3
        + [hbm if load else vmem] * 3,
        out_specs=[vmem] * (len(blocks) + len(kept)),
        out_shape=[jax.ShapeDtypeStruct((size, model), jnp.bfloat16)] * len(blocks) + kept,
        scratch_shapes=scratch + ([pltpu.SemaphoreType.DMA((3,))] if load else []),
        compiler_params=pltpu.CompilerParams(vmem_limit_bytes=EXPERT_VMEM),
        cost_estimate=pl.CostEstimate(
            flops=12 * rows * model * half, bytes_accessed=6 * rows * model, transcendentals=0
        ),
        name="experts",
    )(
        me,
        *blocks,
        *pinned(halves[:3], pltpu.VMEM),
        *pinned(halves[3:], pltpu.HBM if load else pltpu.VMEM),
    )


def ring_experts(residual, pieces, gate_weight, up_weight, down_weight, others):
    chips = lax.axis_size("seq")
    ring = SNAKES.get(chips, tuple(range(chips)))
    far = chips // 2
    ahead = [(ring[i], ring[(i + 1) % chips]) for i in range(chips)]
    hops = (ahead, [(to, of) for of, to in ahead])
    sides = (0, 1)
    me = lax.axis_index("seq").astype(jnp.int32).reshape(1)
    given = {}

    def keep(keys, outs):
        for (side, distance, piece), out in zip(keys, outs):
            given[(distance if side == 0 else -distance) % chips, piece] = out

    halves = (gate_weight, up_weight, down_weight) + tuple(others)
    outs = experts(pieces, me, halves, load=True)
    halves = halves[:3] + tuple(outs[2:])
    keep([(0, 0, 0), (0, 0, 1)], outs)
    worked = {0: outs[0]}
    came = {(side, 0, piece): pieces[piece] for side in sides for piece in sides}

    def bring(distance, lead, *after):
        keys = [(side, distance - 1, side if lead else 1 - side) for side in sides]
        met = lax.optimization_barrier((*(came[key] for key in keys), *after))
        for (side, _, piece), block in zip(keys, met):
            with jax.named_scope(f"out_{'lead' if lead else 'trail'}{distance}"):
                came[side, distance, piece] = lax.ppermute(block, "seq", hops[side])

    def apply(distance, kinds, *after):
        keys = [(side, distance, side if lead else 1 - side) for lead in kinds for side in sides]
        blocks = [came[key] for key in keys]
        if after:
            blocks[0] = tied(blocks[0], *after)
        with jax.named_scope(f"hop{distance}"):
            outs = experts(blocks, me, halves)
        worked.setdefault(distance, outs[0])
        keep(keys, outs)
        return outs[0]

    for distance in range(1, far + 1):
        bring(distance, True, *([worked[distance - 2]] if distance > 1 else []))
        trails = []
        if distance < far:
            before = [came[side, distance - 1, side] for side in sides] if distance > 1 else []
            bring(distance, False, *before)
            if 1 < distance < far - 1:
                trails = [came[side, distance, 1 - side] for side in sides]
        latest = apply(distance, (True,), worked[distance - 1], *trails)
    latest = apply(far - 1, (False,), latest)

    moving = {}

    def send(distance, lead, *after):
        met = [moving.get((side, side if lead else 1 - side)) for side in sides]
        if met[0] is not None:
            met = list(lax.optimization_barrier(tuple(met)))
        for side in sides:
            piece = side if lead else 1 - side
            value = given[(-distance if side == 0 else distance) % chips, piece]
            if after:
                value = tied(value, *after)
            if met[0] is not None:
                value = met[side].astype(jnp.float32) + value.astype(jnp.float32)
                value = value.astype(jnp.bfloat16)
            with jax.named_scope(f"back_{'lead' if lead else 'trail'}{distance}"):
                moving[side, piece] = lax.ppermute(value, "seq", hops[side])

    send(far, True)
    send(far - 1, False, *[came[side, far, side] for side in sides])
    for distance in range(far - 1, 0, -1):
        leads = [moving[side, side] for side in sides]
        send(distance, True)
        if distance > 1:
            latest = apply(distance - 1, (False,), latest, *leads)
            send(distance - 1, False, leads[0])
    final = []
    for piece in sides:
        total = given[0, piece].astype(jnp.float32)
        for side in sides:
            total += moving[side, piece].astype(jnp.float32)
        final.append(total)
    return (residual.astype(jnp.float32) + jnp.concatenate(final, axis=0)).astype(jnp.bfloat16)


def dispatched_experts(
    residual, normed, expert_ids, route_weights, gate_weight, up_weight, down_weight
):
    tokens_here = normed.shape[0]
    resid_f = residual.astype(jnp.float32)
    expert_count = EXP_DEV * lax.axis_size("seq")
    capacity = max(2, 3 * tokens_here * TOP // (2 * expert_count))
    flat_ids = expert_ids.reshape(-1)
    onehot = (flat_ids[:, None] == jnp.arange(expert_count, dtype=jnp.int32)[None, :]).astype(
        jnp.int32
    )
    earlier_count = jnp.cumsum(onehot, axis=0) - onehot
    slot_index = jnp.sum(earlier_count * onehot, axis=1)
    cell_index = (flat_ids * capacity + slot_index).reshape(tokens_here, TOP)
    chooser = jnp.any(
        cell_index[None, :, :]
        == jnp.arange(expert_count * capacity, dtype=jnp.int32)[:, None, None],
        axis=2,
    ).astype(jnp.bfloat16)
    outgoing = mm(chooser, normed).astype(jnp.bfloat16)
    outgoing = outgoing.reshape(expert_count, capacity, normed.shape[1])
    paired = lax.all_gather(outgoing, "rep", axis=1, tiled=True)
    arrived = lax.all_to_all(paired, "seq", split_axis=0, concat_axis=1, tiled=True)[0]
    gate_pre = mm(arrived, gate_weight)
    up_pre = mm(arrived, up_weight)
    activated = (gate_pre * jax.nn.sigmoid(1.702 * gate_pre) * (up_pre + 1.0)).astype(jnp.bfloat16)
    returned = lax.all_to_all(
        mm(activated, down_weight).astype(jnp.bfloat16)[None],
        "seq",
        split_axis=1,
        concat_axis=0,
        tiled=True,
    )
    expert_out = lax.psum_scatter(returned, "rep", scatter_dimension=1, tiled=True)
    picked = expert_out.reshape(expert_count * capacity, -1)[cell_index.reshape(-1)]
    picked = picked.reshape(tokens_here, TOP, -1)
    expert_sum = jnp.sum(route_weights[:, :, None] * picked.astype(jnp.float32), axis=1)
    return (resid_f + expert_sum).astype(jnp.bfloat16)


def per_device(
    stream,
    queries,
    key_rows,
    value_rows,
    sink_logits,
    out_weight,
    norm_gain,
    expert_ids,
    route_weights,
    gate_weight,
    up_weight,
    down_weight,
):
    block_len = queries.shape[0]
    seq = lax.axis_index("seq")
    rank = lax.axis_index("rep").astype(jnp.int32).reshape(1)
    gate_weight, up_weight, down_weight = gate_weight[0], up_weight[0], down_weight[0]
    use_ring = EXP_DEV * lax.axis_size("seq") <= 2 * TOP

    before = shifted(tail(key_rows, value_rows), "seq", 1)
    others = []
    if use_ring:
        others = [swapped(w, "rep") for w in (gate_weight, up_weight, down_weight)]
    first = (seq == 0).astype(jnp.int32).reshape(1)
    *operands, later_half = attend(
        sink_logits.reshape(1, -1), queries, key_rows, value_rows, out_weight
    )
    send, own = attend(*operands, (first, before, rank, later_half))
    came = swapped(send, "rep")
    expert_count = lax.axis_size("seq") * EXP_DEV if use_ring else 0
    residual, *pieces = norm(
        stream, own, came, norm_gain, expert_ids, route_weights, expert_count
    )
    if use_ring:
        *pieces, _ = lax.optimization_barrier((*pieces, others))
        return ring_experts(residual, pieces, gate_weight, up_weight, down_weight, others)
    return dispatched_experts(
        residual,
        pieces[0],
        expert_ids,
        route_weights,
        gate_weight,
        up_weight,
        down_weight,
    )


def solution(mesh):
    return jax.shard_map(
        per_device,
        mesh=mesh,
        in_specs=(
            P(("groups", "seq", "rep"), None),
            P(("groups", "seq"), "rep"),
            P(("groups", "seq"), "rep"),
            P(("groups", "seq"), "rep"),
            P("rep"),
            P("rep", None),
            P(),
            P(("groups", "seq", "rep"), None),
            P(("groups", "seq", "rep"), None),
            P("seq", None, "rep"),
            P("seq", None, "rep"),
            P("seq", "rep", None),
        ),
        out_specs=P(("groups", "seq", "rep"), None),
        check_vma=False,
    )
```

```python
import functools
import math

import jax
import jax.numpy as jnp
from jax import lax
from jax.experimental import pallas as pl
from jax.experimental.pallas import tpu as pltpu
from jax.sharding import PartitionSpec as P

HEAD_DIM = 64
WINDOW = 128
TOP = 4
TAIL = 16
EXP_DEV = 1
LANES = 128
SNAKES = {8: (0, 2, 4, 6, 7, 5, 3, 1)}
MIB = 1 << 20
EXPERT_VMEM = 8 * MIB


def shifted(value, axis, by):
    peers = lax.axis_size(axis)
    return lax.ppermute(value, axis, [(i, (i + by) % peers) for i in range(peers)])


def pinned(values, space):
    return [pltpu.with_memory_space_constraint(value, space) for value in values]


def tied(value, *after):
    return lax.optimization_barrier((value,) + after)[0]


def swapped(value, axis, bit=1):
    peers = lax.axis_size(axis)
    return lax.ppermute(value, axis, [(i, i ^ bit) for i in range(peers)])


def mm(a, b):
    return jnp.dot(a, b, preferred_element_type=jnp.float32)


def attend_kernel(mix, *refs):
    if mix:
        sink_ref, q_ref, k_ref, v_ref, ow_ref = refs[:5]
        first_ref, k_before, v_before, rank_ref, later_ref, send_ref, own_ref, done_ref = refs[5:]
        rows = later_ref.shape[0]
        queries = slice(0, rows)
        k = jnp.concatenate([k_before[rows:], k_ref[:rows]], axis=0)
        v = jnp.concatenate([v_before[rows:], v_ref[:rows]], axis=0)
        done_ref[rows:] = later_ref[...]
        copies = []
    else:
        sink_ref, q_ref, k_ref, v_ref, ow_ref, done_ref = refs[5:11]
        rows = done_ref.shape[0]
        queries = slice(rows, 2 * rows)
        sems = refs[-1]
        early, late = pl.ds(0, rows), pl.ds(rows, rows)
        sources = [(refs[2], k_ref), (refs[3], v_ref), (refs[1].at[late], q_ref.at[late])]
        sources += [(refs[0], sink_ref), (refs[4], ow_ref), (refs[1].at[early], q_ref.at[early])]
        copies = [
            pltpu.make_async_copy(here, there, sems.at[index])
            for index, (here, there) in enumerate(sources)
        ]
        for copy in copies:
            copy.start()
        for copy in copies[:4]:
            copy.wait()
        k, v = k_ref[...], v_ref[...]
    keys = 2 * rows
    pairs = q_ref.shape[1] // LANES
    groups = k_ref.shape[1] // HEAD_DIM

    low = lax.broadcasted_iota(jnp.int32, (keys, LANES), 1) < HEAD_DIM
    k = k.astype(jnp.float32) * (1.0 / math.sqrt(HEAD_DIM))
    v = v.astype(jnp.float32)
    k_turned, v_turned = pltpu.roll(k, HEAD_DIM, 1), pltpu.roll(v, HEAD_DIM, 1)
    key = lax.broadcasted_iota(jnp.int32, (keys, rows), 0)
    query = lax.broadcasted_iota(jnp.int32, (keys, rows), 1)
    allowed = (key <= query + rows) & (key > query)
    if mix:
        allowed = allowed & (key >= jnp.where(first_ref[0] == 1, rows, 0))
    ones = jnp.ones((8, keys), jnp.float32)
    zeros = jnp.zeros((8, keys), jnp.float32)

    for group in range(groups):
        here, there = (k, v), (k_turned, v_turned)
        lows, highs = (here, there) if group == 0 else (there, here)
        kk = jnp.concatenate(
            [jnp.where(low, lows[0], 0.0), jnp.where(low, 0.0, highs[0])], axis=0
        ).astype(jnp.bfloat16)
        v_low = jnp.where(low, lows[1], 0.0).T
        v_high = jnp.where(low, 0.0, highs[1]).T
        vv = jnp.concatenate(
            [
                jnp.concatenate([v_low, v_high], axis=1),
                jnp.concatenate([ones, zeros], axis=1),
                jnp.concatenate([zeros, ones], axis=1),
            ],
            axis=0,
        ).astype(jnp.bfloat16)
        for pair in range(group * pairs // groups, (group + 1) * pairs // groups):
            lanes = slice(pair * LANES, (pair + 1) * LANES)
            scores = lax.dot_general(
                kk, q_ref[queries, lanes], (((1,), (1,)), ((), ())), preferred_element_type=jnp.float32
            )
            weights, sinks = [], []
            for side in range(2):
                part = jnp.where(allowed, scores[side * keys : (side + 1) * keys], -jnp.inf)
                sink = sink_ref[:, 2 * pair + side : 2 * pair + side + 1]
                highest = jnp.maximum(jnp.max(part, axis=0, keepdims=True), sink)
                weights.append(jnp.exp(part - highest).astype(jnp.bfloat16))
                sinks.append(jnp.exp(sink - highest))
            both = mm(vv, jnp.concatenate(weights, axis=0))
            parts = [
                both[side * HEAD_DIM : (side + 1) * HEAD_DIM]
                / (both[LANES + 8 * side : LANES + 8 * side + 1] + sinks[side])
                for side in range(2)
            ]
            done_ref[:rows, lanes] = jnp.concatenate(parts, axis=0).T.astype(jnp.bfloat16)

    for copy in copies[4:]:
        copy.wait()
    if not mix:
        return
    model = ow_ref.shape[1]
    width = 512 if model % 512 == 0 else model
    own_first = rank_ref[0] == 0
    for start in range(0, model, width):
        lanes = slice(start, start + width)
        both = mm(done_ref[...], ow_ref[:, lanes])
        early, late = both[:rows], both[rows:]
        own_ref[:, lanes] = jnp.where(own_first, early, late)
        send_ref[:, lanes] = jnp.where(own_first, late, early).astype(jnp.bfloat16)


def attend(sinks, queries, keys, values, out_weight, mixed=()):
    mix = bool(mixed)
    rows, width, model = WINDOW, queries.shape[1], out_weight.shape[1]
    smem = pl.BlockSpec(memory_space=pltpu.SMEM)
    vmem = pl.BlockSpec(memory_space=pltpu.VMEM)
    hbm = pl.BlockSpec(memory_space=pltpu.HBM)
    operands = (sinks, queries, keys, values, out_weight)
    wide = jax.ShapeDtypeStruct((rows, model), jnp.float32)
    narrow = jax.ShapeDtypeStruct((rows, model), jnp.bfloat16)
    shapes = (narrow, wide)
    if not mix:
        shapes = tuple(jax.ShapeDtypeStruct(a.shape, a.dtype) for a in operands)
        shapes += (jax.ShapeDtypeStruct((rows, width), jnp.bfloat16),)
    return pl.pallas_call(
        functools.partial(attend_kernel, mix),
        in_specs=[vmem if mix else hbm] * 5 + ([smem, vmem, vmem, smem, vmem] if mix else []),
        out_specs=(vmem,) * len(shapes),
        out_shape=shapes,
        scratch_shapes=[
            pltpu.VMEM((2 * rows, width), jnp.bfloat16) if mix else pltpu.SemaphoreType.DMA((6,))
        ],
        compiler_params=pltpu.CompilerParams(vmem_limit_bytes=8 * MIB),
        cost_estimate=pl.CostEstimate(
            flops=2 * rows * width * (model + 1024), bytes_accessed=6 * MIB, transcendentals=0
        ),
        name="attend",
    )(*pinned(operands, pltpu.VMEM if mix else pltpu.HBM), *mixed)


def norm_kernel(
    expert_count, stream_ref, own_ref, came_ref, gain_ref, ids_ref, route_ref, *rest
):
    residual_ref, *message_refs = rest
    rows, model = stream_ref.shape
    residual = (
        stream_ref[...].astype(jnp.float32) + own_ref[...] + came_ref[...].astype(jnp.float32)
    ).astype(jnp.bfloat16)
    residual_ref[...] = residual
    wide = residual.astype(jnp.float32)
    mean = jnp.mean(wide * wide, axis=-1, keepdims=True)
    normed = (wide * lax.rsqrt(mean + 1e-05) * gain_ref[...]).astype(jnp.bfloat16)
    if not expert_count:
        message_refs[0][...] = normed
        return
    size = rows // len(message_refs)
    expert = lax.broadcasted_iota(jnp.int32, (TAIL, rows), 0)
    dense = jnp.zeros((TAIL, rows), jnp.float32)
    for k in range(TOP):
        dense += jnp.where(expert == ids_ref[k : k + 1, :], route_ref[k : k + 1, :], 0.0)
    lead = dense.astype(jnp.bfloat16).astype(jnp.float32)
    rest = dense - lead
    for index, ref in enumerate(message_refs):
        for block in range(model // LANES):
            ref[block * size : (block + 1) * size] = normed[
                index * size : (index + 1) * size, block * LANES : (block + 1) * LANES
            ]
        span = slice(index * size, (index + 1) * size)
        both = jnp.concatenate([lead[:, span], rest[:, span]], axis=1)
        ref[model // LANES * size :] = both.astype(jnp.bfloat16)


def norm(stream, own, came, gain, expert_ids, route_weights, expert_count):
    rows, model = stream.shape
    vmem = pl.BlockSpec(memory_space=pltpu.VMEM)
    pieces, shape = 1, (rows, model)
    if expert_count:
        pieces = 2
        shape = (rows // pieces * (model // LANES) + TAIL, LANES)
    return pl.pallas_call(
        functools.partial(norm_kernel, expert_count),
        in_specs=[vmem] * 6,
        out_shape=[jax.ShapeDtypeStruct((rows, model), jnp.bfloat16)]
        + [jax.ShapeDtypeStruct(shape, jnp.bfloat16)] * pieces,
        compiler_params=pltpu.CompilerParams(vmem_limit_bytes=8 * MIB),
        cost_estimate=pl.CostEstimate(
            flops=8 * rows * model, bytes_accessed=14 * rows * model, transcendentals=rows
        ),
        name="norm",
    )(stream, own, came, gain.reshape(1, model), expert_ids.T, route_weights.T)


def expert_kernel(tile, count, load, me_ref, *refs):
    x_refs, halves = refs[:count], refs[count : count + 6]
    out_refs, rest = refs[count + 6 : 2 * count + 6], refs[2 * count + 6 :]
    copies = []
    if load:
        kept, rest = rest[:3], rest[3:]
        copies = [
            pltpu.make_async_copy(here, there, rest[2].at[index])
            for index, (here, there) in enumerate(zip(halves[3:], kept))
        ]
        for copy in copies:
            copy.start()
        halves = halves[:3] + kept
    x, hidden = rest[:2]
    model, half = halves[0].shape
    rows = x.shape[0] // count
    body = rows * (model // LANES)
    for index, ref in enumerate(x_refs):
        for block in range(model // LANES):
            x[index * rows : (index + 1) * rows, block * LANES : (block + 1) * LANES] = ref[
                block * rows : (block + 1) * rows
            ]

    def arrived(*which):
        for index in which:
            if copies:
                copies[index].wait()

    def work(side, at):
        gate_ref, up_ref = halves[3 * side : 3 * side + 2]
        gate_pre = mm(x[...], gate_ref[:, at : at + tile])
        up_pre = mm(x[...], up_ref[:, at : at + tile])
        activated = gate_pre * jax.nn.sigmoid(1.702 * gate_pre) * (up_pre + 1.0)
        hidden[:, side * half + at : side * half + at + tile] = activated.astype(jnp.bfloat16)

    for side in range(2):
        if side == 1:
            arrived(0, 1)
        for at in range(0, half, tile):
            work(side, at)
    arrived(2)

    me = me_ref[0]
    scales = []
    for ref in x_refs:
        sent = ref[body:].astype(jnp.float32)
        expert = lax.broadcasted_iota(jnp.int32, sent.shape, 0)
        mine = jnp.sum(jnp.where(expert == me, sent, 0.0), axis=0, keepdims=True)
        mine = jnp.broadcast_to(mine, (8, LANES))
        scales.append((mine + pltpu.roll(mine, LANES - rows, 1)).T[:rows, :1])
    for at in range(0, model, tile):
        lanes = slice(at, at + tile)
        total = mm(hidden[:, :half], halves[2][:, lanes]) + mm(hidden[:, half:], halves[5][:, lanes])
        for index, (ref, scale) in enumerate(zip(out_refs, scales)):
            ref[:, lanes] = (total[index * rows : (index + 1) * rows] * scale).astype(jnp.bfloat16)


def experts(blocks, me, halves, load=False):
    model, half = halves[0].shape
    size = (blocks[0].shape[0] - TAIL) // (model // LANES)
    rows = size * len(blocks)
    vmem = pl.BlockSpec(memory_space=pltpu.VMEM)
    hbm = pl.BlockSpec(memory_space=pltpu.HBM)
    kept = [jax.ShapeDtypeStruct(w.shape, w.dtype) for w in halves[3:]] if load else []
    scratch = [
        pltpu.VMEM((rows, model), jnp.bfloat16),
        pltpu.VMEM((rows, 2 * half), jnp.bfloat16),
    ]
    return pl.pallas_call(
        functools.partial(expert_kernel, min(256, half), len(blocks), load),
        in_specs=[pl.BlockSpec(memory_space=pltpu.SMEM)]
        + [vmem] * len(blocks)
        + [vmem] * 3
        + [hbm if load else vmem] * 3,
        out_specs=[vmem] * (len(blocks) + len(kept)),
        out_shape=[jax.ShapeDtypeStruct((size, model), jnp.bfloat16)] * len(blocks) + kept,
        scratch_shapes=scratch + ([pltpu.SemaphoreType.DMA((3,))] if load else []),
        compiler_params=pltpu.CompilerParams(vmem_limit_bytes=EXPERT_VMEM),
        cost_estimate=pl.CostEstimate(
            flops=12 * rows * model * half, bytes_accessed=6 * rows * model, transcendentals=0
        ),
        name="experts",
    )(
        me,
        *blocks,
        *pinned(halves[:3], pltpu.VMEM),
        *pinned(halves[3:], pltpu.HBM if load else pltpu.VMEM),
    )


def ring_experts(residual, pieces, gate_weight, up_weight, down_weight, others):
    chips = lax.axis_size("seq")
    ring = SNAKES.get(chips, tuple(range(chips)))
    far = chips // 2
    ahead = [(ring[i], ring[(i + 1) % chips]) for i in range(chips)]
    hops = (ahead, [(to, of) for of, to in ahead])
    sides = (0, 1)
    me = lax.axis_index("seq").astype(jnp.int32).reshape(1)
    given = {}

    def keep(keys, outs):
        for (side, distance, piece), out in zip(keys, outs):
            given[(distance if side == 0 else -distance) % chips, piece] = out

    halves = (gate_weight, up_weight, down_weight) + tuple(others)
    outs = experts(pieces, me, halves, load=True)
    halves = halves[:3] + tuple(outs[2:])
    keep([(0, 0, 0), (0, 0, 1)], outs)
    worked = {0: outs[0]}
    came = {(side, 0, piece): pieces[piece] for side in sides for piece in sides}

    def bring(distance, lead, *after):
        keys = [(side, distance - 1, side if lead else 1 - side) for side in sides]
        met = lax.optimization_barrier(tuple(came[key] for key in keys))
        for (side, _, piece), block in zip(keys, met):
            block = tied(block, *after)
            with jax.named_scope(f"out_{'lead' if lead else 'trail'}{distance}"):
                came[side, distance, piece] = lax.ppermute(block, "seq", hops[side])

    def both(value):
        return swapped(value[:16, :LANES], "rep")

    def apply(distance, kinds, *after):
        keys = [(side, distance, side if lead else 1 - side) for lead in kinds for side in sides]
        blocks = [came[key] for key in keys]
        if after:
            blocks[0] = tied(blocks[0], *after)
        with jax.named_scope(f"hop{distance}"):
            outs = experts(blocks, me, halves)
        worked.setdefault(distance, outs[0])
        keep(keys, outs)
        return outs[0]

    for distance in range(1, far + 1):
        hold = [worked[distance - 2]] if distance > 1 else []
        if distance == far:
            hold.append(both(hold[0]))
        bring(distance, True, *hold)
        trails = []
        if distance < far:
            before = [came[side, distance - 1, side] for side in sides] if distance > 1 else []
            bring(distance, False, *before)
            if 1 < distance < far - 1:
                trails = [came[side, distance, 1 - side] for side in sides]
        latest = apply(distance, (True,), worked[distance - 1], *trails)
    latest = apply(far - 1, (False,), latest)

    moving = {}

    def send(distance, lead, *after):
        met = [moving.get((side, side if lead else 1 - side)) for side in sides]
        if met[0] is not None:
            met = list(lax.optimization_barrier(tuple(met)))
        for side in sides:
            piece = side if lead else 1 - side
            value = given[(-distance if side == 0 else distance) % chips, piece]
            if after:
                value = tied(value, *after)
            if met[0] is not None:
                value = met[side].astype(jnp.float32) + value.astype(jnp.float32)
                value = value.astype(jnp.bfloat16)
            with jax.named_scope(f"back_{'lead' if lead else 'trail'}{distance}"):
                moving[side, piece] = lax.ppermute(value, "seq", hops[side])

    send(far, True, both(worked[far - 1]))
    send(far - 1, False, *[came[side, far, side] for side in sides])
    for distance in range(far - 1, 0, -1):
        leads = [moving[side, side] for side in sides]
        send(distance, True)
        if distance > 1:
            latest = apply(distance - 1, (False,), latest, *leads)
            send(distance - 1, False, leads[0])
    final = []
    for piece in sides:
        total = given[0, piece].astype(jnp.float32)
        for side in sides:
            total += moving[side, piece].astype(jnp.float32)
        final.append(total)
    return (residual.astype(jnp.float32) + jnp.concatenate(final, axis=0)).astype(jnp.bfloat16)


def dispatched_experts(
    residual, normed, expert_ids, route_weights, gate_weight, up_weight, down_weight
):
    tokens_here = normed.shape[0]
    resid_f = residual.astype(jnp.float32)
    expert_count = EXP_DEV * lax.axis_size("seq")
    capacity = max(2, 3 * tokens_here * TOP // (2 * expert_count))
    flat_ids = expert_ids.reshape(-1)
    onehot = (flat_ids[:, None] == jnp.arange(expert_count, dtype=jnp.int32)[None, :]).astype(
        jnp.int32
    )
    earlier_count = jnp.cumsum(onehot, axis=0) - onehot
    slot_index = jnp.sum(earlier_count * onehot, axis=1)
    cell_index = (flat_ids * capacity + slot_index).reshape(tokens_here, TOP)
    chooser = jnp.any(
        cell_index[None, :, :]
        == jnp.arange(expert_count * capacity, dtype=jnp.int32)[:, None, None],
        axis=2,
    ).astype(jnp.bfloat16)
    outgoing = mm(chooser, normed).astype(jnp.bfloat16)
    outgoing = outgoing.reshape(expert_count, capacity, normed.shape[1])
    paired = lax.all_gather(outgoing, "rep", axis=1, tiled=True)
    arrived = lax.all_to_all(paired, "seq", split_axis=0, concat_axis=1, tiled=True)[0]
    gate_pre = mm(arrived, gate_weight)
    up_pre = mm(arrived, up_weight)
    activated = (gate_pre * jax.nn.sigmoid(1.702 * gate_pre) * (up_pre + 1.0)).astype(jnp.bfloat16)
    returned = lax.all_to_all(
        mm(activated, down_weight).astype(jnp.bfloat16)[None],
        "seq",
        split_axis=1,
        concat_axis=0,
        tiled=True,
    )
    expert_out = lax.psum_scatter(returned, "rep", scatter_dimension=1, tiled=True)
    picked = expert_out.reshape(expert_count * capacity, -1)[cell_index.reshape(-1)]
    picked = picked.reshape(tokens_here, TOP, -1)
    expert_sum = jnp.sum(route_weights[:, :, None] * picked.astype(jnp.float32), axis=1)
    return (resid_f + expert_sum).astype(jnp.bfloat16)


def per_device(
    stream,
    queries,
    key_rows,
    value_rows,
    sink_logits,
    out_weight,
    norm_gain,
    expert_ids,
    route_weights,
    gate_weight,
    up_weight,
    down_weight,
):
    block_len = queries.shape[0]
    seq = lax.axis_index("seq")
    rank = lax.axis_index("rep").astype(jnp.int32).reshape(1)
    gate_weight, up_weight, down_weight = gate_weight[0], up_weight[0], down_weight[0]
    use_ring = EXP_DEV * lax.axis_size("seq") <= 2 * TOP

    before = shifted(key_rows, "seq", 1), shifted(value_rows, "seq", 1)
    others = []
    if use_ring:
        others = [swapped(w, "rep") for w in (gate_weight, up_weight, down_weight)]
    first = (seq == 0).astype(jnp.int32).reshape(1)
    *operands, later_half = attend(
        sink_logits.reshape(1, -1), queries, key_rows, value_rows, out_weight
    )
    send, own = attend(*operands, (first, *before, rank, later_half))
    came = swapped(send, "rep")
    expert_count = lax.axis_size("seq") * EXP_DEV if use_ring else 0
    residual, *pieces = norm(
        stream, own, came, norm_gain, expert_ids, route_weights, expert_count
    )
    if use_ring:
        *pieces, _ = lax.optimization_barrier((*pieces, others))
        return ring_experts(residual, pieces, gate_weight, up_weight, down_weight, others)
    return dispatched_experts(
        residual,
        pieces[0],
        expert_ids,
        route_weights,
        gate_weight,
        up_weight,
        down_weight,
    )


def solution(mesh):
    return jax.shard_map(
        per_device,
        mesh=mesh,
        in_specs=(
            P(("groups", "seq", "rep"), None),
            P(("groups", "seq"), "rep"),
            P(("groups", "seq"), "rep"),
            P(("groups", "seq"), "rep"),
            P("rep"),
            P("rep", None),
            P(),
            P(("groups", "seq", "rep"), None),
            P(("groups", "seq", "rep"), None),
            P("seq", None, "rep"),
            P("seq", None, "rep"),
            P("seq", "rep", None),
        ),
        out_specs=P(("groups", "seq", "rep"), None),
        check_vma=False,
    )
```

```python
import functools
import math

import jax
import jax.numpy as jnp
from jax import lax
from jax.experimental import pallas as pl
from jax.experimental.pallas import tpu as pltpu
from jax.sharding import PartitionSpec as P

HEAD_DIM = 64
WINDOW = 128
TOP = 4
TAIL = 16
EXP_DEV = 1
LANES = 128
SNAKES = {8: (0, 2, 4, 6, 7, 5, 3, 1)}
MIB = 1 << 20
EXPERT_VMEM = 8 * MIB


def shifted(value, axis, by):
    peers = lax.axis_size(axis)
    return lax.ppermute(value, axis, [(i, (i + by) % peers) for i in range(peers)])


def pinned(values, space):
    return [pltpu.with_memory_space_constraint(value, space) for value in values]


def tied(value, *after):
    return lax.optimization_barrier((value,) + after)[0]


def swapped(value, axis, bit=1):
    peers = lax.axis_size(axis)
    return lax.ppermute(value, axis, [(i, i ^ bit) for i in range(peers)])


def mm(a, b):
    return jnp.dot(a, b, preferred_element_type=jnp.float32)


def attend_kernel(mix, *refs):
    if mix:
        sink_ref, q_ref, k_ref, v_ref, ow_ref = refs[:5]
        first_ref, k_before, v_before, rank_ref, later_ref, send_ref, own_ref, done_ref = refs[5:]
        rows = later_ref.shape[0]
        queries = slice(0, rows)
        k = jnp.concatenate([k_before[rows:], k_ref[:rows]], axis=0)
        v = jnp.concatenate([v_before[rows:], v_ref[:rows]], axis=0)
        done_ref[rows:] = later_ref[...]
        copies = []
    else:
        sink_ref, q_ref, k_ref, v_ref, ow_ref, done_ref = refs[5:11]
        rows = done_ref.shape[0]
        queries = slice(rows, 2 * rows)
        sems = refs[-1]
        early, late = pl.ds(0, rows), pl.ds(rows, rows)
        sources = [(refs[2], k_ref), (refs[3], v_ref), (refs[1].at[late], q_ref.at[late])]
        sources += [(refs[0], sink_ref), (refs[4], ow_ref), (refs[1].at[early], q_ref.at[early])]
        copies = [
            pltpu.make_async_copy(here, there, sems.at[index])
            for index, (here, there) in enumerate(sources)
        ]
        for copy in copies:
            copy.start()
        for copy in copies[:4]:
            copy.wait()
        k, v = k_ref[...], v_ref[...]
    keys = 2 * rows
    pairs = q_ref.shape[1] // LANES
    groups = k_ref.shape[1] // HEAD_DIM

    low = lax.broadcasted_iota(jnp.int32, (keys, LANES), 1) < HEAD_DIM
    k = k.astype(jnp.float32) * (1.0 / math.sqrt(HEAD_DIM))
    v = v.astype(jnp.float32)
    k_turned, v_turned = pltpu.roll(k, HEAD_DIM, 1), pltpu.roll(v, HEAD_DIM, 1)
    key = lax.broadcasted_iota(jnp.int32, (keys, rows), 0)
    query = lax.broadcasted_iota(jnp.int32, (keys, rows), 1)
    allowed = (key <= query + rows) & (key > query)
    if mix:
        allowed = allowed & (key >= jnp.where(first_ref[0] == 1, rows, 0))
    ones = jnp.ones((8, keys), jnp.float32)
    zeros = jnp.zeros((8, keys), jnp.float32)

    for group in range(groups):
        here, there = (k, v), (k_turned, v_turned)
        lows, highs = (here, there) if group == 0 else (there, here)
        kk = jnp.concatenate(
            [jnp.where(low, lows[0], 0.0), jnp.where(low, 0.0, highs[0])], axis=0
        ).astype(jnp.bfloat16)
        v_low = jnp.where(low, lows[1], 0.0).T
        v_high = jnp.where(low, 0.0, highs[1]).T
        vv = jnp.concatenate(
            [
                jnp.concatenate([v_low, v_high], axis=1),
                jnp.concatenate([ones, zeros], axis=1),
                jnp.concatenate([zeros, ones], axis=1),
            ],
            axis=0,
        ).astype(jnp.bfloat16)
        for pair in range(group * pairs // groups, (group + 1) * pairs // groups):
            lanes = slice(pair * LANES, (pair + 1) * LANES)
            scores = lax.dot_general(
                kk, q_ref[queries, lanes], (((1,), (1,)), ((), ())), preferred_element_type=jnp.float32
            )
            weights, sinks = [], []
            for side in range(2):
                part = jnp.where(allowed, scores[side * keys : (side + 1) * keys], -jnp.inf)
                sink = sink_ref[:, 2 * pair + side : 2 * pair + side + 1]
                highest = jnp.maximum(jnp.max(part, axis=0, keepdims=True), sink)
                weights.append(jnp.exp(part - highest).astype(jnp.bfloat16))
                sinks.append(jnp.exp(sink - highest))
            both = mm(vv, jnp.concatenate(weights, axis=0))
            parts = [
                both[side * HEAD_DIM : (side + 1) * HEAD_DIM]
                / (both[LANES + 8 * side : LANES + 8 * side + 1] + sinks[side])
                for side in range(2)
            ]
            done_ref[:rows, lanes] = jnp.concatenate(parts, axis=0).T.astype(jnp.bfloat16)

    for copy in copies[4:]:
        copy.wait()
    if not mix:
        return
    model = ow_ref.shape[1]
    width = 512 if model % 512 == 0 else model
    own_first = rank_ref[0] == 0
    for start in range(0, model, width):
        lanes = slice(start, start + width)
        both = mm(done_ref[...], ow_ref[:, lanes])
        early, late = both[:rows], both[rows:]
        own_ref[:, lanes] = jnp.where(own_first, early, late)
        send_ref[:, lanes] = jnp.where(own_first, late, early).astype(jnp.bfloat16)


def attend(sinks, queries, keys, values, out_weight, mixed=()):
    mix = bool(mixed)
    rows, width, model = WINDOW, queries.shape[1], out_weight.shape[1]
    smem = pl.BlockSpec(memory_space=pltpu.SMEM)
    vmem = pl.BlockSpec(memory_space=pltpu.VMEM)
    hbm = pl.BlockSpec(memory_space=pltpu.HBM)
    operands = (sinks, queries, keys, values, out_weight)
    wide = jax.ShapeDtypeStruct((rows, model), jnp.float32)
    narrow = jax.ShapeDtypeStruct((rows, model), jnp.bfloat16)
    shapes = (narrow, wide)
    if not mix:
        shapes = tuple(jax.ShapeDtypeStruct(a.shape, a.dtype) for a in operands)
        shapes += (jax.ShapeDtypeStruct((rows, width), jnp.bfloat16),)
    return pl.pallas_call(
        functools.partial(attend_kernel, mix),
        in_specs=[vmem if mix else hbm] * 5 + ([smem, vmem, vmem, smem, vmem] if mix else []),
        out_specs=(vmem,) * len(shapes),
        out_shape=shapes,
        scratch_shapes=[
            pltpu.VMEM((2 * rows, width), jnp.bfloat16) if mix else pltpu.SemaphoreType.DMA((6,))
        ],
        compiler_params=pltpu.CompilerParams(vmem_limit_bytes=8 * MIB),
        cost_estimate=pl.CostEstimate(
            flops=2 * rows * width * (model + 1024), bytes_accessed=6 * MIB, transcendentals=0
        ),
        name="attend",
    )(*pinned(operands, pltpu.VMEM if mix else pltpu.HBM), *mixed)


def norm_kernel(
    expert_count, stream_ref, own_ref, came_ref, gain_ref, ids_ref, route_ref, *rest
):
    residual_ref, *message_refs = rest
    rows, model = stream_ref.shape
    residual = (
        stream_ref[...].astype(jnp.float32) + own_ref[...] + came_ref[...].astype(jnp.float32)
    ).astype(jnp.bfloat16)
    residual_ref[...] = residual
    wide = residual.astype(jnp.float32)
    mean = jnp.mean(wide * wide, axis=-1, keepdims=True)
    normed = (wide * lax.rsqrt(mean + 1e-05) * gain_ref[...]).astype(jnp.bfloat16)
    if not expert_count:
        message_refs[0][...] = normed
        return
    size = rows // len(message_refs)
    expert = lax.broadcasted_iota(jnp.int32, (TAIL, rows), 0)
    dense = jnp.zeros((TAIL, rows), jnp.float32)
    for k in range(TOP):
        dense += jnp.where(expert == ids_ref[k : k + 1, :], route_ref[k : k + 1, :], 0.0)
    lead = dense.astype(jnp.bfloat16).astype(jnp.float32)
    rest = dense - lead
    for index, ref in enumerate(message_refs):
        for block in range(model // LANES):
            ref[block * size : (block + 1) * size] = normed[
                index * size : (index + 1) * size, block * LANES : (block + 1) * LANES
            ]
        span = slice(index * size, (index + 1) * size)
        both = jnp.concatenate([lead[:, span], rest[:, span]], axis=1)
        ref[model // LANES * size :] = both.astype(jnp.bfloat16)


def norm(stream, own, came, gain, expert_ids, route_weights, expert_count):
    rows, model = stream.shape
    vmem = pl.BlockSpec(memory_space=pltpu.VMEM)
    pieces, shape = 1, (rows, model)
    if expert_count:
        pieces = 2
        shape = (rows // pieces * (model // LANES) + TAIL, LANES)
    return pl.pallas_call(
        functools.partial(norm_kernel, expert_count),
        in_specs=[vmem] * 6,
        out_shape=[jax.ShapeDtypeStruct((rows, model), jnp.bfloat16)]
        + [jax.ShapeDtypeStruct(shape, jnp.bfloat16)] * pieces,
        compiler_params=pltpu.CompilerParams(vmem_limit_bytes=8 * MIB),
        cost_estimate=pl.CostEstimate(
            flops=8 * rows * model, bytes_accessed=14 * rows * model, transcendentals=rows
        ),
        name="norm",
    )(stream, own, came, gain.reshape(1, model), expert_ids.T, route_weights.T)


def expert_kernel(tile, count, load, me_ref, *refs):
    x_refs, halves = refs[:count], refs[count : count + 6]
    out_refs, rest = refs[count + 6 : 2 * count + 6], refs[2 * count + 6 :]
    copies = []
    if load:
        kept, rest = rest[:3], rest[3:]
        copies = [
            pltpu.make_async_copy(here, there, rest[2].at[index])
            for index, (here, there) in enumerate(zip(halves[3:], kept))
        ]
        for copy in copies:
            copy.start()
        halves = halves[:3] + kept
    x, hidden = rest[:2]
    model, half = halves[0].shape
    rows = x.shape[0] // count
    body = rows * (model // LANES)
    for index, ref in enumerate(x_refs):
        for block in range(model // LANES):
            x[index * rows : (index + 1) * rows, block * LANES : (block + 1) * LANES] = ref[
                block * rows : (block + 1) * rows
            ]

    def arrived(*which):
        for index in which:
            if copies:
                copies[index].wait()

    def work(side, at):
        gate_ref, up_ref = halves[3 * side : 3 * side + 2]
        gate_pre = mm(x[...], gate_ref[:, at : at + tile])
        up_pre = mm(x[...], up_ref[:, at : at + tile])
        activated = gate_pre * jax.nn.sigmoid(1.702 * gate_pre) * (up_pre + 1.0)
        hidden[:, side * half + at : side * half + at + tile] = activated.astype(jnp.bfloat16)

    for side in range(2):
        if side == 1:
            arrived(0, 1)
        for at in range(0, half, tile):
            work(side, at)
    arrived(2)

    me = me_ref[0]
    scales = []
    for ref in x_refs:
        sent = ref[body:].astype(jnp.float32)
        expert = lax.broadcasted_iota(jnp.int32, sent.shape, 0)
        mine = jnp.sum(jnp.where(expert == me, sent, 0.0), axis=0, keepdims=True)
        mine = jnp.broadcast_to(mine, (8, LANES))
        scales.append((mine + pltpu.roll(mine, LANES - rows, 1)).T[:rows, :1])
    for at in range(0, model, tile):
        lanes = slice(at, at + tile)
        total = mm(hidden[:, :half], halves[2][:, lanes]) + mm(hidden[:, half:], halves[5][:, lanes])
        for index, (ref, scale) in enumerate(zip(out_refs, scales)):
            ref[:, lanes] = (total[index * rows : (index + 1) * rows] * scale).astype(jnp.bfloat16)


def experts(blocks, me, halves, load=False):
    model, half = halves[0].shape
    size = (blocks[0].shape[0] - TAIL) // (model // LANES)
    rows = size * len(blocks)
    vmem = pl.BlockSpec(memory_space=pltpu.VMEM)
    hbm = pl.BlockSpec(memory_space=pltpu.HBM)
    kept = [jax.ShapeDtypeStruct(w.shape, w.dtype) for w in halves[3:]] if load else []
    scratch = [
        pltpu.VMEM((rows, model), jnp.bfloat16),
        pltpu.VMEM((rows, 2 * half), jnp.bfloat16),
    ]
    return pl.pallas_call(
        functools.partial(expert_kernel, min(256, half), len(blocks), load),
        in_specs=[pl.BlockSpec(memory_space=pltpu.SMEM)]
        + [vmem] * len(blocks)
        + [vmem] * 3
        + [hbm if load else vmem] * 3,
        out_specs=[vmem] * (len(blocks) + len(kept)),
        out_shape=[jax.ShapeDtypeStruct((size, model), jnp.bfloat16)] * len(blocks) + kept,
        scratch_shapes=scratch + ([pltpu.SemaphoreType.DMA((3,))] if load else []),
        compiler_params=pltpu.CompilerParams(vmem_limit_bytes=EXPERT_VMEM),
        cost_estimate=pl.CostEstimate(
            flops=12 * rows * model * half, bytes_accessed=6 * rows * model, transcendentals=0
        ),
        name="experts",
    )(
        me,
        *blocks,
        *pinned(halves[:3], pltpu.VMEM),
        *pinned(halves[3:], pltpu.HBM if load else pltpu.VMEM),
    )


def ring_experts(residual, pieces, gate_weight, up_weight, down_weight, others):
    chips = lax.axis_size("seq")
    ring = SNAKES.get(chips, tuple(range(chips)))
    far = chips // 2
    ahead = [(ring[i], ring[(i + 1) % chips]) for i in range(chips)]
    hops = (ahead, [(to, of) for of, to in ahead])
    sides = (0, 1)
    me = lax.axis_index("seq").astype(jnp.int32).reshape(1)
    given = {}

    def keep(keys, outs):
        for (side, distance, piece), out in zip(keys, outs):
            given[(distance if side == 0 else -distance) % chips, piece] = out

    halves = (gate_weight, up_weight, down_weight) + tuple(others)
    outs = experts(pieces, me, halves, load=True)
    halves = halves[:3] + tuple(outs[2:])
    keep([(0, 0, 0), (0, 0, 1)], outs)
    worked = {0: outs[0]}
    came = {(side, 0, piece): pieces[piece] for side in sides for piece in sides}

    def bring(distance, lead, *after):
        keys = [(side, distance - 1, side if lead else 1 - side) for side in sides]
        met = lax.optimization_barrier(tuple(came[key] for key in keys))
        for (side, _, piece), block in zip(keys, met):
            block = tied(block, *after)
            with jax.named_scope(f"out_{'lead' if lead else 'trail'}{distance}"):
                came[side, distance, piece] = lax.ppermute(block, "seq", hops[side])

    def apply(distance, kinds, *after):
        keys = [(side, distance, side if lead else 1 - side) for lead in kinds for side in sides]
        blocks = [came[key] for key in keys]
        if after:
            blocks[0] = tied(blocks[0], *after)
        with jax.named_scope(f"hop{distance}"):
            outs = experts(blocks, me, halves)
        worked.setdefault(distance, outs[0])
        keep(keys, outs)
        return outs[0]

    for distance in range(1, far + 1):
        bring(distance, True, *([worked[distance - 2]] if distance > 1 else []))
        trails = []
        if distance < far:
            before = [came[side, distance - 1, side] for side in sides] if distance > 1 else []
            bring(distance, False, *before)
            if 1 < distance < far - 1:
                trails = [came[side, distance, 1 - side] for side in sides]
        latest = apply(distance, (True,), worked[distance - 1], *trails)
    latest = apply(far - 1, (False,), latest)

    moving = {}

    def send(distance, lead, *after):
        met = [moving.get((side, side if lead else 1 - side)) for side in sides]
        if met[0] is not None:
            met = list(lax.optimization_barrier(tuple(met)))
        for side in sides:
            piece = side if lead else 1 - side
            value = given[(-distance if side == 0 else distance) % chips, piece]
            if after:
                value = tied(value, *after)
            if met[0] is not None:
                value = met[side].astype(jnp.float32) + value.astype(jnp.float32)
                value = value.astype(jnp.bfloat16)
            with jax.named_scope(f"back_{'lead' if lead else 'trail'}{distance}"):
                moving[side, piece] = lax.ppermute(value, "seq", hops[side])

    send(far, True)
    send(far - 1, False, *[came[side, far, side] for side in sides])
    for distance in range(far - 1, 0, -1):
        leads = [moving[side, side] for side in sides]
        send(distance, True)
        if distance > 1:
            latest = apply(distance - 1, (False,), latest, *leads)
            send(distance - 1, False, leads[0])
    final = []
    for piece in sides:
        total = given[0, piece].astype(jnp.float32)
        for side in sides:
            total += moving[side, piece].astype(jnp.float32)
        final.append(total)
    return (residual.astype(jnp.float32) + jnp.concatenate(final, axis=0)).astype(jnp.bfloat16)


def dispatched_experts(
    residual, normed, expert_ids, route_weights, gate_weight, up_weight, down_weight
):
    tokens_here = normed.shape[0]
    resid_f = residual.astype(jnp.float32)
    expert_count = EXP_DEV * lax.axis_size("seq")
    capacity = max(2, 3 * tokens_here * TOP // (2 * expert_count))
    flat_ids = expert_ids.reshape(-1)
    onehot = (flat_ids[:, None] == jnp.arange(expert_count, dtype=jnp.int32)[None, :]).astype(
        jnp.int32
    )
    earlier_count = jnp.cumsum(onehot, axis=0) - onehot
    slot_index = jnp.sum(earlier_count * onehot, axis=1)
    cell_index = (flat_ids * capacity + slot_index).reshape(tokens_here, TOP)
    chooser = jnp.any(
        cell_index[None, :, :]
        == jnp.arange(expert_count * capacity, dtype=jnp.int32)[:, None, None],
        axis=2,
    ).astype(jnp.bfloat16)
    outgoing = mm(chooser, normed).astype(jnp.bfloat16)
    outgoing = outgoing.reshape(expert_count, capacity, normed.shape[1])
    paired = lax.all_gather(outgoing, "rep", axis=1, tiled=True)
    arrived = lax.all_to_all(paired, "seq", split_axis=0, concat_axis=1, tiled=True)[0]
    gate_pre = mm(arrived, gate_weight)
    up_pre = mm(arrived, up_weight)
    activated = (gate_pre * jax.nn.sigmoid(1.702 * gate_pre) * (up_pre + 1.0)).astype(jnp.bfloat16)
    returned = lax.all_to_all(
        mm(activated, down_weight).astype(jnp.bfloat16)[None],
        "seq",
        split_axis=1,
        concat_axis=0,
        tiled=True,
    )
    expert_out = lax.psum_scatter(returned, "rep", scatter_dimension=1, tiled=True)
    picked = expert_out.reshape(expert_count * capacity, -1)[cell_index.reshape(-1)]
    picked = picked.reshape(tokens_here, TOP, -1)
    expert_sum = jnp.sum(route_weights[:, :, None] * picked.astype(jnp.float32), axis=1)
    return (resid_f + expert_sum).astype(jnp.bfloat16)


def per_device(
    stream,
    queries,
    key_rows,
    value_rows,
    sink_logits,
    out_weight,
    norm_gain,
    expert_ids,
    route_weights,
    gate_weight,
    up_weight,
    down_weight,
):
    block_len = queries.shape[0]
    seq = lax.axis_index("seq")
    rank = lax.axis_index("rep").astype(jnp.int32).reshape(1)
    gate_weight, up_weight, down_weight = gate_weight[0], up_weight[0], down_weight[0]
    use_ring = EXP_DEV * lax.axis_size("seq") <= 2 * TOP

    before = shifted(key_rows, "seq", 1), shifted(value_rows, "seq", 1)
    others = []
    if use_ring:
        others = [swapped(w, "rep") for w in (gate_weight, up_weight, down_weight)]
    first = (seq == 0).astype(jnp.int32).reshape(1)
    *operands, later_half = attend(
        sink_logits.reshape(1, -1), queries, key_rows, value_rows, out_weight
    )
    send, own = attend(*operands, (first, *before, rank, later_half))
    came = swapped(send, "rep")
    expert_count = lax.axis_size("seq") * EXP_DEV if use_ring else 0
    residual, *pieces = norm(
        stream, own, came, norm_gain, expert_ids, route_weights, expert_count
    )
    if use_ring:
        *pieces, _ = lax.optimization_barrier((*pieces, others))
        return ring_experts(residual, pieces, gate_weight, up_weight, down_weight, others)
    return dispatched_experts(
        residual,
        pieces[0],
        expert_ids,
        route_weights,
        gate_weight,
        up_weight,
        down_weight,
    )


def solution(mesh):
    return jax.shard_map(
        per_device,
        mesh=mesh,
        in_specs=(
            P(("groups", "seq", "rep"), None),
            P(("groups", "seq"), "rep"),
            P(("groups", "seq"), "rep"),
            P(("groups", "seq"), "rep"),
            P("rep"),
            P("rep", None),
            P(),
            P(("groups", "seq", "rep"), None),
            P(("groups", "seq", "rep"), None),
            P("seq", None, "rep"),
            P("seq", None, "rep"),
            P("seq", "rep", None),
        ),
        out_specs=P(("groups", "seq", "rep"), None),
        check_vma=False,
    )
```

```python
import functools
import math

import jax
import jax.numpy as jnp
from jax import lax
from jax.experimental import pallas as pl
from jax.experimental.pallas import tpu as pltpu
from jax.sharding import PartitionSpec as P

HEAD_DIM = 64
WINDOW = 128
TOP = 4
TAIL = 16
EXP_DEV = 1
LANES = 128
SNAKES = {8: (0, 2, 4, 6, 7, 5, 3, 1)}
MIB = 1 << 20
EXPERT_VMEM = 8 * MIB


def shifted(value, axis, by):
    peers = lax.axis_size(axis)
    return lax.ppermute(value, axis, [(i, (i + by) % peers) for i in range(peers)])


def pinned(values, space):
    return [pltpu.with_memory_space_constraint(value, space) for value in values]


def tied(value, *after):
    return lax.optimization_barrier((value,) + after)[0]


def swapped(value, axis, bit=1):
    peers = lax.axis_size(axis)
    return lax.ppermute(value, axis, [(i, i ^ bit) for i in range(peers)])


def mm(a, b):
    return jnp.dot(a, b, preferred_element_type=jnp.float32)


def attend_kernel(mix, *refs):
    if mix:
        sink_ref, q_ref, k_ref, v_ref, ow_ref = refs[:5]
        first_ref, k_before, v_before, rank_ref, later_ref, send_ref, own_ref, done_ref = refs[5:]
        rows = later_ref.shape[0]
        queries = slice(0, rows)
        k = jnp.concatenate([k_before[rows:], k_ref[:rows]], axis=0)
        v = jnp.concatenate([v_before[rows:], v_ref[:rows]], axis=0)
        done_ref[rows:] = later_ref[...]
        copies = []
    else:
        sink_ref, q_ref, k_ref, v_ref, ow_ref, done_ref = refs[5:11]
        rows = done_ref.shape[0]
        queries = slice(rows, 2 * rows)
        sems = refs[-1]
        early, late = pl.ds(0, rows), pl.ds(rows, rows)
        sources = [(refs[2], k_ref), (refs[3], v_ref), (refs[1].at[late], q_ref.at[late])]
        sources += [(refs[0], sink_ref), (refs[4], ow_ref), (refs[1].at[early], q_ref.at[early])]
        copies = [
            pltpu.make_async_copy(here, there, sems.at[index])
            for index, (here, there) in enumerate(sources)
        ]
        for copy in copies:
            copy.start()
        for copy in copies[:4]:
            copy.wait()
        k, v = k_ref[...], v_ref[...]
    keys = 2 * rows
    pairs = q_ref.shape[1] // LANES
    groups = k_ref.shape[1] // HEAD_DIM

    low = lax.broadcasted_iota(jnp.int32, (keys, LANES), 1) < HEAD_DIM
    k = k.astype(jnp.float32) * (1.0 / math.sqrt(HEAD_DIM))
    v = v.astype(jnp.float32)
    k_turned, v_turned = pltpu.roll(k, HEAD_DIM, 1), pltpu.roll(v, HEAD_DIM, 1)
    key = lax.broadcasted_iota(jnp.int32, (keys, rows), 0)
    query = lax.broadcasted_iota(jnp.int32, (keys, rows), 1)
    allowed = (key <= query + rows) & (key > query)
    if mix:
        allowed = allowed & (key >= jnp.where(first_ref[0] == 1, rows, 0))
    ones = jnp.ones((8, keys), jnp.float32)
    zeros = jnp.zeros((8, keys), jnp.float32)

    for group in range(groups):
        here, there = (k, v), (k_turned, v_turned)
        lows, highs = (here, there) if group == 0 else (there, here)
        kk = jnp.concatenate(
            [jnp.where(low, lows[0], 0.0), jnp.where(low, 0.0, highs[0])], axis=0
        ).astype(jnp.bfloat16)
        v_low = jnp.where(low, lows[1], 0.0).T
        v_high = jnp.where(low, 0.0, highs[1]).T
        vv = jnp.concatenate(
            [
                jnp.concatenate([v_low, v_high], axis=1),
                jnp.concatenate([ones, zeros], axis=1),
                jnp.concatenate([zeros, ones], axis=1),
            ],
            axis=0,
        ).astype(jnp.bfloat16)
        for pair in range(group * pairs // groups, (group + 1) * pairs // groups):
            lanes = slice(pair * LANES, (pair + 1) * LANES)
            scores = lax.dot_general(
                kk, q_ref[queries, lanes], (((1,), (1,)), ((), ())), preferred_element_type=jnp.float32
            )
            weights, sinks = [], []
            for side in range(2):
                part = jnp.where(allowed, scores[side * keys : (side + 1) * keys], -jnp.inf)
                sink = sink_ref[:, 2 * pair + side : 2 * pair + side + 1]
                highest = jnp.maximum(jnp.max(part, axis=0, keepdims=True), sink)
                weights.append(jnp.exp(part - highest).astype(jnp.bfloat16))
                sinks.append(jnp.exp(sink - highest))
            both = mm(vv, jnp.concatenate(weights, axis=0))
            parts = [
                both[side * HEAD_DIM : (side + 1) * HEAD_DIM]
                / (both[LANES + 8 * side : LANES + 8 * side + 1] + sinks[side])
                for side in range(2)
            ]
            done_ref[:rows, lanes] = jnp.concatenate(parts, axis=0).T.astype(jnp.bfloat16)

    for copy in copies[4:]:
        copy.wait()
    if not mix:
        return
    model = ow_ref.shape[1]
    width = 512 if model % 512 == 0 else model
    own_first = rank_ref[0] == 0
    for start in range(0, model, width):
        lanes = slice(start, start + width)
        both = mm(done_ref[...], ow_ref[:, lanes])
        early, late = both[:rows], both[rows:]
        own_ref[:, lanes] = jnp.where(own_first, early, late)
        send_ref[:, lanes] = jnp.where(own_first, late, early).astype(jnp.bfloat16)


def attend(sinks, queries, keys, values, out_weight, mixed=()):
    mix = bool(mixed)
    rows, width, model = WINDOW, queries.shape[1], out_weight.shape[1]
    smem = pl.BlockSpec(memory_space=pltpu.SMEM)
    vmem = pl.BlockSpec(memory_space=pltpu.VMEM)
    hbm = pl.BlockSpec(memory_space=pltpu.HBM)
    operands = (sinks, queries, keys, values, out_weight)
    wide = jax.ShapeDtypeStruct((rows, model), jnp.float32)
    narrow = jax.ShapeDtypeStruct((rows, model), jnp.bfloat16)
    shapes = (narrow, wide)
    if not mix:
        shapes = tuple(jax.ShapeDtypeStruct(a.shape, a.dtype) for a in operands)
        shapes += (jax.ShapeDtypeStruct((rows, width), jnp.bfloat16),)
    return pl.pallas_call(
        functools.partial(attend_kernel, mix),
        in_specs=[vmem if mix else hbm] * 5 + ([smem, vmem, vmem, smem, vmem] if mix else []),
        out_specs=(vmem,) * len(shapes),
        out_shape=shapes,
        scratch_shapes=[
            pltpu.VMEM((2 * rows, width), jnp.bfloat16) if mix else pltpu.SemaphoreType.DMA((6,))
        ],
        compiler_params=pltpu.CompilerParams(vmem_limit_bytes=8 * MIB),
        cost_estimate=pl.CostEstimate(
            flops=2 * rows * width * (model + 1024), bytes_accessed=6 * MIB, transcendentals=0
        ),
        name="attend",
    )(*pinned(operands, pltpu.VMEM if mix else pltpu.HBM), *mixed)


def norm_kernel(
    expert_count, stream_ref, own_ref, came_ref, gain_ref, ids_ref, route_ref, *rest
):
    residual_ref, *message_refs = rest
    rows, model = stream_ref.shape
    residual = (
        stream_ref[...].astype(jnp.float32) + own_ref[...] + came_ref[...].astype(jnp.float32)
    ).astype(jnp.bfloat16)
    residual_ref[...] = residual
    wide = residual.astype(jnp.float32)
    mean = jnp.mean(wide * wide, axis=-1, keepdims=True)
    normed = (wide * lax.rsqrt(mean + 1e-05) * gain_ref[...]).astype(jnp.bfloat16)
    if not expert_count:
        message_refs[0][...] = normed
        return
    size = rows // len(message_refs)
    expert = lax.broadcasted_iota(jnp.int32, (TAIL, rows), 0)
    dense = jnp.zeros((TAIL, rows), jnp.float32)
    for k in range(TOP):
        dense += jnp.where(expert == ids_ref[k : k + 1, :], route_ref[k : k + 1, :], 0.0)
    lead = dense.astype(jnp.bfloat16).astype(jnp.float32)
    rest = dense - lead
    for index, ref in enumerate(message_refs):
        for block in range(model // LANES):
            ref[block * size : (block + 1) * size] = normed[
                index * size : (index + 1) * size, block * LANES : (block + 1) * LANES
            ]
        span = slice(index * size, (index + 1) * size)
        both = jnp.concatenate([lead[:, span], rest[:, span]], axis=1)
        ref[model // LANES * size :] = both.astype(jnp.bfloat16)


def norm(stream, own, came, gain, expert_ids, route_weights, expert_count):
    rows, model = stream.shape
    vmem = pl.BlockSpec(memory_space=pltpu.VMEM)
    pieces, shape = 1, (rows, model)
    if expert_count:
        pieces = 2
        shape = (rows // pieces * (model // LANES) + TAIL, LANES)
    return pl.pallas_call(
        functools.partial(norm_kernel, expert_count),
        in_specs=[vmem] * 6,
        out_shape=[jax.ShapeDtypeStruct((rows, model), jnp.bfloat16)]
        + [jax.ShapeDtypeStruct(shape, jnp.bfloat16)] * pieces,
        compiler_params=pltpu.CompilerParams(vmem_limit_bytes=8 * MIB),
        cost_estimate=pl.CostEstimate(
            flops=8 * rows * model, bytes_accessed=14 * rows * model, transcendentals=rows
        ),
        name="norm",
    )(stream, own, came, gain.reshape(1, model), expert_ids.T, route_weights.T)


def expert_kernel(tile, count, load, me_ref, *refs):
    x_refs, halves = refs[:count], refs[count : count + 6]
    out_refs, rest = refs[count + 6 : 2 * count + 6], refs[2 * count + 6 :]
    copies = []
    if load:
        kept, rest = rest[:3], rest[3:]
        copies = [
            pltpu.make_async_copy(here, there, rest[2].at[index])
            for index, (here, there) in enumerate(zip(halves[3:], kept))
        ]
        for copy in copies:
            copy.start()
        halves = halves[:3] + kept
    x, hidden = rest[:2]
    model, half = halves[0].shape
    rows = x.shape[0] // count
    body = rows * (model // LANES)
    for index, ref in enumerate(x_refs):
        for block in range(model // LANES):
            x[index * rows : (index + 1) * rows, block * LANES : (block + 1) * LANES] = ref[
                block * rows : (block + 1) * rows
            ]

    def arrived(*which):
        for index in which:
            if copies:
                copies[index].wait()

    def work(side, at):
        gate_ref, up_ref = halves[3 * side : 3 * side + 2]
        gate_pre = mm(x[...], gate_ref[:, at : at + tile])
        up_pre = mm(x[...], up_ref[:, at : at + tile])
        activated = gate_pre * jax.nn.sigmoid(1.702 * gate_pre) * (up_pre + 1.0)
        hidden[:, side * half + at : side * half + at + tile] = activated.astype(jnp.bfloat16)

    for side in range(2):
        if side == 1:
            arrived(0, 1)
        for at in range(0, half, tile):
            work(side, at)
    arrived(2)

    me = me_ref[0]
    scales = []
    for ref in x_refs:
        sent = ref[body:].astype(jnp.float32)
        expert = lax.broadcasted_iota(jnp.int32, sent.shape, 0)
        mine = jnp.sum(jnp.where(expert == me, sent, 0.0), axis=0, keepdims=True)
        mine = jnp.broadcast_to(mine, (8, LANES))
        scales.append((mine + pltpu.roll(mine, LANES - rows, 1)).T[:rows, :1])
    for at in range(0, model, tile):
        lanes = slice(at, at + tile)
        total = mm(hidden[:, :half], halves[2][:, lanes]) + mm(hidden[:, half:], halves[5][:, lanes])
        for index, (ref, scale) in enumerate(zip(out_refs, scales)):
            ref[:, lanes] = (total[index * rows : (index + 1) * rows] * scale).astype(jnp.bfloat16)


def experts(blocks, me, halves, load=False):
    model, half = halves[0].shape
    size = (blocks[0].shape[0] - TAIL) // (model // LANES)
    rows = size * len(blocks)
    vmem = pl.BlockSpec(memory_space=pltpu.VMEM)
    hbm = pl.BlockSpec(memory_space=pltpu.HBM)
    kept = [jax.ShapeDtypeStruct(w.shape, w.dtype) for w in halves[3:]] if load else []
    scratch = [
        pltpu.VMEM((rows, model), jnp.bfloat16),
        pltpu.VMEM((rows, 2 * half), jnp.bfloat16),
    ]
    return pl.pallas_call(
        functools.partial(expert_kernel, min(256, half), len(blocks), load),
        in_specs=[pl.BlockSpec(memory_space=pltpu.SMEM)]
        + [vmem] * len(blocks)
        + [vmem] * 3
        + [hbm if load else vmem] * 3,
        out_specs=[vmem] * (len(blocks) + len(kept)),
        out_shape=[jax.ShapeDtypeStruct((size, model), jnp.bfloat16)] * len(blocks) + kept,
        scratch_shapes=scratch + ([pltpu.SemaphoreType.DMA((3,))] if load else []),
        compiler_params=pltpu.CompilerParams(vmem_limit_bytes=EXPERT_VMEM),
        cost_estimate=pl.CostEstimate(
            flops=12 * rows * model * half, bytes_accessed=6 * rows * model, transcendentals=0
        ),
        name="experts",
    )(
        me,
        *blocks,
        *pinned(halves[:3], pltpu.VMEM),
        *pinned(halves[3:], pltpu.HBM if load else pltpu.VMEM),
    )


def ring_experts(residual, pieces, gate_weight, up_weight, down_weight, others):
    chips = lax.axis_size("seq")
    ring = SNAKES.get(chips, tuple(range(chips)))
    far = chips // 2
    ahead = [(ring[i], ring[(i + 1) % chips]) for i in range(chips)]
    hops = (ahead, [(to, of) for of, to in ahead])
    sides = (0, 1)
    me = lax.axis_index("seq").astype(jnp.int32).reshape(1)
    given = {}

    def keep(keys, outs):
        for (side, distance, piece), out in zip(keys, outs):
            given[(distance if side == 0 else -distance) % chips, piece] = out

    halves = (gate_weight, up_weight, down_weight) + tuple(others)
    outs = experts(pieces, me, halves, load=True)
    halves = halves[:3] + tuple(outs[2:])
    keep([(0, 0, 0), (0, 0, 1)], outs)
    worked = {0: outs[0]}
    came = {(side, 0, piece): pieces[piece] for side in sides for piece in sides}

    def bring(distance, lead, *after):
        keys = [(side, distance - 1, side if lead else 1 - side) for side in sides]
        met = lax.optimization_barrier(tuple(came[key] for key in keys))
        for (side, _, piece), block in zip(keys, met):
            block = tied(block, *after)
            with jax.named_scope(f"out_{'lead' if lead else 'trail'}{distance}"):
                came[side, distance, piece] = lax.ppermute(block, "seq", hops[side])

    def apply(distance, kinds, *after):
        keys = [(side, distance, side if lead else 1 - side) for lead in kinds for side in sides]
        blocks = [came[key] for key in keys]
        if after:
            blocks[0] = tied(blocks[0], *after)
        with jax.named_scope(f"hop{distance}"):
            outs = experts(blocks, me, halves)
        worked.setdefault(distance, outs[0])
        keep(keys, outs)
        return outs[0]

    for distance in range(1, far + 1):
        bring(distance, True, *([worked[distance - 2]] if distance > 1 else []))
        trails = []
        if distance < far:
            before = [came[side, distance - 1, side] for side in sides] if distance > 1 else []
            bring(distance, False, *before)
            if distance > 1:
                trails = [came[side, distance, 1 - side] for side in sides]
        latest = apply(distance, (True,), worked[distance - 1], *trails)
    latest = apply(far - 1, (False,), latest)

    moving = {}

    def send(distance, lead, *after):
        met = [moving.get((side, side if lead else 1 - side)) for side in sides]
        if met[0] is not None:
            met = list(lax.optimization_barrier(tuple(met)))
        for side in sides:
            piece = side if lead else 1 - side
            value = given[(-distance if side == 0 else distance) % chips, piece]
            if after:
                value = tied(value, *after)
            if met[0] is not None:
                value = met[side].astype(jnp.float32) + value.astype(jnp.float32)
                value = value.astype(jnp.bfloat16)
            with jax.named_scope(f"back_{'lead' if lead else 'trail'}{distance}"):
                moving[side, piece] = lax.ppermute(value, "seq", hops[side])

    send(far - 1, False)
    send(far, True)
    for distance in range(far - 1, 0, -1):
        leads = [moving[side, side] for side in sides]
        send(distance, True)
        if distance > 1:
            latest = apply(distance - 1, (False,), latest, *leads)
            send(distance - 1, False, leads[0])
    final = []
    for piece in sides:
        total = given[0, piece].astype(jnp.float32)
        for side in sides:
            total += moving[side, piece].astype(jnp.float32)
        final.append(total)
    return (residual.astype(jnp.float32) + jnp.concatenate(final, axis=0)).astype(jnp.bfloat16)


def dispatched_experts(
    residual, normed, expert_ids, route_weights, gate_weight, up_weight, down_weight
):
    tokens_here = normed.shape[0]
    resid_f = residual.astype(jnp.float32)
    expert_count = EXP_DEV * lax.axis_size("seq")
    capacity = max(2, 3 * tokens_here * TOP // (2 * expert_count))
    flat_ids = expert_ids.reshape(-1)
    onehot = (flat_ids[:, None] == jnp.arange(expert_count, dtype=jnp.int32)[None, :]).astype(
        jnp.int32
    )
    earlier_count = jnp.cumsum(onehot, axis=0) - onehot
    slot_index = jnp.sum(earlier_count * onehot, axis=1)
    cell_index = (flat_ids * capacity + slot_index).reshape(tokens_here, TOP)
    chooser = jnp.any(
        cell_index[None, :, :]
        == jnp.arange(expert_count * capacity, dtype=jnp.int32)[:, None, None],
        axis=2,
    ).astype(jnp.bfloat16)
    outgoing = mm(chooser, normed).astype(jnp.bfloat16)
    outgoing = outgoing.reshape(expert_count, capacity, normed.shape[1])
    paired = lax.all_gather(outgoing, "rep", axis=1, tiled=True)
    arrived = lax.all_to_all(paired, "seq", split_axis=0, concat_axis=1, tiled=True)[0]
    gate_pre = mm(arrived, gate_weight)
    up_pre = mm(arrived, up_weight)
    activated = (gate_pre * jax.nn.sigmoid(1.702 * gate_pre) * (up_pre + 1.0)).astype(jnp.bfloat16)
    returned = lax.all_to_all(
        mm(activated, down_weight).astype(jnp.bfloat16)[None],
        "seq",
        split_axis=1,
        concat_axis=0,
        tiled=True,
    )
    expert_out = lax.psum_scatter(returned, "rep", scatter_dimension=1, tiled=True)
    picked = expert_out.reshape(expert_count * capacity, -1)[cell_index.reshape(-1)]
    picked = picked.reshape(tokens_here, TOP, -1)
    expert_sum = jnp.sum(route_weights[:, :, None] * picked.astype(jnp.float32), axis=1)
    return (resid_f + expert_sum).astype(jnp.bfloat16)


def per_device(
    stream,
    queries,
    key_rows,
    value_rows,
    sink_logits,
    out_weight,
    norm_gain,
    expert_ids,
    route_weights,
    gate_weight,
    up_weight,
    down_weight,
):
    block_len = queries.shape[0]
    seq = lax.axis_index("seq")
    rank = lax.axis_index("rep").astype(jnp.int32).reshape(1)
    gate_weight, up_weight, down_weight = gate_weight[0], up_weight[0], down_weight[0]
    use_ring = EXP_DEV * lax.axis_size("seq") <= 2 * TOP

    before = shifted(key_rows, "seq", 1), shifted(value_rows, "seq", 1)
    others = []
    if use_ring:
        others = [swapped(w, "rep") for w in (gate_weight, up_weight, down_weight)]
    first = (seq == 0).astype(jnp.int32).reshape(1)
    *operands, later_half = attend(
        sink_logits.reshape(1, -1), queries, key_rows, value_rows, out_weight
    )
    send, own = attend(*operands, (first, *before, rank, later_half))
    came = swapped(send, "rep")
    expert_count = lax.axis_size("seq") * EXP_DEV if use_ring else 0
    residual, *pieces = norm(
        stream, own, came, norm_gain, expert_ids, route_weights, expert_count
    )
    if use_ring:
        *pieces, _ = lax.optimization_barrier((*pieces, others))
        return ring_experts(residual, pieces, gate_weight, up_weight, down_weight, others)
    return dispatched_experts(
        residual,
        pieces[0],
        expert_ids,
        route_weights,
        gate_weight,
        up_weight,
        down_weight,
    )


def solution(mesh):
    return jax.shard_map(
        per_device,
        mesh=mesh,
        in_specs=(
            P(("groups", "seq", "rep"), None),
            P(("groups", "seq"), "rep"),
            P(("groups", "seq"), "rep"),
            P(("groups", "seq"), "rep"),
            P("rep"),
            P("rep", None),
            P(),
            P(("groups", "seq", "rep"), None),
            P(("groups", "seq", "rep"), None),
            P("seq", None, "rep"),
            P("seq", None, "rep"),
            P("seq", "rep", None),
        ),
        out_specs=P(("groups", "seq", "rep"), None),
        check_vma=False,
    )
```

```python
import functools
import math

import jax
import jax.numpy as jnp
from jax import lax
from jax.experimental import pallas as pl
from jax.experimental.pallas import tpu as pltpu
from jax.sharding import PartitionSpec as P

HEAD_DIM = 64
WINDOW = 128
TOP = 4
TAIL = 16
EXP_DEV = 1
LANES = 128
SNAKES = {8: (0, 2, 4, 6, 7, 5, 3, 1)}
MIB = 1 << 20
EXPERT_VMEM = 8 * MIB


def shifted(value, axis, by):
    peers = lax.axis_size(axis)
    return lax.ppermute(value, axis, [(i, (i + by) % peers) for i in range(peers)])


def pinned(values, space):
    return [pltpu.with_memory_space_constraint(value, space) for value in values]


def tied(value, *after):
    return lax.optimization_barrier((value,) + after)[0]


def swapped(value, axis, bit=1):
    peers = lax.axis_size(axis)
    return lax.ppermute(value, axis, [(i, i ^ bit) for i in range(peers)])


def mm(a, b):
    return jnp.dot(a, b, preferred_element_type=jnp.float32)


def tail_kernel(keys_hbm, values_hbm, out_ref, sems):
    rows = out_ref.shape[0] // 2
    last = pl.ds(keys_hbm.shape[0] - rows, rows)
    copies = [
        pltpu.make_async_copy(ref.at[last], out_ref.at[pl.ds(index * rows, rows)], sems.at[index])
        for index, ref in enumerate((keys_hbm, values_hbm))
    ]
    for copy in copies:
        copy.start()
    for copy in copies:
        copy.wait()


def tail(keys, values):
    return pl.pallas_call(
        tail_kernel,
        in_specs=[pl.BlockSpec(memory_space=pltpu.HBM)] * 2,
        out_specs=pl.BlockSpec(memory_space=pltpu.VMEM),
        out_shape=jax.ShapeDtypeStruct((2 * WINDOW, keys.shape[1]), keys.dtype),
        scratch_shapes=[pltpu.SemaphoreType.DMA((2,))],
        name="tail",
    )(*pinned((keys, values), pltpu.HBM))


def attend_kernel(mix, *refs):
    if mix:
        sink_ref, q_ref, k_ref, v_ref, ow_ref = refs[:5]
        first_ref, before_ref, rank_ref, later_ref, send_ref, own_ref, done_ref = refs[5:]
        rows = later_ref.shape[0]
        queries = slice(0, rows)
        k = jnp.concatenate([before_ref[:rows], k_ref[:rows]], axis=0)
        v = jnp.concatenate([before_ref[rows:], v_ref[:rows]], axis=0)
        done_ref[rows:] = later_ref[...]
        copies = []
    else:
        sink_ref, q_ref, k_ref, v_ref, ow_ref, done_ref = refs[5:11]
        rows = done_ref.shape[0]
        queries = slice(rows, 2 * rows)
        sems = refs[-1]
        early, late = pl.ds(0, rows), pl.ds(rows, rows)
        sources = [(refs[2], k_ref), (refs[3], v_ref), (refs[1].at[late], q_ref.at[late])]
        sources += [(refs[0], sink_ref), (refs[4], ow_ref), (refs[1].at[early], q_ref.at[early])]
        copies = [
            pltpu.make_async_copy(here, there, sems.at[index])
            for index, (here, there) in enumerate(sources)
        ]
        for copy in copies:
            copy.start()
        for copy in copies[:4]:
            copy.wait()
        k, v = k_ref[...], v_ref[...]
    keys = 2 * rows
    pairs = q_ref.shape[1] // LANES
    groups = k_ref.shape[1] // HEAD_DIM

    low = lax.broadcasted_iota(jnp.int32, (keys, LANES), 1) < HEAD_DIM
    k = k.astype(jnp.float32) * (1.0 / math.sqrt(HEAD_DIM))
    v = v.astype(jnp.float32)
    k_turned, v_turned = pltpu.roll(k, HEAD_DIM, 1), pltpu.roll(v, HEAD_DIM, 1)
    key = lax.broadcasted_iota(jnp.int32, (keys, rows), 0)
    query = lax.broadcasted_iota(jnp.int32, (keys, rows), 1)
    allowed = (key <= query + rows) & (key > query)
    if mix:
        allowed = allowed & (key >= jnp.where(first_ref[0] == 1, rows, 0))
    ones = jnp.ones((8, keys), jnp.float32)
    zeros = jnp.zeros((8, keys), jnp.float32)

    for group in range(groups):
        here, there = (k, v), (k_turned, v_turned)
        lows, highs = (here, there) if group == 0 else (there, here)
        kk = jnp.concatenate(
            [jnp.where(low, lows[0], 0.0), jnp.where(low, 0.0, highs[0])], axis=0
        ).astype(jnp.bfloat16)
        v_low = jnp.where(low, lows[1], 0.0).T
        v_high = jnp.where(low, 0.0, highs[1]).T
        vv = jnp.concatenate(
            [
                jnp.concatenate([v_low, v_high], axis=1),
                jnp.concatenate([ones, zeros], axis=1),
                jnp.concatenate([zeros, ones], axis=1),
            ],
            axis=0,
        ).astype(jnp.bfloat16)
        for pair in range(group * pairs // groups, (group + 1) * pairs // groups):
            lanes = slice(pair * LANES, (pair + 1) * LANES)
            scores = lax.dot_general(
                kk, q_ref[queries, lanes], (((1,), (1,)), ((), ())), preferred_element_type=jnp.float32
            )
            weights, sinks = [], []
            for side in range(2):
                part = jnp.where(allowed, scores[side * keys : (side + 1) * keys], -jnp.inf)
                sink = sink_ref[:, 2 * pair + side : 2 * pair + side + 1]
                highest = jnp.maximum(jnp.max(part, axis=0, keepdims=True), sink)
                weights.append(jnp.exp(part - highest).astype(jnp.bfloat16))
                sinks.append(jnp.exp(sink - highest))
            both = mm(vv, jnp.concatenate(weights, axis=0))
            parts = [
                both[side * HEAD_DIM : (side + 1) * HEAD_DIM]
                / (both[LANES + 8 * side : LANES + 8 * side + 1] + sinks[side])
                for side in range(2)
            ]
            done_ref[:rows, lanes] = jnp.concatenate(parts, axis=0).T.astype(jnp.bfloat16)

    for copy in copies[4:]:
        copy.wait()
    if not mix:
        return
    model = ow_ref.shape[1]
    width = 512 if model % 512 == 0 else model
    own_first = rank_ref[0] == 0
    for start in range(0, model, width):
        lanes = slice(start, start + width)
        both = mm(done_ref[...], ow_ref[:, lanes])
        early, late = both[:rows], both[rows:]
        own_ref[:, lanes] = jnp.where(own_first, early, late)
        send_ref[:, lanes] = jnp.where(own_first, late, early).astype(jnp.bfloat16)


def attend(sinks, queries, keys, values, out_weight, mixed=()):
    mix = bool(mixed)
    rows, width, model = WINDOW, queries.shape[1], out_weight.shape[1]
    smem = pl.BlockSpec(memory_space=pltpu.SMEM)
    vmem = pl.BlockSpec(memory_space=pltpu.VMEM)
    hbm = pl.BlockSpec(memory_space=pltpu.HBM)
    operands = (sinks, queries, keys, values, out_weight)
    wide = jax.ShapeDtypeStruct((rows, model), jnp.float32)
    narrow = jax.ShapeDtypeStruct((rows, model), jnp.bfloat16)
    shapes = (narrow, wide)
    if not mix:
        shapes = tuple(jax.ShapeDtypeStruct(a.shape, a.dtype) for a in operands)
        shapes += (jax.ShapeDtypeStruct((rows, width), jnp.bfloat16),)
    return pl.pallas_call(
        functools.partial(attend_kernel, mix),
        in_specs=[vmem if mix else hbm] * 5 + ([smem, vmem, smem, vmem] if mix else []),
        out_specs=(vmem,) * len(shapes),
        out_shape=shapes,
        scratch_shapes=[
            pltpu.VMEM((2 * rows, width), jnp.bfloat16) if mix else pltpu.SemaphoreType.DMA((6,))
        ],
        compiler_params=pltpu.CompilerParams(vmem_limit_bytes=8 * MIB),
        cost_estimate=pl.CostEstimate(
            flops=2 * rows * width * (model + 1024), bytes_accessed=6 * MIB, transcendentals=0
        ),
        name="attend",
    )(*pinned(operands, pltpu.VMEM if mix else pltpu.HBM), *mixed)


def norm_kernel(
    expert_count, stream_ref, own_ref, came_ref, gain_ref, ids_ref, route_ref, *rest
):
    residual_ref, *message_refs = rest
    rows, model = stream_ref.shape
    residual = (
        stream_ref[...].astype(jnp.float32) + own_ref[...] + came_ref[...].astype(jnp.float32)
    ).astype(jnp.bfloat16)
    residual_ref[...] = residual
    wide = residual.astype(jnp.float32)
    mean = jnp.mean(wide * wide, axis=-1, keepdims=True)
    normed = (wide * lax.rsqrt(mean + 1e-05) * gain_ref[...]).astype(jnp.bfloat16)
    if not expert_count:
        message_refs[0][...] = normed
        return
    size = rows // len(message_refs)
    expert = lax.broadcasted_iota(jnp.int32, (TAIL, rows), 0)
    dense = jnp.zeros((TAIL, rows), jnp.float32)
    for k in range(TOP):
        dense += jnp.where(expert == ids_ref[k : k + 1, :], route_ref[k : k + 1, :], 0.0)
    lead = dense.astype(jnp.bfloat16).astype(jnp.float32)
    rest = dense - lead
    for index, ref in enumerate(message_refs):
        for block in range(model // LANES):
            ref[block * size : (block + 1) * size] = normed[
                index * size : (index + 1) * size, block * LANES : (block + 1) * LANES
            ]
        span = slice(index * size, (index + 1) * size)
        both = jnp.concatenate([lead[:, span], rest[:, span]], axis=1)
        ref[model // LANES * size :] = both.astype(jnp.bfloat16)


def norm(stream, own, came, gain, expert_ids, route_weights, expert_count):
    rows, model = stream.shape
    vmem = pl.BlockSpec(memory_space=pltpu.VMEM)
    pieces, shape = 1, (rows, model)
    if expert_count:
        pieces = 2
        shape = (rows // pieces * (model // LANES) + TAIL, LANES)
    return pl.pallas_call(
        functools.partial(norm_kernel, expert_count),
        in_specs=[vmem] * 6,
        out_shape=[jax.ShapeDtypeStruct((rows, model), jnp.bfloat16)]
        + [jax.ShapeDtypeStruct(shape, jnp.bfloat16)] * pieces,
        compiler_params=pltpu.CompilerParams(vmem_limit_bytes=8 * MIB),
        cost_estimate=pl.CostEstimate(
            flops=8 * rows * model, bytes_accessed=14 * rows * model, transcendentals=rows
        ),
        name="norm",
    )(stream, own, came, gain.reshape(1, model), expert_ids.T, route_weights.T)


def expert_kernel(tile, count, load, me_ref, *refs):
    x_refs, halves = refs[:count], refs[count : count + 6]
    out_refs, rest = refs[count + 6 : 2 * count + 6], refs[2 * count + 6 :]
    copies = []
    if load:
        kept, rest = rest[:3], rest[3:]
        copies = [
            pltpu.make_async_copy(here, there, rest[2].at[index])
            for index, (here, there) in enumerate(zip(halves[3:], kept))
        ]
        for copy in copies:
            copy.start()
        halves = halves[:3] + kept
    x, hidden = rest[:2]
    model, half = halves[0].shape
    rows = x.shape[0] // count
    body = rows * (model // LANES)
    for index, ref in enumerate(x_refs):
        for block in range(model // LANES):
            x[index * rows : (index + 1) * rows, block * LANES : (block + 1) * LANES] = ref[
                block * rows : (block + 1) * rows
            ]

    def arrived(*which):
        for index in which:
            if copies:
                copies[index].wait()

    def work(side, at):
        gate_ref, up_ref = halves[3 * side : 3 * side + 2]
        gate_pre = mm(x[...], gate_ref[:, at : at + tile])
        up_pre = mm(x[...], up_ref[:, at : at + tile])
        activated = gate_pre * jax.nn.sigmoid(1.702 * gate_pre) * (up_pre + 1.0)
        hidden[:, side * half + at : side * half + at + tile] = activated.astype(jnp.bfloat16)

    for side in range(2):
        if side == 1:
            arrived(0, 1)
        for at in range(0, half, tile):
            work(side, at)
    arrived(2)

    me = me_ref[0]
    scales = []
    for ref in x_refs:
        sent = ref[body:].astype(jnp.float32)
        expert = lax.broadcasted_iota(jnp.int32, sent.shape, 0)
        mine = jnp.sum(jnp.where(expert == me, sent, 0.0), axis=0, keepdims=True)
        mine = jnp.broadcast_to(mine, (8, LANES))
        scales.append((mine + pltpu.roll(mine, LANES - rows, 1)).T[:rows, :1])
    for at in range(0, model, tile):
        lanes = slice(at, at + tile)
        total = mm(hidden[:, :half], halves[2][:, lanes]) + mm(hidden[:, half:], halves[5][:, lanes])
        for index, (ref, scale) in enumerate(zip(out_refs, scales)):
            ref[:, lanes] = (total[index * rows : (index + 1) * rows] * scale).astype(jnp.bfloat16)


def experts(blocks, me, halves, load=False):
    model, half = halves[0].shape
    size = (blocks[0].shape[0] - TAIL) // (model // LANES)
    rows = size * len(blocks)
    vmem = pl.BlockSpec(memory_space=pltpu.VMEM)
    hbm = pl.BlockSpec(memory_space=pltpu.HBM)
    kept = [jax.ShapeDtypeStruct(w.shape, w.dtype) for w in halves[3:]] if load else []
    scratch = [
        pltpu.VMEM((rows, model), jnp.bfloat16),
        pltpu.VMEM((rows, 2 * half), jnp.bfloat16),
    ]
    return pl.pallas_call(
        functools.partial(expert_kernel, min(256, half), len(blocks), load),
        in_specs=[pl.BlockSpec(memory_space=pltpu.SMEM)]
        + [vmem] * len(blocks)
        + [vmem] * 3
        + [hbm if load else vmem] * 3,
        out_specs=[vmem] * (len(blocks) + len(kept)),
        out_shape=[jax.ShapeDtypeStruct((size, model), jnp.bfloat16)] * len(blocks) + kept,
        scratch_shapes=scratch + ([pltpu.SemaphoreType.DMA((3,))] if load else []),
        compiler_params=pltpu.CompilerParams(vmem_limit_bytes=EXPERT_VMEM),
        cost_estimate=pl.CostEstimate(
            flops=12 * rows * model * half, bytes_accessed=6 * rows * model, transcendentals=0
        ),
        name="experts",
    )(
        me,
        *blocks,
        *pinned(halves[:3], pltpu.VMEM),
        *pinned(halves[3:], pltpu.HBM if load else pltpu.VMEM),
    )


def ring_experts(residual, pieces, gate_weight, up_weight, down_weight, others):
    chips = lax.axis_size("seq")
    ring = SNAKES.get(chips, tuple(range(chips)))
    far = chips // 2
    ahead = [(ring[i], ring[(i + 1) % chips]) for i in range(chips)]
    hops = (ahead, [(to, of) for of, to in ahead])
    sides = (0, 1)
    me = lax.axis_index("seq").astype(jnp.int32).reshape(1)
    given = {}

    def keep(keys, outs):
        for (side, distance, piece), out in zip(keys, outs):
            given[(distance if side == 0 else -distance) % chips, piece] = out

    halves = (gate_weight, up_weight, down_weight) + tuple(others)
    outs = experts(pieces, me, halves, load=True)
    halves = halves[:3] + tuple(outs[2:])
    keep([(0, 0, 0), (0, 0, 1)], outs)
    worked = {0: outs[0]}
    came = {(side, 0, piece): pieces[piece] for side in sides for piece in sides}

    def bring(distance, lead, *after):
        keys = [(side, distance - 1, side if lead else 1 - side) for side in sides]
        met = lax.optimization_barrier(tuple(came[key] for key in keys))
        for (side, _, piece), block in zip(keys, met):
            block = tied(block, *after)
            with jax.named_scope(f"out_{'lead' if lead else 'trail'}{distance}"):
                came[side, distance, piece] = lax.ppermute(block, "seq", hops[side])

    def apply(distance, kinds, *after):
        keys = [(side, distance, side if lead else 1 - side) for lead in kinds for side in sides]
        blocks = [came[key] for key in keys]
        if after:
            blocks[0] = tied(blocks[0], *after)
        with jax.named_scope(f"hop{distance}"):
            outs = experts(blocks, me, halves)
        worked.setdefault(distance, outs[0])
        keep(keys, outs)
        return outs[0]

    for distance in range(1, far + 1):
        bring(distance, True, *([worked[distance - 2]] if distance > 1 else []))
        trails = []
        if distance < far:
            before = [came[side, distance - 1, side] for side in sides] if distance > 1 else []
            bring(distance, False, *before)
            if 1 < distance < far - 1:
                trails = [came[side, distance, 1 - side] for side in sides]
        else:
            trails = [came[side, far - 1, 1 - side] for side in sides]
        latest = apply(distance, (True,), worked[distance - 1], *trails)
    latest = apply(far - 1, (False,), latest)

    moving = {}

    def send(distance, lead, *after):
        met = [moving.get((side, side if lead else 1 - side)) for side in sides]
        if met[0] is not None:
            met = list(lax.optimization_barrier(tuple(met)))
        for side in sides:
            piece = side if lead else 1 - side
            value = given[(-distance if side == 0 else distance) % chips, piece]
            if after:
                value = tied(value, *after)
            if met[0] is not None:
                value = met[side].astype(jnp.float32) + value.astype(jnp.float32)
                value = value.astype(jnp.bfloat16)
            with jax.named_scope(f"back_{'lead' if lead else 'trail'}{distance}"):
                moving[side, piece] = lax.ppermute(value, "seq", hops[side])

    send(far - 1, False)
    send(far, True)
    for distance in range(far - 1, 0, -1):
        leads = [moving[side, side] for side in sides]
        send(distance, True)
        if distance > 1:
            latest = apply(distance - 1, (False,), latest, *leads)
            send(distance - 1, False, leads[0])
    final = []
    for piece in sides:
        total = given[0, piece].astype(jnp.float32)
        for side in sides:
            total += moving[side, piece].astype(jnp.float32)
        final.append(total)
    return (residual.astype(jnp.float32) + jnp.concatenate(final, axis=0)).astype(jnp.bfloat16)


def dispatched_experts(
    residual, normed, expert_ids, route_weights, gate_weight, up_weight, down_weight
):
    tokens_here = normed.shape[0]
    resid_f = residual.astype(jnp.float32)
    expert_count = EXP_DEV * lax.axis_size("seq")
    capacity = max(2, 3 * tokens_here * TOP // (2 * expert_count))
    flat_ids = expert_ids.reshape(-1)
    onehot = (flat_ids[:, None] == jnp.arange(expert_count, dtype=jnp.int32)[None, :]).astype(
        jnp.int32
    )
    earlier_count = jnp.cumsum(onehot, axis=0) - onehot
    slot_index = jnp.sum(earlier_count * onehot, axis=1)
    cell_index = (flat_ids * capacity + slot_index).reshape(tokens_here, TOP)
    chooser = jnp.any(
        cell_index[None, :, :]
        == jnp.arange(expert_count * capacity, dtype=jnp.int32)[:, None, None],
        axis=2,
    ).astype(jnp.bfloat16)
    outgoing = mm(chooser, normed).astype(jnp.bfloat16)
    outgoing = outgoing.reshape(expert_count, capacity, normed.shape[1])
    paired = lax.all_gather(outgoing, "rep", axis=1, tiled=True)
    arrived = lax.all_to_all(paired, "seq", split_axis=0, concat_axis=1, tiled=True)[0]
    gate_pre = mm(arrived, gate_weight)
    up_pre = mm(arrived, up_weight)
    activated = (gate_pre * jax.nn.sigmoid(1.702 * gate_pre) * (up_pre + 1.0)).astype(jnp.bfloat16)
    returned = lax.all_to_all(
        mm(activated, down_weight).astype(jnp.bfloat16)[None],
        "seq",
        split_axis=1,
        concat_axis=0,
        tiled=True,
    )
    expert_out = lax.psum_scatter(returned, "rep", scatter_dimension=1, tiled=True)
    picked = expert_out.reshape(expert_count * capacity, -1)[cell_index.reshape(-1)]
    picked = picked.reshape(tokens_here, TOP, -1)
    expert_sum = jnp.sum(route_weights[:, :, None] * picked.astype(jnp.float32), axis=1)
    return (resid_f + expert_sum).astype(jnp.bfloat16)


def per_device(
    stream,
    queries,
    key_rows,
    value_rows,
    sink_logits,
    out_weight,
    norm_gain,
    expert_ids,
    route_weights,
    gate_weight,
    up_weight,
    down_weight,
):
    block_len = queries.shape[0]
    seq = lax.axis_index("seq")
    rank = lax.axis_index("rep").astype(jnp.int32).reshape(1)
    gate_weight, up_weight, down_weight = gate_weight[0], up_weight[0], down_weight[0]
    use_ring = EXP_DEV * lax.axis_size("seq") <= 2 * TOP

    before = shifted(tail(key_rows, value_rows), "seq", 1)
    others = []
    if use_ring:
        others = [swapped(w, "rep") for w in (gate_weight, up_weight, down_weight)]
    first = (seq == 0).astype(jnp.int32).reshape(1)
    *operands, later_half = attend(
        sink_logits.reshape(1, -1), queries, key_rows, value_rows, out_weight
    )
    send, own = attend(*operands, (first, before, rank, later_half))
    came = swapped(send, "rep")
    expert_count = lax.axis_size("seq") * EXP_DEV if use_ring else 0
    residual, *pieces = norm(
        stream, own, came, norm_gain, expert_ids, route_weights, expert_count
    )
    if use_ring:
        *pieces, _ = lax.optimization_barrier((*pieces, others))
        return ring_experts(residual, pieces, gate_weight, up_weight, down_weight, others)
    return dispatched_experts(
        residual,
        pieces[0],
        expert_ids,
        route_weights,
        gate_weight,
        up_weight,
        down_weight,
    )


def solution(mesh):
    return jax.shard_map(
        per_device,
        mesh=mesh,
        in_specs=(
            P(("groups", "seq", "rep"), None),
            P(("groups", "seq"), "rep"),
            P(("groups", "seq"), "rep"),
            P(("groups", "seq"), "rep"),
            P("rep"),
            P("rep", None),
            P(),
            P(("groups", "seq", "rep"), None),
            P(("groups", "seq", "rep"), None),
            P("seq", None, "rep"),
            P("seq", None, "rep"),
            P("seq", "rep", None),
        ),
        out_specs=P(("groups", "seq", "rep"), None),
        check_vma=False,
    )
```

```python
import functools
import math

import jax
import jax.numpy as jnp
from jax import lax
from jax.experimental import pallas as pl
from jax.experimental.pallas import tpu as pltpu
from jax.sharding import PartitionSpec as P

HEAD_DIM = 64
WINDOW = 128
TOP = 4
TAIL = 16
EXP_DEV = 1
LANES = 128
SNAKES = {8: (0, 2, 4, 6, 7, 5, 3, 1)}
MIB = 1 << 20
EXPERT_VMEM = 8 * MIB


def neighbours(value, axis):
    peers = lax.axis_size(axis)
    within = [(i, i ^ 1) for i in range(peers)]
    across = [(i, i if i in (0, peers - 1) else ((i + 1) ^ 1) - 1) for i in range(peers)]
    return lax.ppermute(value, axis, within), lax.ppermute(value, axis, across)


def pinned(values, space):
    return [pltpu.with_memory_space_constraint(value, space) for value in values]


def tied(value, *after):
    return lax.optimization_barrier((value,) + after)[0]


def swapped(value, axis, bit=1):
    peers = lax.axis_size(axis)
    return lax.ppermute(value, axis, [(i, i ^ bit) for i in range(peers)])


def mm(a, b):
    return jnp.dot(a, b, preferred_element_type=jnp.float32)


def tail_kernel(keys_hbm, values_hbm, out_ref, sems):
    rows = out_ref.shape[0] // 2
    last = pl.ds(keys_hbm.shape[0] - rows, rows)
    copies = [
        pltpu.make_async_copy(ref.at[last], out_ref.at[pl.ds(index * rows, rows)], sems.at[index])
        for index, ref in enumerate((keys_hbm, values_hbm))
    ]
    for copy in copies:
        copy.start()
    for copy in copies:
        copy.wait()


def tail(keys, values):
    return pl.pallas_call(
        tail_kernel,
        in_specs=[pl.BlockSpec(memory_space=pltpu.HBM)] * 2,
        out_specs=pl.BlockSpec(memory_space=pltpu.VMEM),
        out_shape=jax.ShapeDtypeStruct((2 * WINDOW, keys.shape[1]), keys.dtype),
        scratch_shapes=[pltpu.SemaphoreType.DMA((2,))],
        name="tail",
    )(*pinned((keys, values), pltpu.HBM))


def attend_kernel(mix, *refs):
    if mix:
        sink_ref, q_ref, k_ref, v_ref, ow_ref = refs[:5]
        place_ref, one_ref, two_ref, rank_ref, later_ref, send_ref, own_ref, done_ref = refs[5:]
        rows = later_ref.shape[0]
        queries = slice(0, rows)
        before = jnp.where(place_ref[1] == 1, one_ref[...], two_ref[...])
        k = jnp.concatenate([before[:rows], k_ref[:rows]], axis=0)
        v = jnp.concatenate([before[rows:], v_ref[:rows]], axis=0)
        done_ref[rows:] = later_ref[...]
        copies = []
    else:
        sink_ref, q_ref, k_ref, v_ref, ow_ref, done_ref = refs[5:11]
        rows = done_ref.shape[0]
        queries = slice(rows, 2 * rows)
        sems = refs[-1]
        early, late = pl.ds(0, rows), pl.ds(rows, rows)
        sources = [(refs[2], k_ref), (refs[3], v_ref), (refs[1].at[late], q_ref.at[late])]
        sources += [(refs[0], sink_ref), (refs[4], ow_ref), (refs[1].at[early], q_ref.at[early])]
        copies = [
            pltpu.make_async_copy(here, there, sems.at[index])
            for index, (here, there) in enumerate(sources)
        ]
        for copy in copies:
            copy.start()
        for copy in copies[:4]:
            copy.wait()
        k, v = k_ref[...], v_ref[...]
    keys = 2 * rows
    pairs = q_ref.shape[1] // LANES
    groups = k_ref.shape[1] // HEAD_DIM

    low = lax.broadcasted_iota(jnp.int32, (keys, LANES), 1) < HEAD_DIM
    k = k.astype(jnp.float32) * (1.0 / math.sqrt(HEAD_DIM))
    v = v.astype(jnp.float32)
    k_turned, v_turned = pltpu.roll(k, HEAD_DIM, 1), pltpu.roll(v, HEAD_DIM, 1)
    key = lax.broadcasted_iota(jnp.int32, (keys, rows), 0)
    query = lax.broadcasted_iota(jnp.int32, (keys, rows), 1)
    allowed = (key <= query + rows) & (key > query)
    if mix:
        allowed = allowed & (key >= jnp.where(place_ref[0] == 1, rows, 0))
    ones = jnp.ones((8, keys), jnp.float32)
    zeros = jnp.zeros((8, keys), jnp.float32)

    for group in range(groups):
        here, there = (k, v), (k_turned, v_turned)
        lows, highs = (here, there) if group == 0 else (there, here)
        kk = jnp.concatenate(
            [jnp.where(low, lows[0], 0.0), jnp.where(low, 0.0, highs[0])], axis=0
        ).astype(jnp.bfloat16)
        v_low = jnp.where(low, lows[1], 0.0).T
        v_high = jnp.where(low, 0.0, highs[1]).T
        vv = jnp.concatenate(
            [
                jnp.concatenate([v_low, v_high], axis=1),
                jnp.concatenate([ones, zeros], axis=1),
                jnp.concatenate([zeros, ones], axis=1),
            ],
            axis=0,
        ).astype(jnp.bfloat16)
        for pair in range(group * pairs // groups, (group + 1) * pairs // groups):
            lanes = slice(pair * LANES, (pair + 1) * LANES)
            scores = lax.dot_general(
                kk, q_ref[queries, lanes], (((1,), (1,)), ((), ())), preferred_element_type=jnp.float32
            )
            weights, sinks = [], []
            for side in range(2):
                part = jnp.where(allowed, scores[side * keys : (side + 1) * keys], -jnp.inf)
                sink = sink_ref[:, 2 * pair + side : 2 * pair + side + 1]
                highest = jnp.maximum(jnp.max(part, axis=0, keepdims=True), sink)
                weights.append(jnp.exp(part - highest).astype(jnp.bfloat16))
                sinks.append(jnp.exp(sink - highest))
            both = mm(vv, jnp.concatenate(weights, axis=0))
            parts = [
                both[side * HEAD_DIM : (side + 1) * HEAD_DIM]
                / (both[LANES + 8 * side : LANES + 8 * side + 1] + sinks[side])
                for side in range(2)
            ]
            done_ref[:rows, lanes] = jnp.concatenate(parts, axis=0).T.astype(jnp.bfloat16)

    for copy in copies[4:]:
        copy.wait()
    if not mix:
        return
    model = ow_ref.shape[1]
    width = 512 if model % 512 == 0 else model
    own_first = rank_ref[0] == 0
    for start in range(0, model, width):
        lanes = slice(start, start + width)
        both = mm(done_ref[...], ow_ref[:, lanes])
        early, late = both[:rows], both[rows:]
        own_ref[:, lanes] = jnp.where(own_first, early, late)
        send_ref[:, lanes] = jnp.where(own_first, late, early).astype(jnp.bfloat16)


def attend(sinks, queries, keys, values, out_weight, mixed=()):
    mix = bool(mixed)
    rows, width, model = WINDOW, queries.shape[1], out_weight.shape[1]
    smem = pl.BlockSpec(memory_space=pltpu.SMEM)
    vmem = pl.BlockSpec(memory_space=pltpu.VMEM)
    hbm = pl.BlockSpec(memory_space=pltpu.HBM)
    operands = (sinks, queries, keys, values, out_weight)
    wide = jax.ShapeDtypeStruct((rows, model), jnp.float32)
    narrow = jax.ShapeDtypeStruct((rows, model), jnp.bfloat16)
    shapes = (narrow, wide)
    if not mix:
        shapes = tuple(jax.ShapeDtypeStruct(a.shape, a.dtype) for a in operands)
        shapes += (jax.ShapeDtypeStruct((rows, width), jnp.bfloat16),)
    return pl.pallas_call(
        functools.partial(attend_kernel, mix),
        in_specs=[vmem if mix else hbm] * 5 + ([smem, vmem, vmem, smem, vmem] if mix else []),
        out_specs=(vmem,) * len(shapes),
        out_shape=shapes,
        scratch_shapes=[
            pltpu.VMEM((2 * rows, width), jnp.bfloat16) if mix else pltpu.SemaphoreType.DMA((6,))
        ],
        compiler_params=pltpu.CompilerParams(vmem_limit_bytes=8 * MIB),
        cost_estimate=pl.CostEstimate(
            flops=2 * rows * width * (model + 1024), bytes_accessed=6 * MIB, transcendentals=0
        ),
        name="attend",
    )(*pinned(operands, pltpu.VMEM if mix else pltpu.HBM), *mixed)


def norm_kernel(
    expert_count, stream_ref, own_ref, came_ref, gain_ref, ids_ref, route_ref, *rest
):
    residual_ref, *message_refs = rest
    rows, model = stream_ref.shape
    residual = (
        stream_ref[...].astype(jnp.float32) + own_ref[...] + came_ref[...].astype(jnp.float32)
    ).astype(jnp.bfloat16)
    residual_ref[...] = residual
    wide = residual.astype(jnp.float32)
    mean = jnp.mean(wide * wide, axis=-1, keepdims=True)
    normed = (wide * lax.rsqrt(mean + 1e-05) * gain_ref[...]).astype(jnp.bfloat16)
    if not expert_count:
        message_refs[0][...] = normed
        return
    size = rows // len(message_refs)
    expert = lax.broadcasted_iota(jnp.int32, (TAIL, rows), 0)
    dense = jnp.zeros((TAIL, rows), jnp.float32)
    for k in range(TOP):
        dense += jnp.where(expert == ids_ref[k : k + 1, :], route_ref[k : k + 1, :], 0.0)
    lead = dense.astype(jnp.bfloat16).astype(jnp.float32)
    rest = dense - lead
    for index, ref in enumerate(message_refs):
        for block in range(model // LANES):
            ref[block * size : (block + 1) * size] = normed[
                index * size : (index + 1) * size, block * LANES : (block + 1) * LANES
            ]
        span = slice(index * size, (index + 1) * size)
        both = jnp.concatenate([lead[:, span], rest[:, span]], axis=1)
        ref[model // LANES * size :] = both.astype(jnp.bfloat16)


def norm(stream, own, came, gain, expert_ids, route_weights, expert_count):
    rows, model = stream.shape
    vmem = pl.BlockSpec(memory_space=pltpu.VMEM)
    pieces, shape = 1, (rows, model)
    if expert_count:
        pieces = 2
        shape = (rows // pieces * (model // LANES) + TAIL, LANES)
    return pl.pallas_call(
        functools.partial(norm_kernel, expert_count),
        in_specs=[vmem] * 6,
        out_shape=[jax.ShapeDtypeStruct((rows, model), jnp.bfloat16)]
        + [jax.ShapeDtypeStruct(shape, jnp.bfloat16)] * pieces,
        compiler_params=pltpu.CompilerParams(vmem_limit_bytes=8 * MIB),
        cost_estimate=pl.CostEstimate(
            flops=8 * rows * model, bytes_accessed=14 * rows * model, transcendentals=rows
        ),
        name="norm",
    )(stream, own, came, gain.reshape(1, model), expert_ids.T, route_weights.T)


def expert_kernel(tile, count, load, me_ref, *refs):
    x_refs, halves = refs[:count], refs[count : count + 6]
    out_refs, rest = refs[count + 6 : 2 * count + 6], refs[2 * count + 6 :]
    copies = []
    if load:
        kept, rest = rest[:3], rest[3:]
        copies = [
            pltpu.make_async_copy(here, there, rest[2].at[index])
            for index, (here, there) in enumerate(zip(halves[3:], kept))
        ]
        for copy in copies:
            copy.start()
        halves = halves[:3] + kept
    x, hidden = rest[:2]
    model, half = halves[0].shape
    rows = x.shape[0] // count
    body = rows * (model // LANES)
    for index, ref in enumerate(x_refs):
        for block in range(model // LANES):
            x[index * rows : (index + 1) * rows, block * LANES : (block + 1) * LANES] = ref[
                block * rows : (block + 1) * rows
            ]

    def arrived(*which):
        for index in which:
            if copies:
                copies[index].wait()

    def work(side, at):
        gate_ref, up_ref = halves[3 * side : 3 * side + 2]
        gate_pre = mm(x[...], gate_ref[:, at : at + tile])
        up_pre = mm(x[...], up_ref[:, at : at + tile])
        activated = gate_pre * jax.nn.sigmoid(1.702 * gate_pre) * (up_pre + 1.0)
        hidden[:, side * half + at : side * half + at + tile] = activated.astype(jnp.bfloat16)

    for side in range(2):
        if side == 1:
            arrived(0, 1)
        for at in range(0, half, tile):
            work(side, at)
    arrived(2)

    me = me_ref[0]
    scales = []
    for ref in x_refs:
        sent = ref[body:].astype(jnp.float32)
        expert = lax.broadcasted_iota(jnp.int32, sent.shape, 0)
        mine = jnp.sum(jnp.where(expert == me, sent, 0.0), axis=0, keepdims=True)
        mine = jnp.broadcast_to(mine, (8, LANES))
        scales.append((mine + pltpu.roll(mine, LANES - rows, 1)).T[:rows, :1])
    for at in range(0, model, tile):
        lanes = slice(at, at + tile)
        total = mm(hidden[:, :half], halves[2][:, lanes]) + mm(hidden[:, half:], halves[5][:, lanes])
        for index, (ref, scale) in enumerate(zip(out_refs, scales)):
            ref[:, lanes] = (total[index * rows : (index + 1) * rows] * scale).astype(jnp.bfloat16)


def experts(blocks, me, halves, load=False):
    model, half = halves[0].shape
    size = (blocks[0].shape[0] - TAIL) // (model // LANES)
    rows = size * len(blocks)
    vmem = pl.BlockSpec(memory_space=pltpu.VMEM)
    hbm = pl.BlockSpec(memory_space=pltpu.HBM)
    kept = [jax.ShapeDtypeStruct(w.shape, w.dtype) for w in halves[3:]] if load else []
    scratch = [
        pltpu.VMEM((rows, model), jnp.bfloat16),
        pltpu.VMEM((rows, 2 * half), jnp.bfloat16),
    ]
    return pl.pallas_call(
        functools.partial(expert_kernel, min(256, half), len(blocks), load),
        in_specs=[pl.BlockSpec(memory_space=pltpu.SMEM)]
        + [vmem] * len(blocks)
        + [vmem] * 3
        + [hbm if load else vmem] * 3,
        out_specs=[vmem] * (len(blocks) + len(kept)),
        out_shape=[jax.ShapeDtypeStruct((size, model), jnp.bfloat16)] * len(blocks) + kept,
        scratch_shapes=scratch + ([pltpu.SemaphoreType.DMA((3,))] if load else []),
        compiler_params=pltpu.CompilerParams(vmem_limit_bytes=EXPERT_VMEM),
        cost_estimate=pl.CostEstimate(
            flops=12 * rows * model * half, bytes_accessed=6 * rows * model, transcendentals=0
        ),
        name="experts",
    )(
        me,
        *blocks,
        *pinned(halves[:3], pltpu.VMEM),
        *pinned(halves[3:], pltpu.HBM if load else pltpu.VMEM),
    )


def ring_experts(residual, pieces, gate_weight, up_weight, down_weight, others):
    chips = lax.axis_size("seq")
    ring = SNAKES.get(chips, tuple(range(chips)))
    far = chips // 2
    ahead = [(ring[i], ring[(i + 1) % chips]) for i in range(chips)]
    hops = (ahead, [(to, of) for of, to in ahead])
    sides = (0, 1)
    me = lax.axis_index("seq").astype(jnp.int32).reshape(1)
    given = {}

    def keep(keys, outs):
        for (side, distance, piece), out in zip(keys, outs):
            given[(distance if side == 0 else -distance) % chips, piece] = out

    halves = (gate_weight, up_weight, down_weight) + tuple(others)
    outs = experts(pieces, me, halves, load=True)
    halves = halves[:3] + tuple(outs[2:])
    keep([(0, 0, 0), (0, 0, 1)], outs)
    worked = {0: outs[0]}
    came = {(side, 0, piece): pieces[piece] for side in sides for piece in sides}

    def bring(distance, lead, *after):
        keys = [(side, distance - 1, side if lead else 1 - side) for side in sides]
        met = lax.optimization_barrier(tuple(came[key] for key in keys))
        for (side, _, piece), block in zip(keys, met):
            block = tied(block, *after)
            with jax.named_scope(f"out_{'lead' if lead else 'trail'}{distance}"):
                came[side, distance, piece] = lax.ppermute(block, "seq", hops[side])

    def apply(distance, kinds, *after):
        keys = [(side, distance, side if lead else 1 - side) for lead in kinds for side in sides]
        blocks = [came[key] for key in keys]
        if after:
            blocks[0] = tied(blocks[0], *after)
        with jax.named_scope(f"hop{distance}"):
            outs = experts(blocks, me, halves)
        worked.setdefault(distance, outs[0])
        keep(keys, outs)
        return outs[0]

    for distance in range(1, far + 1):
        bring(distance, True, *([worked[distance - 2]] if distance > 1 else []))
        trails = []
        if distance < far:
            before = [came[side, distance - 1, side] for side in sides] if distance > 1 else []
            bring(distance, False, *before)
            if distance > 1:
                trails = [came[side, distance, 1 - side] for side in sides]
        latest = apply(distance, (True,), worked[distance - 1], *trails)
    latest = apply(far - 1, (False,), latest)

    moving = {}

    def send(distance, lead, *after):
        met = [moving.get((side, side if lead else 1 - side)) for side in sides]
        if met[0] is not None:
            met = list(lax.optimization_barrier(tuple(met)))
        for side in sides:
            piece = side if lead else 1 - side
            value = given[(-distance if side == 0 else distance) % chips, piece]
            if after:
                value = tied(value, *after)
            if met[0] is not None:
                value = met[side].astype(jnp.float32) + value.astype(jnp.float32)
                value = value.astype(jnp.bfloat16)
            with jax.named_scope(f"back_{'lead' if lead else 'trail'}{distance}"):
                moving[side, piece] = lax.ppermute(value, "seq", hops[side])

    send(far - 1, False)
    send(far, True)
    for distance in range(far - 1, 0, -1):
        leads = [moving[side, side] for side in sides]
        send(distance, True)
        if distance > 1:
            latest = apply(distance - 1, (False,), latest, *leads)
            send(distance - 1, False, leads[0])
    final = []
    for piece in sides:
        total = given[0, piece].astype(jnp.float32)
        for side in sides:
            total += moving[side, piece].astype(jnp.float32)
        final.append(total)
    return (residual.astype(jnp.float32) + jnp.concatenate(final, axis=0)).astype(jnp.bfloat16)


def dispatched_experts(
    residual, normed, expert_ids, route_weights, gate_weight, up_weight, down_weight
):
    tokens_here = normed.shape[0]
    resid_f = residual.astype(jnp.float32)
    expert_count = EXP_DEV * lax.axis_size("seq")
    capacity = max(2, 3 * tokens_here * TOP // (2 * expert_count))
    flat_ids = expert_ids.reshape(-1)
    onehot = (flat_ids[:, None] == jnp.arange(expert_count, dtype=jnp.int32)[None, :]).astype(
        jnp.int32
    )
    earlier_count = jnp.cumsum(onehot, axis=0) - onehot
    slot_index = jnp.sum(earlier_count * onehot, axis=1)
    cell_index = (flat_ids * capacity + slot_index).reshape(tokens_here, TOP)
    chooser = jnp.any(
        cell_index[None, :, :]
        == jnp.arange(expert_count * capacity, dtype=jnp.int32)[:, None, None],
        axis=2,
    ).astype(jnp.bfloat16)
    outgoing = mm(chooser, normed).astype(jnp.bfloat16)
    outgoing = outgoing.reshape(expert_count, capacity, normed.shape[1])
    paired = lax.all_gather(outgoing, "rep", axis=1, tiled=True)
    arrived = lax.all_to_all(paired, "seq", split_axis=0, concat_axis=1, tiled=True)[0]
    gate_pre = mm(arrived, gate_weight)
    up_pre = mm(arrived, up_weight)
    activated = (gate_pre * jax.nn.sigmoid(1.702 * gate_pre) * (up_pre + 1.0)).astype(jnp.bfloat16)
    returned = lax.all_to_all(
        mm(activated, down_weight).astype(jnp.bfloat16)[None],
        "seq",
        split_axis=1,
        concat_axis=0,
        tiled=True,
    )
    expert_out = lax.psum_scatter(returned, "rep", scatter_dimension=1, tiled=True)
    picked = expert_out.reshape(expert_count * capacity, -1)[cell_index.reshape(-1)]
    picked = picked.reshape(tokens_here, TOP, -1)
    expert_sum = jnp.sum(route_weights[:, :, None] * picked.astype(jnp.float32), axis=1)
    return (resid_f + expert_sum).astype(jnp.bfloat16)


def per_device(
    stream,
    queries,
    key_rows,
    value_rows,
    sink_logits,
    out_weight,
    norm_gain,
    expert_ids,
    route_weights,
    gate_weight,
    up_weight,
    down_weight,
):
    block_len = queries.shape[0]
    seq = lax.axis_index("seq")
    rank = lax.axis_index("rep").astype(jnp.int32).reshape(1)
    gate_weight, up_weight, down_weight = gate_weight[0], up_weight[0], down_weight[0]
    use_ring = EXP_DEV * lax.axis_size("seq") <= 2 * TOP

    before = neighbours(tail(key_rows, value_rows), "seq")
    others = []
    if use_ring:
        others = [swapped(w, "rep") for w in (gate_weight, up_weight, down_weight)]
    place = jnp.stack([seq == 0, seq % 2 == 1]).astype(jnp.int32)
    *operands, later_half = attend(
        sink_logits.reshape(1, -1), queries, key_rows, value_rows, out_weight
    )
    send, own = attend(*operands, (place, *before, rank, later_half))
    came = swapped(send, "rep")
    expert_count = lax.axis_size("seq") * EXP_DEV if use_ring else 0
    residual, *pieces = norm(
        stream, own, came, norm_gain, expert_ids, route_weights, expert_count
    )
    if use_ring:
        *pieces, _ = lax.optimization_barrier((*pieces, others))
        return ring_experts(residual, pieces, gate_weight, up_weight, down_weight, others)
    return dispatched_experts(
        residual,
        pieces[0],
        expert_ids,
        route_weights,
        gate_weight,
        up_weight,
        down_weight,
    )


def solution(mesh):
    return jax.shard_map(
        per_device,
        mesh=mesh,
        in_specs=(
            P(("groups", "seq", "rep"), None),
            P(("groups", "seq"), "rep"),
            P(("groups", "seq"), "rep"),
            P(("groups", "seq"), "rep"),
            P("rep"),
            P("rep", None),
            P(),
            P(("groups", "seq", "rep"), None),
            P(("groups", "seq", "rep"), None),
            P("seq", None, "rep"),
            P("seq", None, "rep"),
            P("seq", "rep", None),
        ),
        out_specs=P(("groups", "seq", "rep"), None),
        check_vma=False,
    )
```

```python
import functools
import math

import jax
import jax.numpy as jnp
from jax import lax
from jax.experimental import pallas as pl
from jax.experimental.pallas import tpu as pltpu
from jax.sharding import PartitionSpec as P

HEAD_DIM = 64
WINDOW = 128
TOP = 4
TAIL = 16
EXP_DEV = 1
LANES = 128
SNAKES = {8: (0, 2, 4, 6, 7, 5, 3, 1)}
MIB = 1 << 20
EXPERT_VMEM = 8 * MIB


def shifted(value, axis, by):
    peers = lax.axis_size(axis)
    return lax.ppermute(value, axis, [(i, (i + by) % peers) for i in range(peers)])


def pinned(values, space):
    return [pltpu.with_memory_space_constraint(value, space) for value in values]


def tied(value, *after):
    return lax.optimization_barrier((value,) + after)[0]


def swapped(value, axis, bit=1):
    peers = lax.axis_size(axis)
    return lax.ppermute(value, axis, [(i, i ^ bit) for i in range(peers)])


def mm(a, b):
    return jnp.dot(a, b, preferred_element_type=jnp.float32)


def attend_kernel(mix, *refs):
    if mix:
        sink_ref, q_ref, k_ref, v_ref, ow_ref = refs[:5]
        first_ref, k_before, v_before, rank_ref, later_ref, send_ref, own_ref, done_ref = refs[5:]
        rows = later_ref.shape[0]
        queries = slice(0, rows)
        k = jnp.concatenate([k_before[rows:], k_ref[:rows]], axis=0)
        v = jnp.concatenate([v_before[rows:], v_ref[:rows]], axis=0)
        done_ref[rows:] = later_ref[...]
        copies = []
    else:
        sink_ref, q_ref, k_ref, v_ref, ow_ref, done_ref = refs[5:11]
        rows = done_ref.shape[0]
        queries = slice(rows, 2 * rows)
        sems = refs[-1]
        early, late = pl.ds(0, rows), pl.ds(rows, rows)
        sources = [(refs[2], k_ref), (refs[3], v_ref), (refs[1].at[late], q_ref.at[late])]
        sources += [(refs[0], sink_ref), (refs[4], ow_ref), (refs[1].at[early], q_ref.at[early])]
        copies = [
            pltpu.make_async_copy(here, there, sems.at[index])
            for index, (here, there) in enumerate(sources)
        ]
        for copy in copies:
            copy.start()
        for copy in copies[:4]:
            copy.wait()
        k, v = k_ref[...], v_ref[...]
    keys = 2 * rows
    pairs = q_ref.shape[1] // LANES
    groups = k_ref.shape[1] // HEAD_DIM

    low = lax.broadcasted_iota(jnp.int32, (keys, LANES), 1) < HEAD_DIM
    k = k.astype(jnp.float32) * (1.0 / math.sqrt(HEAD_DIM))
    v = v.astype(jnp.float32)
    k_turned, v_turned = pltpu.roll(k, HEAD_DIM, 1), pltpu.roll(v, HEAD_DIM, 1)
    key = lax.broadcasted_iota(jnp.int32, (keys, rows), 0)
    query = lax.broadcasted_iota(jnp.int32, (keys, rows), 1)
    allowed = (key <= query + rows) & (key > query)
    if mix:
        allowed = allowed & (key >= jnp.where(first_ref[0] == 1, rows, 0))
    ones = jnp.ones((8, keys), jnp.float32)
    zeros = jnp.zeros((8, keys), jnp.float32)

    for group in range(groups):
        here, there = (k, v), (k_turned, v_turned)
        lows, highs = (here, there) if group == 0 else (there, here)
        kk = jnp.concatenate(
            [jnp.where(low, lows[0], 0.0), jnp.where(low, 0.0, highs[0])], axis=0
        ).astype(jnp.bfloat16)
        v_low = jnp.where(low, lows[1], 0.0).T
        v_high = jnp.where(low, 0.0, highs[1]).T
        vv = jnp.concatenate(
            [
                jnp.concatenate([v_low, v_high], axis=1),
                jnp.concatenate([ones, zeros], axis=1),
                jnp.concatenate([zeros, ones], axis=1),
            ],
            axis=0,
        ).astype(jnp.bfloat16)
        for pair in range(group * pairs // groups, (group + 1) * pairs // groups):
            lanes = slice(pair * LANES, (pair + 1) * LANES)
            scores = lax.dot_general(
                kk, q_ref[queries, lanes], (((1,), (1,)), ((), ())), preferred_element_type=jnp.float32
            )
            weights, sinks = [], []
            for side in range(2):
                part = jnp.where(allowed, scores[side * keys : (side + 1) * keys], -jnp.inf)
                sink = sink_ref[:, 2 * pair + side : 2 * pair + side + 1]
                highest = jnp.maximum(jnp.max(part, axis=0, keepdims=True), sink)
                weights.append(jnp.exp(part - highest).astype(jnp.bfloat16))
                sinks.append(jnp.exp(sink - highest))
            both = mm(vv, jnp.concatenate(weights, axis=0))
            parts = [
                both[side * HEAD_DIM : (side + 1) * HEAD_DIM]
                / (both[LANES + 8 * side : LANES + 8 * side + 1] + sinks[side])
                for side in range(2)
            ]
            done_ref[:rows, lanes] = jnp.concatenate(parts, axis=0).T.astype(jnp.bfloat16)

    for copy in copies[4:]:
        copy.wait()
    if not mix:
        return
    model = ow_ref.shape[1]
    width = 512 if model % 512 == 0 else model
    own_first = rank_ref[0] == 0
    for start in range(0, model, width):
        lanes = slice(start, start + width)
        both = mm(done_ref[...], ow_ref[:, lanes])
        early, late = both[:rows], both[rows:]
        own_ref[:, lanes] = jnp.where(own_first, early, late)
        send_ref[:, lanes] = jnp.where(own_first, late, early).astype(jnp.bfloat16)


def attend(sinks, queries, keys, values, out_weight, mixed=()):
    mix = bool(mixed)
    rows, width, model = WINDOW, queries.shape[1], out_weight.shape[1]
    smem = pl.BlockSpec(memory_space=pltpu.SMEM)
    vmem = pl.BlockSpec(memory_space=pltpu.VMEM)
    hbm = pl.BlockSpec(memory_space=pltpu.HBM)
    operands = (sinks, queries, keys, values, out_weight)
    wide = jax.ShapeDtypeStruct((rows, model), jnp.float32)
    narrow = jax.ShapeDtypeStruct((rows, model), jnp.bfloat16)
    shapes = (narrow, wide)
    if not mix:
        shapes = tuple(jax.ShapeDtypeStruct(a.shape, a.dtype) for a in operands)
        shapes += (jax.ShapeDtypeStruct((rows, width), jnp.bfloat16),)
    return pl.pallas_call(
        functools.partial(attend_kernel, mix),
        in_specs=[vmem if mix else hbm] * 5 + ([smem, vmem, vmem, smem, vmem] if mix else []),
        out_specs=(vmem,) * len(shapes),
        out_shape=shapes,
        scratch_shapes=[
            pltpu.VMEM((2 * rows, width), jnp.bfloat16) if mix else pltpu.SemaphoreType.DMA((6,))
        ],
        compiler_params=pltpu.CompilerParams(vmem_limit_bytes=8 * MIB),
        cost_estimate=pl.CostEstimate(
            flops=2 * rows * width * (model + 1024), bytes_accessed=6 * MIB, transcendentals=0
        ),
        name="attend",
    )(*pinned(operands, pltpu.VMEM if mix else pltpu.HBM), *mixed)


def norm_kernel(
    expert_count, stream_ref, own_ref, came_ref, gain_ref, ids_ref, route_ref, *rest
):
    residual_ref, *message_refs = rest
    rows, model = stream_ref.shape
    residual = (
        stream_ref[...].astype(jnp.float32) + own_ref[...] + came_ref[...].astype(jnp.float32)
    ).astype(jnp.bfloat16)
    residual_ref[...] = residual
    wide = residual.astype(jnp.float32)
    mean = jnp.mean(wide * wide, axis=-1, keepdims=True)
    normed = (wide * lax.rsqrt(mean + 1e-05) * gain_ref[...]).astype(jnp.bfloat16)
    if not expert_count:
        message_refs[0][...] = normed
        return
    size = rows // len(message_refs)
    expert = lax.broadcasted_iota(jnp.int32, (TAIL, rows), 0)
    dense = jnp.zeros((TAIL, rows), jnp.float32)
    for k in range(TOP):
        dense += jnp.where(expert == ids_ref[k : k + 1, :], route_ref[k : k + 1, :], 0.0)
    lead = dense.astype(jnp.bfloat16).astype(jnp.float32)
    rest = dense - lead
    for index, ref in enumerate(message_refs):
        for block in range(model // LANES):
            ref[block * size : (block + 1) * size] = normed[
                index * size : (index + 1) * size, block * LANES : (block + 1) * LANES
            ]
        span = slice(index * size, (index + 1) * size)
        both = jnp.concatenate([lead[:, span], rest[:, span]], axis=1)
        ref[model // LANES * size :] = both.astype(jnp.bfloat16)


def norm(stream, own, came, gain, expert_ids, route_weights, expert_count):
    rows, model = stream.shape
    vmem = pl.BlockSpec(memory_space=pltpu.VMEM)
    pieces, shape = 1, (rows, model)
    if expert_count:
        pieces = 2
        shape = (rows // pieces * (model // LANES) + TAIL, LANES)
    return pl.pallas_call(
        functools.partial(norm_kernel, expert_count),
        in_specs=[vmem] * 6,
        out_shape=[jax.ShapeDtypeStruct((rows, model), jnp.bfloat16)]
        + [jax.ShapeDtypeStruct(shape, jnp.bfloat16)] * pieces,
        compiler_params=pltpu.CompilerParams(vmem_limit_bytes=8 * MIB),
        cost_estimate=pl.CostEstimate(
            flops=8 * rows * model, bytes_accessed=14 * rows * model, transcendentals=rows
        ),
        name="norm",
    )(stream, own, came, gain.reshape(1, model), expert_ids.T, route_weights.T)


def expert_kernel(tile, count, load, me_ref, *refs):
    x_refs, halves = refs[:count], refs[count : count + 6]
    out_refs, rest = refs[count + 6 : 2 * count + 6], refs[2 * count + 6 :]
    copies = []
    if load:
        kept, rest = rest[:3], rest[3:]
        copies = [
            pltpu.make_async_copy(here, there, rest[2].at[index])
            for index, (here, there) in enumerate(zip(halves[3:], kept))
        ]
        for copy in copies:
            copy.start()
        halves = halves[:3] + kept
    x, hidden = rest[:2]
    model, half = halves[0].shape
    rows = x.shape[0] // count
    body = rows * (model // LANES)
    for index, ref in enumerate(x_refs):
        for block in range(model // LANES):
            x[index * rows : (index + 1) * rows, block * LANES : (block + 1) * LANES] = ref[
                block * rows : (block + 1) * rows
            ]

    def arrived(*which):
        for index in which:
            if copies:
                copies[index].wait()

    def work(side, at):
        gate_ref, up_ref = halves[3 * side : 3 * side + 2]
        gate_pre = mm(x[...], gate_ref[:, at : at + tile])
        up_pre = mm(x[...], up_ref[:, at : at + tile])
        activated = gate_pre * jax.nn.sigmoid(1.702 * gate_pre) * (up_pre + 1.0)
        hidden[:, side * half + at : side * half + at + tile] = activated.astype(jnp.bfloat16)

    for side in range(2):
        if side == 1:
            arrived(0, 1)
        for at in range(0, half, tile):
            work(side, at)
    arrived(2)

    me = me_ref[0]
    scales = []
    for ref in x_refs:
        sent = ref[body:].astype(jnp.float32)
        expert = lax.broadcasted_iota(jnp.int32, sent.shape, 0)
        mine = jnp.sum(jnp.where(expert == me, sent, 0.0), axis=0, keepdims=True)
        mine = jnp.broadcast_to(mine, (8, LANES))
        scales.append((mine + pltpu.roll(mine, LANES - rows, 1)).T[:rows, :1])
    for at in range(0, model, tile):
        lanes = slice(at, at + tile)
        total = mm(hidden[:, :half], halves[2][:, lanes]) + mm(hidden[:, half:], halves[5][:, lanes])
        for index, (ref, scale) in enumerate(zip(out_refs, scales)):
            ref[:, lanes] = (total[index * rows : (index + 1) * rows] * scale).astype(jnp.bfloat16)


def experts(blocks, me, halves, load=False):
    model, half = halves[0].shape
    size = (blocks[0].shape[0] - TAIL) // (model // LANES)
    rows = size * len(blocks)
    vmem = pl.BlockSpec(memory_space=pltpu.VMEM)
    hbm = pl.BlockSpec(memory_space=pltpu.HBM)
    kept = [jax.ShapeDtypeStruct(w.shape, w.dtype) for w in halves[3:]] if load else []
    scratch = [
        pltpu.VMEM((rows, model), jnp.bfloat16),
        pltpu.VMEM((rows, 2 * half), jnp.bfloat16),
    ]
    return pl.pallas_call(
        functools.partial(expert_kernel, min(256, half), len(blocks), load),
        in_specs=[pl.BlockSpec(memory_space=pltpu.SMEM)]
        + [vmem] * len(blocks)
        + [vmem] * 3
        + [hbm if load else vmem] * 3,
        out_specs=[vmem] * (len(blocks) + len(kept)),
        out_shape=[jax.ShapeDtypeStruct((size, model), jnp.bfloat16)] * len(blocks) + kept,
        scratch_shapes=scratch + ([pltpu.SemaphoreType.DMA((3,))] if load else []),
        compiler_params=pltpu.CompilerParams(vmem_limit_bytes=EXPERT_VMEM),
        cost_estimate=pl.CostEstimate(
            flops=12 * rows * model * half, bytes_accessed=6 * rows * model, transcendentals=0
        ),
        name="experts",
    )(
        me,
        *blocks,
        *pinned(halves[:3], pltpu.VMEM),
        *pinned(halves[3:], pltpu.HBM if load else pltpu.VMEM),
    )


def ring_experts(residual, pieces, gate_weight, up_weight, down_weight, others):
    chips = lax.axis_size("seq")
    ring = SNAKES.get(chips, tuple(range(chips)))
    far = chips // 2
    ahead = [(ring[i], ring[(i + 1) % chips]) for i in range(chips)]
    hops = (ahead, [(to, of) for of, to in ahead])
    sides = (0, 1)
    me = lax.axis_index("seq").astype(jnp.int32).reshape(1)
    given = {}

    def keep(keys, outs):
        for (side, distance, piece), out in zip(keys, outs):
            given[(distance if side == 0 else -distance) % chips, piece] = out

    halves = (gate_weight, up_weight, down_weight) + tuple(others)
    outs = experts(pieces, me, halves, load=True)
    halves = halves[:3] + tuple(outs[2:])
    keep([(0, 0, 0), (0, 0, 1)], outs)
    worked = {0: outs[0]}
    came = {(side, 0, piece): pieces[piece] for side in sides for piece in sides}

    def bring(distance, lead, *after):
        keys = [(side, distance - 1, side if lead else 1 - side) for side in sides]
        met = lax.optimization_barrier(tuple(came[key] for key in keys))
        for (side, _, piece), block in zip(keys, met):
            block = tied(block, *after)
            with jax.named_scope(f"out_{'lead' if lead else 'trail'}{distance}"):
                came[side, distance, piece] = lax.ppermute(block, "seq", hops[side])

    def apply(distance, kinds, *after):
        keys = [(side, distance, side if lead else 1 - side) for lead in kinds for side in sides]
        blocks = [came[key] for key in keys]
        if after:
            blocks[0] = tied(blocks[0], *after)
        with jax.named_scope(f"hop{distance}"):
            outs = experts(blocks, me, halves)
        worked.setdefault(distance, outs[0])
        keep(keys, outs)
        return outs[0]

    for distance in range(1, far + 1):
        bring(distance, True, *([worked[distance - 2]] if distance > 1 else []))
        trails = []
        if distance < far:
            before = [came[side, distance - 1, side] for side in sides] if distance > 1 else []
            bring(distance, False, *before)
            if distance > 1:
                trails = [came[side, distance, 1 - side] for side in sides]
        latest = apply(distance, (True,), worked[distance - 1], *trails)
    latest = apply(far - 1, (False,), latest)

    moving = {}

    def send(distance, lead, *after):
        met = [moving.get((side, side if lead else 1 - side)) for side in sides]
        if met[0] is not None:
            met = list(lax.optimization_barrier(tuple(met)))
        for side in sides:
            piece = side if lead else 1 - side
            value = given[(-distance if side == 0 else distance) % chips, piece]
            if after:
                value = tied(value, *after)
            if met[0] is not None:
                value = met[side].astype(jnp.float32) + value.astype(jnp.float32)
                value = value.astype(jnp.bfloat16)
            with jax.named_scope(f"back_{'lead' if lead else 'trail'}{distance}"):
                moving[side, piece] = lax.ppermute(value, "seq", hops[side])

    send(far, True)
    send(far - 1, False, *[came[side, far, side] for side in sides])
    for distance in range(far - 1, 0, -1):
        leads = [moving[side, side] for side in sides]
        send(distance, True)
        if distance > 1:
            latest = apply(distance - 1, (False,), latest, *leads)
            send(distance - 1, False, leads[0])
    final = []
    for piece in sides:
        total = given[0, piece].astype(jnp.float32)
        for side in sides:
            total += moving[side, piece].astype(jnp.float32)
        final.append(total)
    return (residual.astype(jnp.float32) + jnp.concatenate(final, axis=0)).astype(jnp.bfloat16)


def dispatched_experts(
    residual, normed, expert_ids, route_weights, gate_weight, up_weight, down_weight
):
    tokens_here = normed.shape[0]
    resid_f = residual.astype(jnp.float32)
    expert_count = EXP_DEV * lax.axis_size("seq")
    capacity = max(2, 3 * tokens_here * TOP // (2 * expert_count))
    flat_ids = expert_ids.reshape(-1)
    onehot = (flat_ids[:, None] == jnp.arange(expert_count, dtype=jnp.int32)[None, :]).astype(
        jnp.int32
    )
    earlier_count = jnp.cumsum(onehot, axis=0) - onehot
    slot_index = jnp.sum(earlier_count * onehot, axis=1)
    cell_index = (flat_ids * capacity + slot_index).reshape(tokens_here, TOP)
    chooser = jnp.any(
        cell_index[None, :, :]
        == jnp.arange(expert_count * capacity, dtype=jnp.int32)[:, None, None],
        axis=2,
    ).astype(jnp.bfloat16)
    outgoing = mm(chooser, normed).astype(jnp.bfloat16)
    outgoing = outgoing.reshape(expert_count, capacity, normed.shape[1])
    paired = lax.all_gather(outgoing, "rep", axis=1, tiled=True)
    arrived = lax.all_to_all(paired, "seq", split_axis=0, concat_axis=1, tiled=True)[0]
    gate_pre = mm(arrived, gate_weight)
    up_pre = mm(arrived, up_weight)
    activated = (gate_pre * jax.nn.sigmoid(1.702 * gate_pre) * (up_pre + 1.0)).astype(jnp.bfloat16)
    returned = lax.all_to_all(
        mm(activated, down_weight).astype(jnp.bfloat16)[None],
        "seq",
        split_axis=1,
        concat_axis=0,
        tiled=True,
    )
    expert_out = lax.psum_scatter(returned, "rep", scatter_dimension=1, tiled=True)
    picked = expert_out.reshape(expert_count * capacity, -1)[cell_index.reshape(-1)]
    picked = picked.reshape(tokens_here, TOP, -1)
    expert_sum = jnp.sum(route_weights[:, :, None] * picked.astype(jnp.float32), axis=1)
    return (resid_f + expert_sum).astype(jnp.bfloat16)


def per_device(
    stream,
    queries,
    key_rows,
    value_rows,
    sink_logits,
    out_weight,
    norm_gain,
    expert_ids,
    route_weights,
    gate_weight,
    up_weight,
    down_weight,
):
    block_len = queries.shape[0]
    seq = lax.axis_index("seq")
    rank = lax.axis_index("rep").astype(jnp.int32).reshape(1)
    gate_weight, up_weight, down_weight = gate_weight[0], up_weight[0], down_weight[0]
    use_ring = EXP_DEV * lax.axis_size("seq") <= 2 * TOP

    before = shifted(key_rows, "seq", 1), shifted(value_rows, "seq", 1)
    others = []
    if use_ring:
        others = [swapped(w, "rep") for w in (gate_weight, up_weight, down_weight)]
    first = (seq == 0).astype(jnp.int32).reshape(1)
    *operands, later_half = attend(
        sink_logits.reshape(1, -1), queries, key_rows, value_rows, out_weight
    )
    send, own = attend(*operands, (first, *before, rank, later_half))
    came = swapped(send, "rep")
    expert_count = lax.axis_size("seq") * EXP_DEV if use_ring else 0
    residual, *pieces = norm(
        stream, own, came, norm_gain, expert_ids, route_weights, expert_count
    )
    if use_ring:
        *pieces, _ = lax.optimization_barrier((*pieces, others))
        return ring_experts(residual, pieces, gate_weight, up_weight, down_weight, others)
    return dispatched_experts(
        residual,
        pieces[0],
        expert_ids,
        route_weights,
        gate_weight,
        up_weight,
        down_weight,
    )


def solution(mesh):
    return jax.shard_map(
        per_device,
        mesh=mesh,
        in_specs=(
            P(("groups", "seq", "rep"), None),
            P(("groups", "seq"), "rep"),
            P(("groups", "seq"), "rep"),
            P(("groups", "seq"), "rep"),
            P("rep"),
            P("rep", None),
            P(),
            P(("groups", "seq", "rep"), None),
            P(("groups", "seq", "rep"), None),
            P("seq", None, "rep"),
            P("seq", None, "rep"),
            P("seq", "rep", None),
        ),
        out_specs=P(("groups", "seq", "rep"), None),
        check_vma=False,
    )
```
